32 devices in a mesh: gx: 4 (over z), gy: 4 (over x, core), gz: 2 (over y).
Axes of the slice: x: 2, y: 2, z: 4, core: 2. Of those that a mesh axis runs over, the one named last changes fastest.
Arguments:
- local_solution: float32 [3, 68, 180, 256], P(None, 'gx', 'gy', 'gz'), may hold values from -6 to 6
- top_nodes: float32 [3, 68, 180, 2], P(None, 'gx', 'gy', 'gz'), may hold values from -6 to 6
- coarse_solution: float32 [3, 1024], P(None, 'gz'), may hold values from -6 to 6
- corner_dofs: int32 [4, 4, 2, 8], P('gx', 'gy', 'gz'), may hold values from 0 to 1023
- density: float32 [64, 176, 256], P('gx', 'gy', 'gz'), may hold values from 0.1 to 1
- element_stiffness: float32 [24, 24], replicated, may hold values from -0.15 to 4.5, as said below
Outputs:
- filtered_sens: float32 [64, 176, 256], P('gx', 'gy', 'gz')
- filtered_density: float32 [64, 176, 256], P('gx', 'gy', 'gz')
The draws below stay inside these ranges and needn't reach their ends.
Inputs may be any that keep to these rules, and one draw needn't show every extreme that they name: element_stiffness is symmetric.
All inputs are finite; a program needn't handle non-finite values.
Results may differ from the reference program's by a relative error of at most 0.00005.
Values sent between devices are 32-bit elements; how exact they have to be, the bound alone decides.
No kernel may reach another device: no remote copies, remote signals or barrier semaphores. Data moves between devices by JAX's collectives and lax.ppermute only.
A program may use at most 64 MiB of HBM per device.

```python
import jax
import jax.numpy as jnp
from jax import lax

CX = 16
CY = 44
CZ = 128
RADIUS = 3
NX = 64
NY = 176
NZ = 256
NXN = 68
NYN = 180
NCOARSE = 1024
N_GX = 4
N_GY = 4
N_GZ = 2


def draw_element_stiffness(key, part):
    first_key, second_key = jax.random.split(key, 2)
    raw_off = jax.random.uniform(first_key, (24, 24), jnp.float32, -0.15, 0.15)
    diag_part = 4.0 + jax.random.uniform(second_key, (24,), jnp.float32, -0.5, 0.5)
    off_part = 0.5 * (raw_off + raw_off.T)
    identity = jnp.eye(24, dtype=jnp.float32)
    return off_part * (1.0 - identity) + identity * diag_part[:, None]


def touch_ends(result, rng, low, largest):
    longest = result.shape.index(max(result.shape))
    spots = []
    for shift in (0, 1):
        where = [jax.random.randint(jax.random.fold_in(rng, axis), (), 0, length) for axis, length in enumerate(result.shape)]
        where[longest] = (where[longest] + shift) % result.shape[longest]
        spots.append(tuple(where))
    return result.at[spots[0]].set(low).at[spots[1]].set(largest)


def shard_levels(stream_key, extent, cuts, smallest, largest):
    level, own = 1.0, jax.random.fold_in(stream_key, 6)
    for dim, parts in cuts:
        steps = jnp.exp(jax.random.uniform(jax.random.fold_in(own, dim), (parts,), jnp.float32, smallest / len(cuts), largest / len(cuts)))
        level = level * jnp.repeat(steps, extent[dim] // parts).reshape([-1 if axis == dim else 1 for axis in range(len(extent))])
    return level


def normal_values(stream_key, shape, deviation, bound, cuts=(), kind=jnp.bfloat16):
    factor_of = shard_levels(stream_key, shape, cuts, -0.22, 0.18) if cuts else 1.0
    result = jax.random.normal(stream_key, shape, jnp.float32) * deviation * factor_of
    return jnp.minimum(jnp.maximum(result, -bound), bound).astype(kind)


def setup_inputs(seed: int = 0) -> dict:
    splits = jax.random.split(jax.random.key(seed), 7)
    local_solution = normal_values(splits[0], (3, NXN, NYN, NZ), 1.0, 6.0, ((1, 4), (2, 4), (3, 2)), jnp.float32)
    top_nodes = normal_values(splits[1], (3, NXN, NYN, N_GZ), 1.0, 6.0, ((1, 4), (2, 4), (3, 2)), jnp.float32)
    coarse_solution = normal_values(splits[2], (3, NCOARSE), 1.0, 6.0, ((1, 2),), jnp.float32)
    corner_dofs = touch_ends(jax.random.randint(splits[3], (N_GX, N_GY, N_GZ, 8), 0, NCOARSE), jax.random.fold_in(splits[3], 1), 0, NCOARSE - 1).astype(jnp.int32)
    density = jnp.clip(0.1 + 0.9 * jax.random.uniform(splits[4], (NX, NY, NZ), jnp.float32) ** shard_levels(splits[4], (NX, NY, NZ), ((0, 4), (1, 4), (2, 2)), -0.2, 0.2), 0.1, 1.0)
    element_stiffness = draw_element_stiffness(jax.random.fold_in(splits[6], 71), 0)
    return {"local_solution": local_solution, "top_nodes": top_nodes, "coarse_solution": coarse_solution, "corner_dofs": corner_dofs, "density": density, "element_stiffness": element_stiffness}


penal_scale = -3.0 / 96.0


def recover(local_nodes, corner_vals):
    ex = local_nodes.shape[1] - 1
    ey = local_nodes.shape[2] - 1
    ez = local_nodes.shape[3] - 1
    ratio_x = jnp.arange(ex + 1, dtype=jnp.float32) / ex
    ratio_y = jnp.arange(ey + 1, dtype=jnp.float32) / ey
    ratio_z = jnp.arange(ez + 1, dtype=jnp.float32) / ez
    summed = local_nodes
    for corner in range(8):
        along_x = ratio_x if corner // 4 == 1 else 1.0 - ratio_x
        along_y = ratio_y if (corner // 2) % 2 == 1 else 1.0 - ratio_y
        along_z = ratio_z if corner % 2 == 1 else 1.0 - ratio_z
        basis = along_x[:, None, None] * along_y[None, :, None] * along_z[None, None, :]
        summed = summed + basis[None] * corner_vals[:, corner][:, None, None, None]
    return summed


def element_energy(node_block, stiffness):
    ex = node_block.shape[1] - 1
    ey = node_block.shape[2] - 1
    ez = node_block.shape[3] - 1

    def rows_energy(first_row):
        node_slab = lax.dynamic_slice_in_dim(node_block, first_row, 5, axis=1)
        columns = []
        for corner in range(8):
            shift_x = corner // 4
            shift_y = (corner // 2) % 2
            shift_z = corner % 2
            columns.append(node_slab[:, shift_x:shift_x + 4, shift_y:shift_y + ey, shift_z:shift_z + ez].reshape(3, -1))
        vectors = jnp.stack(columns, axis=1).reshape(24, -1)
        product = jnp.dot(stiffness, vectors, precision=lax.Precision.HIGHEST, preferred_element_type=jnp.float32)
        return jnp.sum(vectors * product, axis=0).reshape(4, ey, ez)

    starts = (jnp.arange(ex // 4, dtype=jnp.int32) * 4).astype(jnp.int32)
    energies = lax.map(rows_energy, starts)
    return energies.reshape(ex, ey, ez)


def smooth(field, axis, count):
    summed = None
    for offset in range(-RADIUS, RADIUS + 1):
        term_piece = lax.slice_in_dim(field, RADIUS + offset, RADIUS + offset + count, axis=axis)
        term_value = float(RADIUS + 1 - abs(offset)) * term_piece
        summed = term_value if summed is None else summed + term_value
    return summed


def conv_global(field):
    for axis in range(3):
        count = field.shape[axis]
        widths = [(0, 0), (0, 0), (0, 0)]
        widths[axis] = (RADIUS, RADIUS)
        field = smooth(jnp.pad(field, widths), axis, count)
    return field


def reference(local_solution, top_nodes, coarse_solution, corner_dofs, density, element_stiffness):
    blocks = N_GX * N_GY * N_GZ
    lower_part = local_solution.reshape(3, N_GX, CX + 1, N_GY, CY + 1, N_GZ, CZ)
    top_part = top_nodes.reshape(3, N_GX, CX + 1, N_GY, CY + 1, N_GZ, 1)
    grid = jnp.concatenate([lower_part, top_part], axis=6)
    grid = grid.transpose(1, 3, 5, 0, 2, 4, 6).reshape(blocks, 3, CX + 1, CY + 1, CZ + 1)
    indices = corner_dofs.reshape(-1).astype(jnp.int32)
    corner_vals = jnp.take(coarse_solution, indices, axis=1).reshape(3, blocks, 8).transpose(1, 0, 2)

    def recover_pair(pair):
        return recover(pair[0], pair[1])

    grid = lax.map(recover_pair, (grid, corner_vals))
    grid = grid.reshape(N_GX, N_GY, N_GZ, 3, CX + 1, CY + 1, CZ + 1)
    lower = grid[1:, :, :, :, 0]
    upper = grid[:-1, :, :, :, CX]
    middle = lower * 0.5 + upper * 0.5
    grid = grid.at[1:, :, :, :, 0].set(middle).at[:-1, :, :, :, CX].set(middle)
    lower = grid[:, 1:, :, :, :, 0]
    upper = grid[:, :-1, :, :, :, CY]
    middle = lower * 0.5 + upper * 0.5
    grid = grid.at[:, 1:, :, :, :, 0].set(middle).at[:, :-1, :, :, :, CY].set(middle)
    lower = grid[:, :, 1:, :, :, :, 0]
    upper = grid[:, :, :-1, :, :, :, CZ]
    middle = lower * 0.5 + upper * 0.5
    grid = grid.at[:, :, 1:, :, :, :, 0].set(middle).at[:, :, :-1, :, :, :, CZ].set(middle)
    grid = grid.reshape(blocks, 3, CX + 1, CY + 1, CZ + 1)

    def block_energy(node_block):
        return element_energy(node_block, element_stiffness)

    energy = lax.map(block_energy, grid)
    energy = energy.reshape(N_GX, N_GY, N_GZ, CX, CY, CZ).transpose(0, 3, 1, 4, 2, 5).reshape(NX, NY, NZ)
    sens = penal_scale * density * density * energy
    normalizer = conv_global(jnp.ones((NX, NY, NZ), jnp.float32))
    numerator = conv_global(density * sens)
    smooth_density = conv_global(density)
    return numerator / (density * normalizer), smooth_density / normalizer
```

```python
import functools

import jax
import jax.numpy as jnp
from jax import lax
from jax.experimental import pallas as pl
from jax.experimental.pallas import tpu as pltpu
from jax.sharding import PartitionSpec as P

RADIUS = 3
F32 = jnp.float32
BF16 = jnp.bfloat16
SCALE = -3.0 / 96.0
HIGHEST = lax.Precision.HIGHEST
VM = pltpu.VMEM
SM = pltpu.SMEM

EX, EY, EZ = 16, 44, 128
NX, NY = EX + 1, EY + 1
XN, XE = NX + 2 * RADIUS, EX + 2 * RADIUS
ROWS = 48
QROWS = 56
XR = 24


def iota(shape, dim):
    return lax.broadcasted_iota(jnp.int32, shape, dim)


def one_hot(mask):
    return jnp.where(mask, 1.0, 0.0).astype(F32)


def halves(value):
    high = value.astype(BF16)
    return high, (value - high.astype(F32)).astype(BF16)


def corner_scalars(coarse_ref, dof_of, shared):
    width = coarse_ref.shape[2]
    own = lax.axis_index("gz")
    out = [[None] * 8 for _ in range(3)]
    for k in range(8):
        dof = dof_of(k)
        part = dof // width
        place = dof - part * width
        if shared:
            part = jnp.where(part == own, 0, 1)
        for c in range(3):
            out[c][k] = coarse_ref[part, c, place]
    return out


def plane_scalars(corners, c, i):
    wx = i / EX
    return [(1.0 - wx) * corners[c][m] + wx * corners[c][4 + m] for m in range(4)]


def plane_interp(corners, c, i, rows):
    low_low, low_high, high_low, high_high = plane_scalars(corners, c, i)
    rz = iota((1, EZ), 1).astype(F32) * (1.0 / EZ)
    ry = iota((rows, EZ), 0).astype(F32) * (1.0 / EY)
    first = low_low * (1.0 - rz) + low_high * rz
    second = high_low * (1.0 - rz) + high_high * rz
    return (1.0 - ry) * first + ry * second


def stiffness_rows(stiff, in_lanes):
    def target(m, r):
        s, c = r // 4, r % 4
        if in_lanes:
            return jnp.where(c < 3, 8 * c + 4 * (m % 2) + 2 * s + m // 2, -1)
        return jnp.where(c < 3, 8 * c + 2 * m + s, -1)

    row = iota((32, 24), 0)
    left = one_hot(iota((32, 24), 1) == target(row // 8, row % 8))
    col = iota((24, 64), 1)
    right = one_hot(iota((24, 64), 0) == target(col // 16, col % 8))
    full = jnp.dot(left, stiff, precision=HIGHEST, preferred_element_type=F32)
    full = jnp.dot(full, right, precision=HIGHEST, preferred_element_type=F32)
    high = full.astype(BF16).astype(F32)
    return jnp.concatenate([high, full - high], axis=0).astype(BF16)


def build_nodes(plane_of, planes, rows, w_ref, b_ref, first=0):
    for p in planes:
        base = (first + p) * rows * 8
        zero = jnp.zeros((rows, EZ), F32)
        for c in range(3):
            value = plane_of(c, p)
            w_ref[pl.ds(base + c, rows, stride=8), :] = value
            w_ref[pl.ds(base + 4 + c, rows, stride=8), :] = pltpu.roll(value, EZ - 1, 1)
        w_ref[pl.ds(base + 3, rows, stride=8), :] = zero
        w_ref[pl.ds(base + 7, rows, stride=8), :] = zero

    count = len(planes)

    def split(p, _):
        base = (first + p) * rows
        for r in range(rows):
            value = w_ref[pl.ds(pl.multiple_of((base + r) * 8, 8), 8), :]
            high = value.astype(BF16).astype(F32)
            b_ref[pl.ds(pl.multiple_of((base + r) * 16, 16), 16), :] = jnp.concatenate([high, value - high], axis=0).astype(BF16)
        return 0

    lax.fori_loop(0, count, split, 0)


def energy_planes(lhs, w_ref, b_ref, s_ref, e_ref, first, count, rows, starts, out_first):
    def step(i, _):
        base = (first + i) * rows
        for r in starts:
            right = []
            for t in (0, 1):
                here = pl.multiple_of((base + r + t) * 16, 16)
                there = pl.multiple_of((base + rows + r + t) * 16, 16)
                right.append(jnp.concatenate([b_ref[pl.ds(here, 32), :], b_ref[pl.ds(there, 32), :]], axis=0))
            product = jnp.dot(lhs, jnp.concatenate(right, axis=1), preferred_element_type=F32)
            product = product[0:32] + product[32:64]
            for t in (0, 1):
                here = pl.multiple_of((base + r + t) * 8, 8)
                there = pl.multiple_of((base + rows + r + t) * 8, 8)
                part = product[:, t * EZ : (t + 1) * EZ]
                low = w_ref[pl.ds(here, 16), :] * part[0:16]
                high = w_ref[pl.ds(there, 16), :] * part[16:32]
                both = low + high
                s_ref[pl.ds(pl.multiple_of((r + t) * 8, 8), 8), :] = both[0:8] + both[8:16]
        total = None
        for s in (0, 1, 2, 4, 5, 6):
            term = s_ref[pl.ds(s, rows, stride=8), :]
            total = term if total is None else total + term
        e_ref[out_first + i] = total
        return 0

    lax.fori_loop(0, count, step, 0)


def pack_kernel(local_ref, top_ref, dens_ref, dofs_ref, up_ref, down_ref):
    for out_ref, node, elem in ((up_ref, EX - RADIUS, EX - RADIUS), (down_ref, 0, 0)):
        out_ref[...] = jnp.zeros(out_ref.shape, F32)
        for c in range(3):
            for j in range(4):
                out_ref[c * 4 + j, 0:NY, :] = local_ref[c, node + j]
                out_ref[c * 4 + j, NY : NY + 1, 0:NY] = top_ref[c, node + j : node + j + 1, :]
        for j in range(3):
            out_ref[12 + j, 0:EY, :] = dens_ref[pl.ds(elem + j, EY, stride=EX), :]
        out_ref[12, EY : EY + 1, 0:8] = dofs_ref[...].astype(F32)


def own_kernel(shared, local_ref, stiff_ref, coarse_ref, dofs_ref, own_ref, e_ref, lhs_ref, w_ref, b_ref, s_ref):
    corners = corner_scalars(coarse_ref, lambda k: dofs_ref[k], shared)
    for i in range(NX):
        for c in range(3):
            own_ref[c * NX + i, 0:NY, :] = local_ref[c, i] + plane_interp(corners, c, i, NY)
            own_ref[c * NX + i, NY:ROWS, :] = jnp.zeros((ROWS - NY, EZ), F32)
    stiff = stiff_ref[...]
    lhs = stiffness_rows(stiff, False)
    lhs_ref[0] = lhs
    lhs_ref[1] = stiffness_rows(stiff, True)
    s_ref[...] = jnp.zeros(s_ref.shape, F32)
    build_nodes(lambda c, p: own_ref[c * NX + p + 1], range(EX - 1), ROWS, w_ref, b_ref)
    energy_planes(lhs, w_ref, b_ref, s_ref, e_ref, 0, EX - 2, ROWS, range(1, EY - 1, 2), 0)


def average(flag, low, high, own):
    return jnp.where(flag, 0.5 * low + 0.5 * high, own)


def has_lower(axis):
    return lax.axis_index(axis) > 0


def has_upper(axis):
    return lax.axis_index(axis) < lax.axis_size(axis) - 1


def message_dofs(message_ref):
    row = message_ref[12, EY : EY + 1, :]
    lane = iota((1, EZ), 1)
    return lambda k: jnp.sum(jnp.where(lane == k, row, 0.0)).astype(jnp.int32)


def top_interp(corners, c, rows):
    rx = iota((rows, EZ), 0).astype(F32) * (1.0 / EX)
    ry = iota((rows, EZ), 1).astype(F32) * (1.0 / EY)
    low = (1.0 - ry) * corners[c][1] + ry * corners[c][3]
    high = (1.0 - ry) * corners[c][5] + ry * corners[c][7]
    return (1.0 - rx) * low + rx * high


TOP_AT = 368
Y_MESSAGE = 392


def x_kernel(shared, own_ref, top_ref, dens_ref, low_ref, high_ref, coarse_ref, dofs_ref,
             xl_ref, xh_ref, tx_ref, up_ref, down_ref, t_ref):
    corners = corner_scalars(coarse_ref, lambda k: dofs_ref[k], shared)
    corners_low = corner_scalars(coarse_ref, message_dofs(low_ref), shared)
    corners_high = corner_scalars(coarse_ref, message_dofs(high_ref), shared)
    lower, upper = has_lower("gx"), has_upper("gx")
    for c in range(3):
        for j in range(4):
            value = low_ref[c * 4 + j] + plane_interp(corners_low, c, EX - RADIUS + j, ROWS)
            if j == 3:
                mine = own_ref[c * NX]
                value = average(lower, value, mine, mine)
            xl_ref[c * 4 + j] = value
            value = high_ref[c * 4 + j] + plane_interp(corners_high, c, j, ROWS)
            if j == 0:
                mine = own_ref[c * NX + EX]
                value = average(upper, mine, value, mine)
            xh_ref[c * 4 + j] = value

    t_ref[...] = jnp.zeros(t_ref.shape, F32)
    for c in range(3):
        mine = top_ref[c] + top_interp(corners, c, NX)[:, 0:NY]
        t_ref[0, 0:NX, 0:NY] = mine
        for j in range(4):
            t_ref[1, j : j + 1, 0:NY] = low_ref[c * 4 + j, NY : NY + 1, 0:NY]
            t_ref[2, j : j + 1, 0:NY] = high_ref[c * 4 + j, NY : NY + 1, 0:NY]
        t_low = t_ref[1, 0:8, :] + pltpu.roll(top_interp(corners_low, c, 24), 24 - (EX - RADIUS), 0)[0:8]
        t_high = t_ref[2, 0:8, :] + top_interp(corners_high, c, 8)
        first = average(lower, t_low[3:4], t_ref[0, 0:1, :], t_ref[0, 0:1, :])
        last = average(upper, t_ref[0, EX : EX + 1, :], t_high[0:1], t_ref[0, EX : EX + 1, :])
        t_ref[3, 0:3, :] = t_low[0:3]
        t_ref[3, 3:4, :] = first
        t_ref[3, 4:19, :] = t_ref[0, 1:EX, :]
        t_ref[3, 19:20, :] = last
        t_ref[3, 20:23, :] = t_high[1:4]
        lane = iota((XR, EZ), 1)
        tx_ref[c] = jnp.where(lane < NY + 8, pltpu.roll(t_ref[3], 8, 1), 0.0)

    def plane(c, p):
        if p < 4:
            return xl_ref[c * 4 + p]
        if p < 19:
            return own_ref[c * NX + p - 3]
        return xh_ref[c * 4 + p - 19]

    def density(x):
        if x < 3:
            return low_ref[12 + x, 0:EY, :]
        if x < 19:
            return dens_ref[pl.ds(x - 3, EY, stride=EX), :]
        return high_ref[12 + x - 19, 0:EY, :]

    for out_ref, node, elem, lane_at in ((up_ref, EY - RADIUS, EY - RADIUS, EY - RADIUS + 8), (down_ref, 0, 0, 8)):
        for c in range(3):
            for p in range(XN):
                at = (c * XN + p) * 4
                out_ref[at : at + 4, :] = plane(c, p)[node : node + 4]
        for x in range(XE):
            at = 3 * XN * 4 + x * 4
            out_ref[at : at + 3, :] = density(x)[elem : elem + 3]
            out_ref[at + 3 : at + 4, :] = jnp.zeros((1, EZ), F32)
        out_ref[364:TOP_AT, :] = jnp.zeros((TOP_AT - 364, EZ), F32)
        lane = iota((XR, EZ), 1)
        total = jnp.zeros((XR, EZ), F32)
        for c in range(3):
            moved = pltpu.roll(tx_ref[c], (4 * c - lane_at) % EZ, 1)
            total = jnp.where((lane >= 4 * c) & (lane < 4 * c + 4), moved, total)
        out_ref[TOP_AT:Y_MESSAGE, :] = total


def side_kernel(own_ref, xl_ref, xh_ref, lhs_ref, e_ref, w_ref, b_ref, s_ref):
    s_ref[...] = jnp.zeros(s_ref.shape, F32)

    def plane(c, p):
        if p < 4:
            return xl_ref[c * 4 + p]
        if p == 4:
            return own_ref[c * NX + 1]
        if p == 5:
            return own_ref[c * NX + EX - 1]
        return xh_ref[c * 4 + p - 6]

    build_nodes(plane, range(10), ROWS, w_ref, b_ref)
    lhs = lhs_ref[0]
    for first, out_first in ((0, 0), (5, 4)):
        energy_planes(lhs, w_ref, b_ref, s_ref, e_ref, first, 4, ROWS, range(1, EY - 1, 2), out_first)


Z_MESSAGE = 192


def y_kernel(own_ref, xl_ref, xh_ref, tx_ref, dens_ref, lowx_ref, highx_ref, low_ref, high_ref,
             first_ref, last_ref, dext_ref, oa_ref, ob_ref, od_ref, up_ref, down_ref, z_ref, d_ref):
    lower, upper = has_lower("gy"), has_upper("gy")

    def plane(c, p):
        if p < 4:
            return xl_ref[c * 4 + p]
        if p < 19:
            return own_ref[c * NX + p - 3]
        return xh_ref[c * 4 + p - 19]

    def keep_planes(dest, at, step, block):
        turned = block.T
        dest[pl.ds(at, 8, stride=step), 0:64] = jnp.concatenate([turned[0:4], turned[EZ - 4 : EZ]], axis=0)

    pad = jnp.zeros((64 - QROWS, EZ), F32)
    z_ref[...] = jnp.zeros(z_ref.shape, F32)
    d_ref[...] = jnp.zeros(d_ref.shape, F32)
    for c in range(3):
        for p in range(XN):
            i = c * XN + p
            mine = plane(c, p)
            first_ref[i, 0:5, :] = jnp.zeros((5, EZ), F32)
            first_ref[i, 5:8, :] = low_ref[i * 4 : i * 4 + 3, :]
            first_ref[i, 8:16, :] = mine[0:8]
            first_ref[i, 8:9, :] = average(lower, low_ref[i * 4 + 3 : i * 4 + 4, :], mine[0:1], mine[0:1])
            last_ref[i, 0:4, :] = mine[40:44]
            last_ref[i, 4:5, :] = average(upper, mine[44:45], high_ref[i * 4 : i * 4 + 1, :], mine[44:45])
            last_ref[i, 5:8, :] = high_ref[i * 4 + 1 : i * 4 + 4, :]
            keep_planes(z_ref, c * XR + p, 3 * XR, jnp.concatenate([first_ref[i], mine[8:40], last_ref[i], pad], axis=0))

    dext_ref[...] = jnp.zeros(dext_ref.shape, F32)
    for x in range(XE):
        at = 3 * XN * 4 + x * 4
        if x < 3:
            mine = lowx_ref[12 + x, 0:EY, :]
        elif x < 19:
            mine = dens_ref[pl.ds(x - 3, EY, stride=EX), :]
        else:
            mine = highx_ref[12 + x - 19, 0:EY, :]
        dext_ref[x, 8 : 8 + EY, :] = mine
        dext_ref[x, 5:8, :] = low_ref[at : at + 3, :]
        dext_ref[x, 52:55, :] = high_ref[at : at + 3, :]
        keep_planes(d_ref, x, XR, jnp.concatenate([dext_ref[x], pad], axis=0))

    lane = iota((XR, EZ), 1)
    tops = []
    for c in range(3):
        mine = tx_ref[c]
        low = pltpu.roll(low_ref[TOP_AT:Y_MESSAGE, :], (5 - 4 * c) % EZ, 1)
        high = pltpu.roll(high_ref[TOP_AT:Y_MESSAGE, :], (52 - 4 * c) % EZ, 1)
        value = jnp.where((lane >= 5) & (lane < 8), low, mine)
        value = jnp.where(lane == 8, average(lower, low, mine, mine), value)
        value = jnp.where(lane == 52, average(upper, mine, high, mine), value)
        tops.append(jnp.where((lane > 52) & (lane < 56), high, value))
    top = jnp.concatenate(tops, axis=0)

    def nodes(k):
        return z_ref[k * 3 * XR : (k + 1) * 3 * XR, :]

    def dens(k):
        return d_ref[k * XR : (k + 1) * XR, :]

    def pack(low, high):
        return low + pltpu.roll(high, 64, 1)

    oa_ref[...] = pack(nodes(0), top)
    ob_ref[...] = pack(nodes(1), nodes(7))
    od_ref[...] = pack(dens(0), dens(7))
    up_ref[0:72, :] = pack(nodes(5), nodes(6))
    up_ref[72:144, :] = pack(nodes(7), top)
    up_ref[144:168, :] = pack(dens(5), dens(6))
    up_ref[168:192, :] = dens(7)
    down_ref[0:72, :] = pack(nodes(0), nodes(1))
    down_ref[72:144, :] = pack(nodes(2), nodes(3))
    down_ref[144:168, :] = pack(dens(0), dens(1))
    down_ref[168:192, :] = dens(2)


def edge_kernel(own_ref, xl_ref, xh_ref, first_ref, last_ref, lhs_ref, el_ref, eh_ref, w_ref, b_ref, s_ref):
    s_ref[...] = jnp.zeros(s_ref.shape, F32)
    lhs = lhs_ref[0]
    build_nodes(lambda c, p: first_ref[c * XN + p], range(XN), 16, w_ref, b_ref)
    energy_planes(lhs, w_ref, b_ref, s_ref, el_ref, 0, XE, 16, (5, 7), 0)
    build_nodes(lambda c, p: last_ref[c * XN + p], range(XN), 8, w_ref, b_ref)
    energy_planes(lhs, w_ref, b_ref, s_ref, eh_ref, 0, XE, 8, (3, 5), 0)


def triangle(value, axis):
    size = value.shape[axis]
    value = value + pltpu.roll(value, size - 1, axis)
    value = value + pltpu.roll(value, size - 2, axis)
    value = value + pltpu.roll(value, 1, axis)
    return value + pltpu.roll(value, 2, axis)


def weights(distance):
    return jnp.maximum(4 - jnp.abs(distance), 0).astype(F32)


def three_parts(value):
    high = value.astype(BF16)
    rest = value - high.astype(F32)
    middle = rest.astype(BF16)
    return high, middle, (rest - middle.astype(F32)).astype(BF16)


def exact_dot(value, right):
    parts = [jnp.dot(part, right, preferred_element_type=F32) for part in three_parts(value)]
    return parts[0] + parts[1] + parts[2]


def edge_total(count, position, parts):
    total = None
    for offset in range(-RADIUS, RADIUS + 1):
        place = position + offset
        term = float(RADIUS + 1 - abs(offset)) * one_hot((place >= 0) & (place < count * parts))
        total = term if total is None else total + term
    return total


def last_kernel(ea_ref, eb_ref, el_ref, eh_ref, dext_ref, oa_ref, ob_ref, od_ref, zl_ref, zh_ref, lhs_ref,
                sens_ref, smooth_ref, w_ref, b_ref, s_ref, ez_ref, f_ref, g_ref, c_ref):
    lower, upper = has_lower("gz"), has_upper("gz")

    def swap(value):
        return pltpu.roll(value, 64, 1)

    is_low = iota((3 * XR, EZ), 1) < 64
    oa, ob = oa_ref[...], ob_ref[...]
    zl0, zl1 = zl_ref[0:72, :], zl_ref[72:144, :]
    zh0, zh1 = zh_ref[0:72, :], zh_ref[72:144, :]
    nodes = (
        jnp.where(is_low, zl0, ob),
        jnp.where(is_low, swap(zl0), average(upper, oa, swap(zh0), oa)),
        jnp.where(is_low, zl1, zh0),
        jnp.where(is_low, average(lower, swap(zl1), oa, oa), swap(zh1)),
        jnp.where(is_low, ob, zh1),
    )
    build_nodes(lambda c, k: nodes[k][c * XR : (c + 1) * XR], range(5), XR, w_ref, b_ref)
    s_ref[...] = jnp.zeros(s_ref.shape, F32)
    energy_planes(lhs_ref[1], w_ref, b_ref, s_ref, ez_ref, 0, 4, XR, range(0, XE, 2), 0)

    lane = iota((XR, EZ), 1)
    low_side = lane < 64
    od = od_ref[...]
    dl0, dl1 = zl_ref[144:168, :], zl_ref[168:192, :]
    dh0, dh1 = zh_ref[144:168, :], zh_ref[168:192, :]
    dens = (
        jnp.where(low_side, dl0, od),
        jnp.where(low_side, swap(dl0), swap(dh0)),
        jnp.where(low_side, dl1, dh0),
        jnp.where(low_side, od, swap(dh1)),
    )
    inside = (lane % 64 >= 5) & (lane % 64 < 55) & (iota((XR, EZ), 0) < XE)
    for j in range(4):
        d = dens[j]
        for f, value in ((0, (SCALE * d) * d * d * ez_ref[j]), (1, d)):
            value = triangle_forward(jnp.where(inside, value, 0.0))
            c_ref[f, j * EX : (j + 1) * EX, :] = value[0:EX]
    row, col = iota((EZ, EZ), 0), iota((EZ, EZ), 1)
    along_y = jnp.where(row // 64 == col // 64, weights(row - col), 0.0).astype(BF16)

    rows = iota((QROWS, EZ), 0)
    lanes = iota((QROWS, EZ), 1)
    ok = (rows >= 5) & (rows < 55) & (lanes > 0) & (lanes < EZ - 1)
    for x in range(XE):
        if x < 4:
            middle = eb_ref[x]
        elif x < 18:
            middle = ea_ref[x - 4]
        else:
            middle = eb_ref[x - 14]
        start = jnp.where(rows[0:8] < 1, el_ref[x, 8:16, :], middle[0:8])
        end = jnp.where(rows[0:8] < 3, middle[40:48], eh_ref[x])
        energy = jnp.concatenate([el_ref[x, 0:8, :], start, middle[8:40], end], axis=0)
        d = dext_ref[x]
        f_ref[0, x] = jnp.where(ok, (SCALE * d) * d * d * energy, 0.0)
        f_ref[1, x] = jnp.where(ok, d, 0.0)

    for f in range(2):
        for t in range(QROWS // 8):
            at = slice(t * 8, t * 8 + 8)
            line = [f_ref[f, x, at, :] for x in range(XE)]
            for step in (1, 2, 1, 2):
                line = [line[i] + line[i + step] for i in range(len(line) - step)]
            for x in range(EX):
                g_ref[f, x, at, :] = line[x]

    k = iota((EZ, EZ), 0)
    j = (k % 64) // EX
    place = jnp.where(k < 64, j - 3, EZ - 1 + j)
    z = iota((EZ, EZ), 1)
    right = jnp.concatenate([weights(k - z), weights(place - z)], axis=0).astype(BF16)

    ends = []
    for f in range(2):
        turned = exact_dot(c_ref[f], along_y)
        turned = jnp.concatenate([turned, jnp.zeros((EZ - 4 * EX, EZ), F32)], axis=0).T
        ends.append(turned[8:56] + pltpu.roll(turned[72:120], 64, 1))

    base_x, base_y, base_z = lax.axis_index("gx") * EX, lax.axis_index("gy") * EY, lax.axis_index("gz") * EZ
    norm_y = edge_total(EY, base_y + iota((ROWS, EZ), 0), lax.axis_size("gy"))
    norm_z = edge_total(EZ, base_z + iota((ROWS, EZ), 1), lax.axis_size("gz"))
    norm_yz = norm_y * norm_z
    lanes = iota((ROWS, EZ), 1)
    for x in range(EX):
        sums = []
        for f in range(2):
            body = triangle(g_ref[f, x], 0)[8:QROWS]
            tail = jnp.where(lanes % EX == x, ends[f], 0.0)
            sums.append(exact_dot(jnp.concatenate([body, tail], axis=1), right))
        norm = norm_yz * edge_total(EX, base_x + x, lax.axis_size("gx"))
        d = dext_ref[x + 3, 8:QROWS, :]
        d = jnp.where(rows[0:ROWS] < EY, d, 1.0)
        sens_ref[pl.ds(x, EY, stride=EX), :] = (sums[0] / (d * norm))[0:EY]
        smooth_ref[pl.ds(x, EY, stride=EX), :] = (sums[1] / norm)[0:EY]


def triangle_forward(value):
    size = value.shape[0]
    for step in (1, 2, 1, 2):
        value = value + pltpu.roll(value, size - step, 0)
    return value


def call(kernel, outs, spaces, scratch=(), limit=32, flops=0, moved=0):
    return pl.pallas_call(
        kernel,
        out_shape=[jax.ShapeDtypeStruct(shape, dtype) for shape, dtype in outs],
        in_specs=[pl.BlockSpec(memory_space=space) for space in spaces],
        out_specs=[pl.BlockSpec(memory_space=VM)] * len(outs),
        scratch_shapes=[pltpu.VMEM(shape, dtype) for shape, dtype in scratch],
        compiler_params=pltpu.CompilerParams(vmem_limit_bytes=limit * 2**20),
        cost_estimate=pl.CostEstimate(flops=flops, bytes_accessed=moved, transcendentals=0),
    )


def both_ways(up, down, axis):
    count = lax.axis_size(axis)
    ups = [(i, i + 1) for i in range(count - 1)]
    downs = [(j, i) for i, j in ups]
    return lax.ppermute(up, axis, ups), lax.ppermute(down, axis, downs)


def local(local_solution, top_nodes, coarse_solution, corner_dofs, density, element_stiffness):
    top = top_nodes.reshape(3, NX, NY)
    dens = jnp.transpose(density, (1, 0, 2)).reshape(EY * EX, EZ)
    dofs = corner_dofs.reshape(8)
    shared = lax.axis_size("gz") == 2
    if shared:
        other = lax.ppermute(coarse_solution, "gz", [(0, 1), (1, 0)])
        coarse = jnp.stack([coarse_solution, other])
    else:
        coarse = lax.all_gather(coarse_solution, "gz")

    up, down = call(pack_kernel, [((15, ROWS, EZ), F32)] * 2, [VM] * 4)(local_solution, top, dens, dofs.reshape(1, 8))
    low_x, high_x = both_ways(up, down, "gx")

    def nodes(count):
        return [((count * 8, EZ), F32), ((count * 16, EZ), BF16)]

    own, ea, lhs = call(
        functools.partial(own_kernel, shared),
        [((3 * NX, ROWS, EZ), F32), ((EX - 2, ROWS, EZ), F32), ((2, 64, 64), BF16)],
        [VM, VM, SM, SM],
        nodes((EX - 1) * ROWS) + [((ROWS * 8, EZ), F32)],
    )(local_solution, element_stiffness, coarse, dofs)

    xl, xh, tx, up, down = call(
        functools.partial(x_kernel, shared),
        [((12, ROWS, EZ), F32), ((12, ROWS, EZ), F32), ((3, XR, EZ), F32), ((Y_MESSAGE, EZ), F32), ((Y_MESSAGE, EZ), F32)],
        [VM, VM, VM, VM, VM, SM, SM],
        [((4, XR, EZ), F32)],
    )(own, top, dens, low_x, high_x, coarse, dofs)
    low_y, high_y = both_ways(up, down, "gy")

    (eb,) = call(side_kernel, [((8, ROWS, EZ), F32)], [VM] * 4, nodes(10 * ROWS) + [((ROWS * 8, EZ), F32)])(own, xl, xh, lhs)

    first, last, dext, oa, ob, od, up, down = call(
        y_kernel,
        [((3 * XN, 16, EZ), F32), ((3 * XN, 8, EZ), F32), ((XE, QROWS, EZ), F32), ((72, EZ), F32), ((72, EZ), F32),
         ((XR, EZ), F32), ((Z_MESSAGE, EZ), F32), ((Z_MESSAGE, EZ), F32)],
        [VM] * 9,
        [((8 * 3 * XR, EZ), F32), ((8 * XR, EZ), F32)],
    )(own, xl, xh, tx, dens, low_x, high_x, low_y, high_y)
    if shared:
        is_first = lax.axis_index("gz") == 0
        other = lax.ppermute(jnp.where(is_first, up, down), "gz", [(0, 1), (1, 0)])
        low_z = jnp.where(is_first, 0.0, other)
        high_z = jnp.where(is_first, other, 0.0)
    else:
        low_z, high_z = both_ways(up, down, "gz")

    el, eh = call(
        edge_kernel,
        [((XE, 16, EZ), F32), ((XE, 8, EZ), F32)],
        [VM] * 6,
        nodes(XN * 16) + [((16 * 8, EZ), F32)],
    )(own, xl, xh, first, last, lhs)

    sens, smooth = call(
        last_kernel,
        [((EY * EX, EZ), F32)] * 2,
        [VM] * 11,
        nodes(5 * XR) + [((XR * 8, EZ), F32), ((4, XR, EZ), F32), ((2, XE, QROWS, EZ), F32), ((2, EX, QROWS, EZ), F32),
                         ((2, 4 * EX, EZ), F32)],
    )(ea, eb, el, eh, dext, oa, ob, od, low_z, high_z, lhs)

    def grid(value):
        return jnp.transpose(value.reshape(EY, EX, EZ), (1, 0, 2))

    return grid(sens), grid(smooth)


def solution(mesh):
    in_specs = (
        P(None, "gx", "gy", "gz"),
        P(None, "gx", "gy", "gz"),
        P(None, "gz"),
        P("gx", "gy", "gz", None),
        P("gx", "gy", "gz"),
        P(),
    )
    out_specs = (P("gx", "gy", "gz"), P("gx", "gy", "gz"))
    return jax.shard_map(local, mesh=mesh, in_specs=in_specs, out_specs=out_specs, check_vma=False)
```

```python
import functools

import jax
import jax.numpy as jnp
from jax import lax
from jax.experimental import pallas as pl
from jax.experimental.pallas import tpu as pltpu
from jax.sharding import PartitionSpec as P

RADIUS = 3
F32 = jnp.float32
BF16 = jnp.bfloat16
SCALE = -3.0 / 96.0
HIGHEST = lax.Precision.HIGHEST
VM = pltpu.VMEM
SM = pltpu.SMEM

EX, EY, EZ = 16, 44, 128
NX, NY = EX + 1, EY + 1
XN, XE = NX + 2 * RADIUS, EX + 2 * RADIUS
ROWS = 48
QROWS = 56
XR = 24


def iota(shape, dim):
    return lax.broadcasted_iota(jnp.int32, shape, dim)


def one_hot(mask):
    return jnp.where(mask, 1.0, 0.0).astype(F32)


def halves(value):
    high = value.astype(BF16)
    return high, (value - high.astype(F32)).astype(BF16)


def corner_scalars(coarse_ref, dof_of, shared):
    width = coarse_ref.shape[2]
    own = lax.axis_index("gz")
    out = [[None] * 8 for _ in range(3)]
    for k in range(8):
        dof = dof_of(k)
        part = dof // width
        place = dof - part * width
        if shared:
            part = jnp.where(part == own, 0, 1)
        for c in range(3):
            out[c][k] = coarse_ref[part, c, place]
    return out


def plane_scalars(corners, c, i):
    wx = i / EX
    return [(1.0 - wx) * corners[c][m] + wx * corners[c][4 + m] for m in range(4)]


def plane_interp(corners, c, i, rows):
    low_low, low_high, high_low, high_high = plane_scalars(corners, c, i)
    rz = iota((1, EZ), 1).astype(F32) * (1.0 / EZ)
    ry = iota((rows, EZ), 0).astype(F32) * (1.0 / EY)
    first = low_low * (1.0 - rz) + low_high * rz
    second = high_low * (1.0 - rz) + high_high * rz
    return (1.0 - ry) * first + ry * second


def stiffness_rows(stiff, in_lanes):
    def target(m, r):
        s, c = r // 4, r % 4
        if in_lanes:
            return jnp.where(c < 3, 8 * c + 4 * (m % 2) + 2 * s + m // 2, -1)
        return jnp.where(c < 3, 8 * c + 2 * m + s, -1)

    row = iota((32, 24), 0)
    left = one_hot(iota((32, 24), 1) == target(row // 8, row % 8))
    col = iota((24, 64), 1)
    right = one_hot(iota((24, 64), 0) == target(col // 16, col % 8))
    full = jnp.dot(left, stiff, precision=HIGHEST, preferred_element_type=F32)
    full = jnp.dot(full, right, precision=HIGHEST, preferred_element_type=F32)
    high = full.astype(BF16).astype(F32)
    return jnp.concatenate([high, full - high], axis=0).astype(BF16)


def build_nodes(plane_of, planes, rows, w_ref, b_ref, first=0):
    for p in planes:
        base = (first + p) * rows * 8
        zero = jnp.zeros((rows, EZ), F32)
        for c in range(3):
            value = plane_of(c, p)
            w_ref[pl.ds(base + c, rows, stride=8), :] = value
            w_ref[pl.ds(base + 4 + c, rows, stride=8), :] = pltpu.roll(value, EZ - 1, 1)
        w_ref[pl.ds(base + 3, rows, stride=8), :] = zero
        w_ref[pl.ds(base + 7, rows, stride=8), :] = zero

    count = len(planes)

    def split(p, _):
        base = (first + p) * rows
        for r in range(rows):
            value = w_ref[pl.ds(pl.multiple_of((base + r) * 8, 8), 8), :]
            high = value.astype(BF16).astype(F32)
            b_ref[pl.ds(pl.multiple_of((base + r) * 16, 16), 16), :] = jnp.concatenate([high, value - high], axis=0).astype(BF16)
        return 0

    lax.fori_loop(0, count, split, 0)


def energy_planes(lhs, w_ref, b_ref, s_ref, e_ref, first, count, rows, starts, out_first, group):
    def step(i, _):
        for g in range(group):
            base = (first + i * group + g) * rows
            for r in starts:
                right = []
                for t in (0, 1):
                    here = pl.multiple_of((base + r + t) * 16, 16)
                    there = pl.multiple_of((base + rows + r + t) * 16, 16)
                    right.append(jnp.concatenate([b_ref[pl.ds(here, 32), :], b_ref[pl.ds(there, 32), :]], axis=0))
                product = jnp.dot(lhs, jnp.concatenate(right, axis=1), preferred_element_type=F32)
                product = product[0:32] + product[32:64]
                for t in (0, 1):
                    here = pl.multiple_of((base + r + t) * 8, 8)
                    there = pl.multiple_of((base + rows + r + t) * 8, 8)
                    part = product[:, t * EZ : (t + 1) * EZ]
                    low = w_ref[pl.ds(here, 16), :] * part[0:16]
                    high = w_ref[pl.ds(there, 16), :] * part[16:32]
                    both = low + high
                    s_ref[pl.ds((g * rows + r + t) * 8, 8), :] = both[0:8] + both[8:16]
            total = None
            for s in (0, 1, 2, 4, 5, 6):
                term = s_ref[pl.ds(g * rows * 8 + s, rows, stride=8), :]
                total = term if total is None else total + term
            e_ref[out_first + i * group + g] = total
        return 0

    if count == group:
        step(0, 0)
    else:
        lax.fori_loop(0, count // group, step, 0)


def odd_place(axis):
    return lax.axis_index(axis) % 2 == 1


def pack_kernel(local_ref, top_ref, dens_ref, dofs_ref, even_ref, odd_ref, tops_ref, l_ref, t_ref, d_ref, c_ref, sem):
    copies = [pltpu.make_async_copy(top_ref, t_ref, sem.at[0]), pltpu.make_async_copy(dens_ref, d_ref, sem.at[1]),
              pltpu.make_async_copy(dofs_ref, c_ref, sem.at[2])]
    for side, node in ((0, EX - RADIUS), (1, 0)):
        for c in range(3):
            copies.append(pltpu.make_async_copy(local_ref.at[c, node : node + 4], l_ref.at[side, c], sem.at[len(copies)]))
    for copy in copies:
        copy.start()
    even_ref[...] = jnp.zeros(even_ref.shape, F32)
    odd_ref[...] = jnp.zeros(odd_ref.shape, F32)
    tops_ref[...] = jnp.zeros(tops_ref.shape, F32)
    for copy in copies:
        copy.wait()
    for c in range(3):
        for i in range(NX):
            tops_ref[c, i : i + 1, 0:NY] = t_ref[c, i]
    odd = odd_place("gx")
    for out_ref, flip in ((even_ref, odd), (odd_ref, jnp.logical_not(odd))):
        side = flip.astype(jnp.int32)
        for c in range(3):
            for j in range(4):
                out_ref[c * 4 + j, 0:NY, :] = l_ref[side, c, j]
                out_ref[c * 4 + j, NY : NY + 1, :] = jnp.where(
                    flip, tops_ref[c, j : j + 1, :], tops_ref[c, EX - RADIUS + j : EX - RADIUS + j + 1, :])
        for j in range(3):
            out_ref[12 + j, 0:EY, :] = jnp.where(
                flip, d_ref[pl.ds(j, EY, stride=EX), :], d_ref[pl.ds(EX - RADIUS + j, EY, stride=EX), :])
        out_ref[12, EY : EY + 1, 0:8] = c_ref[...].astype(F32)


def sort_sides(axis, even_ref, odd_ref, low_ref, high_ref):
    odd = odd_place(axis)
    even, other = even_ref[...], odd_ref[...]
    low_ref[...] = jnp.where(odd, even, other)
    high_ref[...] = jnp.where(odd, other, even)


def own_kernel(shared, local_ref, stiff_ref, coarse_ref, dofs_ref, own_ref, e_ref, lhs_ref, w_ref, b_ref, s_ref):
    corners = corner_scalars(coarse_ref, lambda k: dofs_ref[k], shared)
    for i in range(NX):
        for c in range(3):
            own_ref[c * NX + i, 0:NY, :] = local_ref[c, i] + plane_interp(corners, c, i, NY)
            own_ref[c * NX + i, NY:ROWS, :] = jnp.zeros((ROWS - NY, EZ), F32)
    stiff = stiff_ref[...]
    lhs = stiffness_rows(stiff, False)
    lhs_ref[0] = lhs
    lhs_ref[1] = stiffness_rows(stiff, True)
    s_ref[...] = jnp.zeros(s_ref.shape, F32)
    build_nodes(lambda c, p: own_ref[c * NX + p + 1], range(EX - 1), ROWS, w_ref, b_ref)
    energy_planes(lhs, w_ref, b_ref, s_ref, e_ref, 0, EX - 2, ROWS, range(1, EY - 1, 2), 0, EX - 2)


def average(flag, low, high, own):
    return jnp.where(flag, 0.5 * low + 0.5 * high, own)


def has_lower(axis):
    return lax.axis_index(axis) > 0


def has_upper(axis):
    return lax.axis_index(axis) < lax.axis_size(axis) - 1


def message_dofs(message_ref):
    row = message_ref[12, EY : EY + 1, :]
    lane = iota((1, EZ), 1)
    return lambda k: jnp.sum(jnp.where(lane == k, row, 0.0)).astype(jnp.int32)


def top_interp(corners, c, rows):
    rx = iota((rows, EZ), 0).astype(F32) * (1.0 / EX)
    ry = iota((rows, EZ), 1).astype(F32) * (1.0 / EY)
    low = (1.0 - ry) * corners[c][1] + ry * corners[c][3]
    high = (1.0 - ry) * corners[c][5] + ry * corners[c][7]
    return (1.0 - rx) * low + rx * high


TOP_AT = 368
Y_MESSAGE = 392


def x_kernel(shared, own_ref, top_ref, dens_ref, even_ref, odd_ref, coarse_ref, dofs_ref,
             xl_ref, xh_ref, tx_ref, yeven_ref, yodd_ref, low_ref, high_ref, up_ref, down_ref, t_ref):
    sort_sides("gx", even_ref, odd_ref, low_ref, high_ref)
    corners = corner_scalars(coarse_ref, lambda k: dofs_ref[k], shared)
    corners_low = corner_scalars(coarse_ref, message_dofs(low_ref), shared)
    corners_high = corner_scalars(coarse_ref, message_dofs(high_ref), shared)
    lower, upper = has_lower("gx"), has_upper("gx")
    for c in range(3):
        for j in range(4):
            value = low_ref[c * 4 + j] + plane_interp(corners_low, c, EX - RADIUS + j, ROWS)
            if j == 3:
                mine = own_ref[c * NX]
                value = average(lower, value, mine, mine)
            xl_ref[c * 4 + j] = value
            value = high_ref[c * 4 + j] + plane_interp(corners_high, c, j, ROWS)
            if j == 0:
                mine = own_ref[c * NX + EX]
                value = average(upper, mine, value, mine)
            xh_ref[c * 4 + j] = value

    t_ref[...] = jnp.zeros(t_ref.shape, F32)
    for c in range(3):
        t_ref[0] = top_ref[c] + top_interp(corners, c, XR)
        for j in range(4):
            t_ref[1, j : j + 1, 0:NY] = low_ref[c * 4 + j, NY : NY + 1, 0:NY]
            t_ref[2, j : j + 1, 0:NY] = high_ref[c * 4 + j, NY : NY + 1, 0:NY]
        t_low = t_ref[1, 0:8, :] + pltpu.roll(top_interp(corners_low, c, 24), 24 - (EX - RADIUS), 0)[0:8]
        t_high = t_ref[2, 0:8, :] + top_interp(corners_high, c, 8)
        first = average(lower, t_low[3:4], t_ref[0, 0:1, :], t_ref[0, 0:1, :])
        last = average(upper, t_ref[0, EX : EX + 1, :], t_high[0:1], t_ref[0, EX : EX + 1, :])
        t_ref[3, 0:3, :] = t_low[0:3]
        t_ref[3, 3:4, :] = first
        t_ref[3, 4:19, :] = t_ref[0, 1:EX, :]
        t_ref[3, 19:20, :] = last
        t_ref[3, 20:23, :] = t_high[1:4]
        lane = iota((XR, EZ), 1)
        tx_ref[c] = jnp.where(lane < NY + 8, pltpu.roll(t_ref[3], 8, 1), 0.0)

    def plane(c, p):
        if p < 4:
            return xl_ref[c * 4 + p]
        if p < 19:
            return own_ref[c * NX + p - 3]
        return xh_ref[c * 4 + p - 19]

    def density(x):
        if x < 3:
            return low_ref[12 + x, 0:EY, :]
        if x < 19:
            return dens_ref[pl.ds(x - 3, EY, stride=EX), :]
        return high_ref[12 + x - 19, 0:EY, :]

    for out_ref, node, elem, lane_at in ((up_ref, EY - RADIUS, EY - RADIUS, EY - RADIUS + 8), (down_ref, 0, 0, 8)):
        for c in range(3):
            for p in range(XN):
                at = (c * XN + p) * 4
                out_ref[at : at + 4, :] = plane(c, p)[node : node + 4]
        for x in range(XE):
            at = 3 * XN * 4 + x * 4
            out_ref[at : at + 3, :] = density(x)[elem : elem + 3]
            out_ref[at + 3 : at + 4, :] = jnp.zeros((1, EZ), F32)
        out_ref[364:TOP_AT, :] = jnp.zeros((TOP_AT - 364, EZ), F32)
        lane = iota((XR, EZ), 1)
        total = jnp.zeros((XR, EZ), F32)
        for c in range(3):
            moved = pltpu.roll(tx_ref[c], (4 * c - lane_at) % EZ, 1)
            total = jnp.where((lane >= 4 * c) & (lane < 4 * c + 4), moved, total)
        out_ref[TOP_AT:Y_MESSAGE, :] = total
    sort_sides("gy", up_ref, down_ref, yodd_ref, yeven_ref)


def side_kernel(own_ref, xl_ref, xh_ref, lhs_ref, e_ref, w_ref, b_ref, s_ref):
    s_ref[...] = jnp.zeros(s_ref.shape, F32)

    def plane(c, p):
        if p < 4:
            return xl_ref[c * 4 + p]
        if p == 4:
            return own_ref[c * NX + 1]
        if p == 5:
            return own_ref[c * NX + EX - 1]
        return xh_ref[c * 4 + p - 6]

    build_nodes(plane, range(10), ROWS, w_ref, b_ref)
    lhs = lhs_ref[0]
    for first, out_first in ((0, 0), (5, 4)):
        energy_planes(lhs, w_ref, b_ref, s_ref, e_ref, first, 4, ROWS, range(1, EY - 1, 2), out_first, 4)


Z_MESSAGE = 192


def y_kernel(own_ref, xl_ref, xh_ref, tx_ref, dens_ref, lowx_ref, highx_ref, even_ref, odd_ref,
             first_ref, last_ref, dext_ref, oa_ref, ob_ref, od_ref, zeven_ref, zodd_ref,
             z_ref, d_ref, low_ref, high_ref, up_ref, down_ref):
    sort_sides("gy", even_ref, odd_ref, low_ref, high_ref)
    lower, upper = has_lower("gy"), has_upper("gy")

    def plane(c, p):
        if p < 4:
            return xl_ref[c * 4 + p]
        if p < 19:
            return own_ref[c * NX + p - 3]
        return xh_ref[c * 4 + p - 19]

    def keep_planes(dest, at, step, block):
        turned = block.T
        dest[pl.ds(at, 8, stride=step), 0:64] = jnp.concatenate([turned[0:4], turned[EZ - 4 : EZ]], axis=0)

    pad = jnp.zeros((64 - QROWS, EZ), F32)
    z_ref[...] = jnp.zeros(z_ref.shape, F32)
    d_ref[...] = jnp.zeros(d_ref.shape, F32)
    for c in range(3):
        for p in range(XN):
            i = c * XN + p
            mine = plane(c, p)
            first_ref[i, 0:5, :] = jnp.zeros((5, EZ), F32)
            first_ref[i, 5:8, :] = low_ref[i * 4 : i * 4 + 3, :]
            first_ref[i, 8:16, :] = mine[0:8]
            first_ref[i, 8:9, :] = average(lower, low_ref[i * 4 + 3 : i * 4 + 4, :], mine[0:1], mine[0:1])
            last_ref[i, 0:4, :] = mine[40:44]
            last_ref[i, 4:5, :] = average(upper, mine[44:45], high_ref[i * 4 : i * 4 + 1, :], mine[44:45])
            last_ref[i, 5:8, :] = high_ref[i * 4 + 1 : i * 4 + 4, :]
            keep_planes(z_ref, c * XR + p, 3 * XR, jnp.concatenate([first_ref[i], mine[8:40], last_ref[i], pad], axis=0))

    dext_ref[...] = jnp.zeros(dext_ref.shape, F32)
    for x in range(XE):
        at = 3 * XN * 4 + x * 4
        if x < 3:
            mine = lowx_ref[12 + x, 0:EY, :]
        elif x < 19:
            mine = dens_ref[pl.ds(x - 3, EY, stride=EX), :]
        else:
            mine = highx_ref[12 + x - 19, 0:EY, :]
        dext_ref[x, 8 : 8 + EY, :] = mine
        dext_ref[x, 5:8, :] = low_ref[at : at + 3, :]
        dext_ref[x, 52:55, :] = high_ref[at : at + 3, :]
        keep_planes(d_ref, x, XR, jnp.concatenate([dext_ref[x], pad], axis=0))

    lane = iota((XR, EZ), 1)
    tops = []
    for c in range(3):
        mine = tx_ref[c]
        low = pltpu.roll(low_ref[TOP_AT:Y_MESSAGE, :], (5 - 4 * c) % EZ, 1)
        high = pltpu.roll(high_ref[TOP_AT:Y_MESSAGE, :], (52 - 4 * c) % EZ, 1)
        value = jnp.where((lane >= 5) & (lane < 8), low, mine)
        value = jnp.where(lane == 8, average(lower, low, mine, mine), value)
        value = jnp.where(lane == 52, average(upper, mine, high, mine), value)
        tops.append(jnp.where((lane > 52) & (lane < 56), high, value))
    top = jnp.concatenate(tops, axis=0)

    def nodes(k):
        return z_ref[k * 3 * XR : (k + 1) * 3 * XR, :]

    def dens(k):
        return d_ref[k * XR : (k + 1) * XR, :]

    def pack(low, high):
        return low + pltpu.roll(high, 64, 1)

    oa_ref[...] = pack(nodes(0), top)
    ob_ref[...] = pack(nodes(1), nodes(7))
    od_ref[...] = pack(dens(0), dens(7))
    up_ref[0:72, :] = pack(nodes(5), nodes(6))
    up_ref[72:144, :] = pack(nodes(7), top)
    up_ref[144:168, :] = pack(dens(5), dens(6))
    up_ref[168:192, :] = dens(7)
    down_ref[0:72, :] = pack(nodes(0), nodes(1))
    down_ref[72:144, :] = pack(nodes(2), nodes(3))
    down_ref[144:168, :] = pack(dens(0), dens(1))
    down_ref[168:192, :] = dens(2)
    sort_sides("gz", up_ref, down_ref, zodd_ref, zeven_ref)


def edge_kernel(own_ref, xl_ref, xh_ref, first_ref, last_ref, lhs_ref, el_ref, eh_ref, w_ref, b_ref, s_ref):
    s_ref[...] = jnp.zeros(s_ref.shape, F32)
    lhs = lhs_ref[0]
    build_nodes(lambda c, p: first_ref[c * XN + p], range(XN), 16, w_ref, b_ref)
    energy_planes(lhs, w_ref, b_ref, s_ref, el_ref, 0, XE, 16, (5, 7), 0, XE)
    build_nodes(lambda c, p: last_ref[c * XN + p], range(XN), 8, w_ref, b_ref)
    energy_planes(lhs, w_ref, b_ref, s_ref, eh_ref, 0, XE, 8, (3, 5), 0, XE)


def triangle(value, axis):
    size = value.shape[axis]
    value = value + pltpu.roll(value, size - 1, axis)
    value = value + pltpu.roll(value, size - 2, axis)
    value = value + pltpu.roll(value, 1, axis)
    return value + pltpu.roll(value, 2, axis)


def weights(distance):
    return jnp.maximum(4 - jnp.abs(distance), 0).astype(F32)


def three_parts(value):
    high = value.astype(BF16)
    rest = value - high.astype(F32)
    middle = rest.astype(BF16)
    return high, middle, (rest - middle.astype(F32)).astype(BF16)


def exact_dot(value, right):
    parts = [jnp.dot(part, right, preferred_element_type=F32) for part in three_parts(value)]
    return parts[0] + parts[1] + parts[2]


def edge_total(count, position, parts):
    total = None
    for offset in range(-RADIUS, RADIUS + 1):
        place = position + offset
        term = float(RADIUS + 1 - abs(offset)) * one_hot((place >= 0) & (place < count * parts))
        total = term if total is None else total + term
    return total


def last_kernel(ea_ref, eb_ref, el_ref, eh_ref, dext_ref, oa_ref, ob_ref, od_ref, even_ref, odd_ref, lhs_ref,
                sens_ref, smooth_ref, w_ref, b_ref, s_ref, ez_ref, f_ref, g_ref, c_ref, zl_ref, zh_ref):
    sort_sides("gz", even_ref, odd_ref, zl_ref, zh_ref)
    lower, upper = has_lower("gz"), has_upper("gz")

    def swap(value):
        return pltpu.roll(value, 64, 1)

    is_low = iota((3 * XR, EZ), 1) < 64
    oa, ob = oa_ref[...], ob_ref[...]
    zl0, zl1 = zl_ref[0:72, :], zl_ref[72:144, :]
    zh0, zh1 = zh_ref[0:72, :], zh_ref[72:144, :]
    nodes = (
        jnp.where(is_low, zl0, ob),
        jnp.where(is_low, swap(zl0), average(upper, oa, swap(zh0), oa)),
        jnp.where(is_low, zl1, zh0),
        jnp.where(is_low, average(lower, swap(zl1), oa, oa), swap(zh1)),
        jnp.where(is_low, ob, zh1),
    )
    build_nodes(lambda c, k: nodes[k][c * XR : (c + 1) * XR], range(5), XR, w_ref, b_ref)
    s_ref[...] = jnp.zeros(s_ref.shape, F32)
    energy_planes(lhs_ref[1], w_ref, b_ref, s_ref, ez_ref, 0, 4, XR, range(0, XE, 2), 0, 4)

    lane = iota((XR, EZ), 1)
    low_side = lane < 64
    od = od_ref[...]
    dl0, dl1 = zl_ref[144:168, :], zl_ref[168:192, :]
    dh0, dh1 = zh_ref[144:168, :], zh_ref[168:192, :]
    dens = (
        jnp.where(low_side, dl0, od),
        jnp.where(low_side, swap(dl0), swap(dh0)),
        jnp.where(low_side, dl1, dh0),
        jnp.where(low_side, od, swap(dh1)),
    )
    inside = (lane % 64 >= 5) & (lane % 64 < 55) & (iota((XR, EZ), 0) < XE)
    for j in range(4):
        d = dens[j]
        for f, value in ((0, (SCALE * d) * d * d * ez_ref[j]), (1, d)):
            value = triangle_forward(jnp.where(inside, value, 0.0))
            c_ref[f, j * EX : (j + 1) * EX, :] = value[0:EX]
    row, col = iota((EZ, EZ), 0), iota((EZ, EZ), 1)
    along_y = jnp.where(row // 64 == col // 64, weights(row - col), 0.0).astype(BF16)

    rows = iota((QROWS, EZ), 0)
    lanes = iota((QROWS, EZ), 1)
    ok = (rows >= 5) & (rows < 55) & (lanes > 0) & (lanes < EZ - 1)
    for x in range(XE):
        if x < 4:
            middle = eb_ref[x]
        elif x < 18:
            middle = ea_ref[x - 4]
        else:
            middle = eb_ref[x - 14]
        start = jnp.where(rows[0:8] < 1, el_ref[x, 8:16, :], middle[0:8])
        end = jnp.where(rows[0:8] < 3, middle[40:48], eh_ref[x])
        energy = jnp.concatenate([el_ref[x, 0:8, :], start, middle[8:40], end], axis=0)
        d = dext_ref[x]
        f_ref[0, x] = jnp.where(ok, (SCALE * d) * d * d * energy, 0.0)
        f_ref[1, x] = jnp.where(ok, d, 0.0)

    for f in range(2):
        for t in range(QROWS // 8):
            at = slice(t * 8, t * 8 + 8)
            line = [f_ref[f, x, at, :] for x in range(XE)]
            for step in (1, 2, 1, 2):
                line = [line[i] + line[i + step] for i in range(len(line) - step)]
            for x in range(EX):
                g_ref[f, x, at, :] = line[x]

    k = iota((EZ, EZ), 0)
    j = (k % 64) // EX
    place = jnp.where(k < 64, j - 3, EZ - 1 + j)
    z = iota((EZ, EZ), 1)
    right = jnp.concatenate([weights(k - z), weights(place - z)], axis=0).astype(BF16)

    ends = []
    for f in range(2):
        turned = exact_dot(c_ref[f], along_y)
        turned = jnp.concatenate([turned, jnp.zeros((EZ - 4 * EX, EZ), F32)], axis=0).T
        ends.append(turned[8:56] + pltpu.roll(turned[72:120], 64, 1))

    base_x, base_y, base_z = lax.axis_index("gx") * EX, lax.axis_index("gy") * EY, lax.axis_index("gz") * EZ
    norm_y = edge_total(EY, base_y + iota((ROWS, EZ), 0), lax.axis_size("gy"))
    norm_z = edge_total(EZ, base_z + iota((ROWS, EZ), 1), lax.axis_size("gz"))
    norm_yz = norm_y * norm_z
    lanes = iota((ROWS, EZ), 1)
    for x in range(EX):
        sums = []
        for f in range(2):
            body = triangle(g_ref[f, x], 0)[8:QROWS]
            tail = jnp.where(lanes % EX == x, ends[f], 0.0)
            sums.append(exact_dot(jnp.concatenate([body, tail], axis=1), right))
        norm = norm_yz * edge_total(EX, base_x + x, lax.axis_size("gx"))
        d = dext_ref[x + 3, 8:QROWS, :]
        d = jnp.where(rows[0:ROWS] < EY, d, 1.0)
        sens_ref[pl.ds(x, EY, stride=EX), :] = (sums[0] / (d * norm))[0:EY]
        smooth_ref[pl.ds(x, EY, stride=EX), :] = (sums[1] / norm)[0:EY]


def triangle_forward(value):
    size = value.shape[0]
    for step in (1, 2, 1, 2):
        value = value + pltpu.roll(value, size - step, 0)
    return value


def call(kernel, outs, ins, scratch=(), limit=16, micros=1.0):
    return pl.pallas_call(
        kernel,
        out_shape=[jax.ShapeDtypeStruct(shape, dtype) for shape, dtype in outs],
        in_specs=[pl.BlockSpec(memory_space=space) for space in ins],
        out_specs=[pl.BlockSpec(memory_space=VM)] * len(outs),
        scratch_shapes=[pltpu.VMEM(item[0], item[1]) if isinstance(item, tuple) else item for item in scratch],
        compiler_params=pltpu.CompilerParams(vmem_limit_bytes=limit * 2**20),
        cost_estimate=pl.CostEstimate(flops=0, bytes_accessed=int(micros * 3.6e6), transcendentals=0),
    )


def exchange(even, odd, axis):
    count = lax.axis_size(axis)
    results = []
    for value, first in ((even, 0), (odd, 1)):
        pairs = [(i, i + 1) for i in range(first, count - 1, 2)]
        if pairs:
            results.append(lax.ppermute(value, axis, pairs + [(j, i) for i, j in pairs]))
        else:
            results.append(jnp.zeros_like(value))
    return results


def local(local_solution, top_nodes, coarse_solution, corner_dofs, density, element_stiffness):
    dens = jnp.transpose(density, (1, 0, 2)).reshape(EY * EX, EZ)
    dofs = corner_dofs.reshape(8)
    shared = lax.axis_size("gz") == 2
    if shared:
        other = lax.ppermute(coarse_solution, "gz", [(0, 1), (1, 0)])
        coarse = jnp.stack([coarse_solution, other])
    else:
        coarse = lax.all_gather(coarse_solution, "gz")

    message = ((15, ROWS, EZ), F32)
    even, odd, tops = call(
        pack_kernel,
        [message, message, ((3, XR, EZ), F32)],
        [pltpu.HBM] * 4,
        [((2, 3, 4, NY, EZ), F32), ((3, NX, 1, NY), F32), ((EY * EX, EZ), F32), ((1, 8), jnp.int32), pltpu.SemaphoreType.DMA((9,))],
    )(local_solution, jnp.transpose(top_nodes, (0, 1, 3, 2)), dens, dofs.reshape(1, 8))
    even_x, odd_x = exchange(even, odd, "gx")

    def nodes(count):
        return [((count * 8, EZ), F32), ((count * 16, EZ), BF16)]

    own, ea, lhs = call(
        functools.partial(own_kernel, shared),
        [((3 * NX, ROWS, EZ), F32), ((EX - 2, ROWS, EZ), F32), ((2, 64, 64), BF16)],
        [VM, VM, SM, SM],
        nodes((EX - 1) * ROWS) + [(((EX - 2) * ROWS * 8, EZ), F32)],
        micros=6.0,
    )(local_solution, element_stiffness, coarse, dofs)

    face = ((12, ROWS, EZ), F32)
    y_message = ((Y_MESSAGE, EZ), F32)
    xl, xh, tx, even, odd, low_x, high_x = call(
        functools.partial(x_kernel, shared),
        [face, face, ((3, XR, EZ), F32), y_message, y_message, message, message],
        [VM, VM, VM, VM, VM, SM, SM],
        [y_message, y_message, ((4, XR, EZ), F32)],
        micros=2.0,
    )(own, tops, dens, even_x, odd_x, coarse, dofs)
    even_y, odd_y = exchange(even, odd, "gy")

    (eb,) = call(
        side_kernel, [((8, ROWS, EZ), F32)], [VM] * 4, nodes(10 * ROWS) + [((4 * ROWS * 8, EZ), F32)], micros=3.5
    )(own, xl, xh, lhs)

    z_message = ((Z_MESSAGE, EZ), F32)
    first, last, dext, oa, ob, od, even, odd = call(
        y_kernel,
        [((3 * XN, 16, EZ), F32), ((3 * XN, 8, EZ), F32), ((XE, QROWS, EZ), F32), ((72, EZ), F32), ((72, EZ), F32),
         ((XR, EZ), F32), z_message, z_message],
        [VM] * 9,
        [((8 * 3 * XR, EZ), F32), ((8 * XR, EZ), F32), y_message, y_message, z_message, z_message],
        micros=2.7,
    )(own, xl, xh, tx, dens, low_x, high_x, even_y, odd_y)
    even_z, odd_z = exchange(even, odd, "gz")

    el, eh = call(
        edge_kernel,
        [((XE, 16, EZ), F32), ((XE, 8, EZ), F32)],
        [VM] * 6,
        nodes(XN * 16) + [((XE * 16 * 8, EZ), F32)],
        micros=3.0,
    )(own, xl, xh, first, last, lhs)

    sens, smooth = call(
        last_kernel,
        [((EY * EX, EZ), F32)] * 2,
        [VM] * 11,
        nodes(5 * XR) + [((4 * XR * 8, EZ), F32), ((4, XR, EZ), F32), ((2, XE, QROWS, EZ), F32), ((2, EX, QROWS, EZ), F32),
                         ((2, 4 * EX, EZ), F32), z_message, z_message],
        micros=4.3,
    )(ea, eb, el, eh, dext, oa, ob, od, even_z, odd_z, lhs)

    def grid(value):
        return jnp.transpose(value.reshape(EY, EX, EZ), (1, 0, 2))

    return grid(sens), grid(smooth)


def solution(mesh):
    in_specs = (
        P(None, "gx", "gy", "gz"),
        P(None, "gx", "gy", "gz"),
        P(None, "gz"),
        P("gx", "gy", "gz", None),
        P("gx", "gy", "gz"),
        P(),
    )
    out_specs = (P("gx", "gy", "gz"), P("gx", "gy", "gz"))
    return jax.shard_map(local, mesh=mesh, in_specs=in_specs, out_specs=out_specs, check_vma=False)
```

```python
import functools

import jax
import jax.numpy as jnp
from jax import lax
from jax.experimental import pallas as pl
from jax.experimental.pallas import tpu as pltpu
from jax.sharding import PartitionSpec as P

RADIUS = 3
F32 = jnp.float32
BF16 = jnp.bfloat16
SCALE = -3.0 / 96.0
HIGHEST = lax.Precision.HIGHEST
VM = pltpu.VMEM
SM = pltpu.SMEM

EX, EY, EZ = 16, 44, 128
NX, NY = EX + 1, EY + 1
XN, XE = NX + 2 * RADIUS, EX + 2 * RADIUS
ROWS = 48
QROWS = 56
XR = 24


def iota(shape, dim):
    return lax.broadcasted_iota(jnp.int32, shape, dim)


def one_hot(mask):
    return jnp.where(mask, 1.0, 0.0).astype(F32)


def halves(value):
    high = value.astype(BF16)
    return high, (value - high.astype(F32)).astype(BF16)


def corner_scalars(coarse_ref, dof_of, shared):
    width = coarse_ref.shape[2]
    own = lax.axis_index("gz")
    out = [[None] * 8 for _ in range(3)]
    for k in range(8):
        dof = dof_of(k)
        part = dof // width
        place = dof - part * width
        if shared:
            part = jnp.where(part == own, 0, 1)
        for c in range(3):
            out[c][k] = coarse_ref[part, c, place]
    return out


def plane_scalars(corners, c, i):
    wx = i / EX
    return [(1.0 - wx) * corners[c][m] + wx * corners[c][4 + m] for m in range(4)]


def plane_interp(corners, c, i, rows):
    low_low, low_high, high_low, high_high = plane_scalars(corners, c, i)
    rz = iota((1, EZ), 1).astype(F32) * (1.0 / EZ)
    ry = iota((rows, EZ), 0).astype(F32) * (1.0 / EY)
    first = low_low * (1.0 - rz) + low_high * rz
    second = high_low * (1.0 - rz) + high_high * rz
    return (1.0 - ry) * first + ry * second


def stiffness_rows(stiff, in_lanes):
    def target(m, r):
        s, c = r // 4, r % 4
        if in_lanes:
            return jnp.where(c < 3, 8 * c + 4 * (m % 2) + 2 * s + m // 2, -1)
        return jnp.where(c < 3, 8 * c + 2 * m + s, -1)

    row = iota((32, 24), 0)
    left = one_hot(iota((32, 24), 1) == target(row // 8, row % 8))
    col = iota((24, 64), 1)
    right = one_hot(iota((24, 64), 0) == target(col // 16, col % 8))
    full = jnp.dot(left, stiff, precision=HIGHEST, preferred_element_type=F32)
    full = jnp.dot(full, right, precision=HIGHEST, preferred_element_type=F32)
    high = full.astype(BF16).astype(F32)
    return jnp.concatenate([high, full - high], axis=0).astype(BF16)


def build_nodes(plane_of, planes, rows, w_ref, b_ref, first=0):
    for p in planes:
        base = (first + p) * rows * 8
        zero = jnp.zeros((rows, EZ), F32)
        for c in range(3):
            value = plane_of(c, p)
            w_ref[pl.ds(base + c, rows, stride=8), :] = value
            w_ref[pl.ds(base + 4 + c, rows, stride=8), :] = pltpu.roll(value, EZ - 1, 1)
        w_ref[pl.ds(base + 3, rows, stride=8), :] = zero
        w_ref[pl.ds(base + 7, rows, stride=8), :] = zero

    count = len(planes)

    def split(p, _):
        base = (first + p) * rows
        for r in range(rows):
            value = w_ref[pl.ds(pl.multiple_of((base + r) * 8, 8), 8), :]
            high = value.astype(BF16).astype(F32)
            b_ref[pl.ds(pl.multiple_of((base + r) * 16, 16), 16), :] = jnp.concatenate([high, value - high], axis=0).astype(BF16)
        return 0

    lax.fori_loop(0, count, split, 0)


def energy_planes(lhs, w_ref, b_ref, s_ref, e_ref, first, count, rows, starts, out_first, group):
    def step(i, _):
        for g in range(group):
            base = (first + i * group + g) * rows
            for r in starts:
                right = []
                for t in (0, 1):
                    here = pl.multiple_of((base + r + t) * 16, 16)
                    there = pl.multiple_of((base + rows + r + t) * 16, 16)
                    right.append(jnp.concatenate([b_ref[pl.ds(here, 32), :], b_ref[pl.ds(there, 32), :]], axis=0))
                product = jnp.dot(lhs, jnp.concatenate(right, axis=1), preferred_element_type=F32)
                product = product[0:32] + product[32:64]
                for t in (0, 1):
                    here = pl.multiple_of((base + r + t) * 8, 8)
                    there = pl.multiple_of((base + rows + r + t) * 8, 8)
                    part = product[:, t * EZ : (t + 1) * EZ]
                    low = w_ref[pl.ds(here, 16), :] * part[0:16]
                    high = w_ref[pl.ds(there, 16), :] * part[16:32]
                    both = low + high
                    s_ref[pl.ds((g * rows + r + t) * 8, 8), :] = both[0:8] + both[8:16]
            total = None
            for s in (0, 1, 2, 4, 5, 6):
                term = s_ref[pl.ds(g * rows * 8 + s, rows, stride=8), :]
                total = term if total is None else total + term
            e_ref[out_first + i * group + g] = total
        return 0

    if count == group:
        step(0, 0)
    else:
        lax.fori_loop(0, count // group, step, 0)


def odd_place(axis):
    return lax.axis_index(axis) % 2 == 1


def pack_kernel(local_ref, top_ref, dens_ref, dofs_ref, even_ref, odd_ref, tops_ref, l_ref, t_ref, d_ref, c_ref, sem):
    copies = [pltpu.make_async_copy(top_ref, t_ref, sem.at[0]), pltpu.make_async_copy(dens_ref, d_ref, sem.at[1]),
              pltpu.make_async_copy(dofs_ref, c_ref, sem.at[2])]
    for side, node in ((0, EX - RADIUS), (1, 0)):
        for c in range(3):
            copies.append(pltpu.make_async_copy(local_ref.at[c, node : node + 4], l_ref.at[side, c], sem.at[len(copies)]))
    for copy in copies:
        copy.start()
    even_ref[...] = jnp.zeros(even_ref.shape, F32)
    odd_ref[...] = jnp.zeros(odd_ref.shape, F32)
    tops_ref[...] = jnp.zeros(tops_ref.shape, F32)
    for copy in copies:
        copy.wait()
    for c in range(3):
        for i in range(NX):
            tops_ref[c, i : i + 1, 0:NY] = t_ref[c, i]
    odd = odd_place("gx")
    for out_ref, flip in ((even_ref, odd), (odd_ref, jnp.logical_not(odd))):
        side = flip.astype(jnp.int32)
        for c in range(3):
            for j in range(4):
                out_ref[c * 4 + j, 0:NY, :] = l_ref[side, c, j]
                out_ref[c * 4 + j, NY : NY + 1, :] = jnp.where(
                    flip, tops_ref[c, j : j + 1, :], tops_ref[c, EX - RADIUS + j : EX - RADIUS + j + 1, :])
        for j in range(3):
            out_ref[12 + j, 0:EY, :] = jnp.where(
                flip, d_ref[pl.ds(j, EY, stride=EX), :], d_ref[pl.ds(EX - RADIUS + j, EY, stride=EX), :])
        out_ref[12, EY : EY + 1, 0:8] = c_ref[...].astype(F32)


def sort_sides(axis, even_ref, odd_ref, low_ref, high_ref):
    odd = odd_place(axis)
    even, other = even_ref[...], odd_ref[...]
    low_ref[...] = jnp.where(odd, even, other)
    high_ref[...] = jnp.where(odd, other, even)


def own_kernel(shared, local_ref, stiff_ref, coarse_ref, dofs_ref, own_ref, e_ref, lhs_ref, w_ref, b_ref, s_ref):
    corners = corner_scalars(coarse_ref, lambda k: dofs_ref[k], shared)
    for i in range(NX):
        for c in range(3):
            own_ref[c * NX + i, 0:NY, :] = local_ref[c, i] + plane_interp(corners, c, i, NY)
            own_ref[c * NX + i, NY:ROWS, :] = jnp.zeros((ROWS - NY, EZ), F32)
    stiff = stiff_ref[...]
    lhs = stiffness_rows(stiff, False)
    lhs_ref[0] = lhs
    lhs_ref[1] = stiffness_rows(stiff, True)
    s_ref[...] = jnp.zeros(s_ref.shape, F32)
    build_nodes(lambda c, p: own_ref[c * NX + p + 1], range(EX - 1), ROWS, w_ref, b_ref)
    energy_planes(lhs, w_ref, b_ref, s_ref, e_ref, 0, EX - 2, ROWS, range(1, EY - 1, 2), 0, EX - 2)


def average(flag, low, high, own):
    return jnp.where(flag, 0.5 * low + 0.5 * high, own)


def has_lower(axis):
    return lax.axis_index(axis) > 0


def has_upper(axis):
    return lax.axis_index(axis) < lax.axis_size(axis) - 1


def message_dofs(message_ref):
    row = message_ref[12, EY : EY + 1, :]
    lane = iota((1, EZ), 1)
    return lambda k: jnp.sum(jnp.where(lane == k, row, 0.0)).astype(jnp.int32)


def top_interp(corners, c, rows):
    rx = iota((rows, EZ), 0).astype(F32) * (1.0 / EX)
    ry = iota((rows, EZ), 1).astype(F32) * (1.0 / EY)
    low = (1.0 - ry) * corners[c][1] + ry * corners[c][3]
    high = (1.0 - ry) * corners[c][5] + ry * corners[c][7]
    return (1.0 - rx) * low + rx * high


TOP_AT = 368
Y_MESSAGE = 392


def x_kernel(shared, own_ref, top_ref, dens_ref, even_ref, odd_ref, coarse_ref, dofs_ref,
             xl_ref, xh_ref, tx_ref, yeven_ref, yodd_ref, low_ref, high_ref, up_ref, down_ref, t_ref):
    sort_sides("gx", even_ref, odd_ref, low_ref, high_ref)
    corners = corner_scalars(coarse_ref, lambda k: dofs_ref[k], shared)
    corners_low = corner_scalars(coarse_ref, message_dofs(low_ref), shared)
    corners_high = corner_scalars(coarse_ref, message_dofs(high_ref), shared)
    lower, upper = has_lower("gx"), has_upper("gx")
    for c in range(3):
        for j in range(4):
            value = low_ref[c * 4 + j] + plane_interp(corners_low, c, EX - RADIUS + j, ROWS)
            if j == 3:
                mine = own_ref[c * NX]
                value = average(lower, value, mine, mine)
            xl_ref[c * 4 + j] = value
            value = high_ref[c * 4 + j] + plane_interp(corners_high, c, j, ROWS)
            if j == 0:
                mine = own_ref[c * NX + EX]
                value = average(upper, mine, value, mine)
            xh_ref[c * 4 + j] = value

    t_ref[...] = jnp.zeros(t_ref.shape, F32)
    for c in range(3):
        t_ref[0] = top_ref[c] + top_interp(corners, c, XR)
        for j in range(4):
            t_ref[1, j : j + 1, 0:NY] = low_ref[c * 4 + j, NY : NY + 1, 0:NY]
            t_ref[2, j : j + 1, 0:NY] = high_ref[c * 4 + j, NY : NY + 1, 0:NY]
        t_low = t_ref[1, 0:8, :] + pltpu.roll(top_interp(corners_low, c, 24), 24 - (EX - RADIUS), 0)[0:8]
        t_high = t_ref[2, 0:8, :] + top_interp(corners_high, c, 8)
        first = average(lower, t_low[3:4], t_ref[0, 0:1, :], t_ref[0, 0:1, :])
        last = average(upper, t_ref[0, EX : EX + 1, :], t_high[0:1], t_ref[0, EX : EX + 1, :])
        t_ref[3, 0:3, :] = t_low[0:3]
        t_ref[3, 3:4, :] = first
        t_ref[3, 4:19, :] = t_ref[0, 1:EX, :]
        t_ref[3, 19:20, :] = last
        t_ref[3, 20:23, :] = t_high[1:4]
        lane = iota((XR, EZ), 1)
        tx_ref[c] = jnp.where(lane < NY + 8, pltpu.roll(t_ref[3], 8, 1), 0.0)

    for out_ref, node, elem, lane_at in ((up_ref, EY - RADIUS, EY - RADIUS, EY - RADIUS + 8), (down_ref, 0, 0, 8)):
        for c in range(3):
            for p in range(XN):
                at = (c * XN + p) * 4
                out_ref[at : at + 4, :] = x_plane(own_ref, xl_ref, xh_ref, c, p)[node : node + 4]
        for x in range(XE):
            at = 3 * XN * 4 + x * 4
            out_ref[at : at + 3, :] = x_density(dens_ref, low_ref, high_ref, x)[elem : elem + 3]
            out_ref[at + 3 : at + 4, :] = jnp.zeros((1, EZ), F32)
        out_ref[364:TOP_AT, :] = jnp.zeros((TOP_AT - 364, EZ), F32)
        lane = iota((XR, EZ), 1)
        total = jnp.zeros((XR, EZ), F32)
        for c in range(3):
            moved = pltpu.roll(tx_ref[c], (4 * c - lane_at) % EZ, 1)
            total = jnp.where((lane >= 4 * c) & (lane < 4 * c + 4), moved, total)
        out_ref[TOP_AT:Y_MESSAGE, :] = total
    sort_sides("gy", up_ref, down_ref, yodd_ref, yeven_ref)


def side_kernel(own_ref, xl_ref, xh_ref, lhs_ref, e_ref, w_ref, b_ref, s_ref):
    s_ref[...] = jnp.zeros(s_ref.shape, F32)

    def plane(c, p):
        if p < 4:
            return xl_ref[c * 4 + p]
        if p == 4:
            return own_ref[c * NX + 1]
        if p == 5:
            return own_ref[c * NX + EX - 1]
        return xh_ref[c * 4 + p - 6]

    build_nodes(plane, range(10), ROWS, w_ref, b_ref)
    lhs = lhs_ref[0]
    for first, out_first in ((0, 0), (5, 4)):
        energy_planes(lhs, w_ref, b_ref, s_ref, e_ref, first, 4, ROWS, range(1, EY - 1, 2), out_first, 4)


Z_MESSAGE = 192
TILES = 3 * XN + XE


def x_plane(own_ref, xl_ref, xh_ref, c, p):
    if p < 4:
        return xl_ref[c * 4 + p]
    if p < 19:
        return own_ref[c * NX + p - 3]
    return xh_ref[c * 4 + p - 19]


def x_density(dens_ref, low_ref, high_ref, x):
    if x < 3:
        return low_ref[12 + x, 0:EY, :]
    if x < 19:
        return dens_ref[pl.ds(x - 3, EY, stride=EX), :]
    return high_ref[12 + x - 19, 0:EY, :]


def end_planes(turned):
    return jnp.concatenate([turned[0:4], turned[EZ - 4 : EZ]], axis=0)


def turn_kernel(own_ref, xl_ref, xh_ref, dens_ref, lowx_ref, highx_ref, z_ref):
    head = jnp.zeros((8, EZ), F32)
    tail = jnp.zeros((8, EZ), F32)
    for i in range(TILES):
        if i < 3 * XN:
            value = x_plane(own_ref, xl_ref, xh_ref, i // XN, i % XN)
        else:
            value = x_density(dens_ref, lowx_ref, highx_ref, i - 3 * XN)
            value = jnp.concatenate([value, jnp.zeros((ROWS - EY, EZ), F32)], axis=0)
        z_ref[i, :, 0:64] = end_planes(jnp.concatenate([head, value, tail], axis=0).T)
        z_ref[i, :, 64:EZ] = jnp.zeros((8, 64), F32)


def y_kernel(own_ref, xl_ref, xh_ref, tx_ref, zo_ref, eb_ref, even_ref, odd_ref,
             edge_ref, low_ref, high_ref, oa_ref, ob_ref, od_ref, zeven_ref, zodd_ref,
             z_ref, d_ref, up_ref, down_ref):
    del eb_ref
    sort_sides("gy", even_ref, odd_ref, low_ref, high_ref)
    lower, upper = has_lower("gy"), has_upper("gy")
    for i in range(TILES):
        edge_ref[i, 0:4, :] = low_ref[i * 4 : i * 4 + 4, :]
        edge_ref[i, 4:8, :] = high_ref[i * 4 : i * 4 + 4, :]
        if i < 3 * XN:
            c, p = i // XN, i % XN
            mine = x_plane(own_ref, xl_ref, xh_ref, c, p)
            edge_ref[i, 3:4, :] = average(lower, low_ref[i * 4 + 3 : i * 4 + 4, :], mine[0:1], mine[0:1])
            edge_ref[i, 4:5, :] = average(upper, mine[EY:NY], high_ref[i * 4 : i * 4 + 1, :], mine[EY:NY])

    z_ref[...] = jnp.zeros(z_ref.shape, F32)
    d_ref[...] = jnp.zeros(d_ref.shape, F32)
    lane = iota((8, EZ), 1)
    for first in range(0, TILES, 16):
        count = min(16, TILES - first)
        block = edge_ref[first : first + count].reshape(count * 8, EZ)
        if count < 16:
            block = jnp.concatenate([block, jnp.zeros(((16 - count) * 8, EZ), F32)], axis=0)
        turned = end_planes(block.T)
        for t in range(count):
            i = first + t
            low = pltpu.roll(turned, (5 - 8 * t) % EZ, 1)
            high = pltpu.roll(turned, (52 - 8 * t - 4) % EZ, 1)
            width = 4 if i < 3 * XN else 3
            value = jnp.where((lane >= 5) & (lane < 5 + width), low, zo_ref[i])
            value = jnp.where((lane >= 52) & (lane < 52 + width), high, value)
            if i < 3 * XN:
                at = (i // XN) * XR + i % XN
                z_ref[at * 8 : at * 8 + 8, :] = value
            else:
                at = i - 3 * XN
                d_ref[at * 8 : at * 8 + 8, :] = value

    lane = iota((XR, EZ), 1)
    tops = []
    for c in range(3):
        mine = tx_ref[c]
        low = pltpu.roll(low_ref[TOP_AT:Y_MESSAGE, :], (5 - 4 * c) % EZ, 1)
        high = pltpu.roll(high_ref[TOP_AT:Y_MESSAGE, :], (52 - 4 * c) % EZ, 1)
        value = jnp.where((lane >= 5) & (lane < 8), low, mine)
        value = jnp.where(lane == 8, average(lower, low, mine, mine), value)
        value = jnp.where(lane == 52, average(upper, mine, high, mine), value)
        tops.append(jnp.where((lane > 52) & (lane < 56), high, value))
    top = jnp.concatenate(tops, axis=0)

    def nodes(k):
        return z_ref[pl.ds(k, 3 * XR, stride=8), :]

    def dens(k):
        return d_ref[pl.ds(k, XR, stride=8), :]

    def pack(low, high):
        return low + pltpu.roll(high, 64, 1)

    oa_ref[...] = pack(nodes(0), top)
    ob_ref[...] = pack(nodes(1), nodes(7))
    od_ref[...] = pack(dens(0), dens(7))
    up_ref[0:72, :] = pack(nodes(5), nodes(6))
    up_ref[72:144, :] = pack(nodes(7), top)
    up_ref[144:168, :] = pack(dens(5), dens(6))
    up_ref[168:192, :] = dens(7)
    down_ref[0:72, :] = pack(nodes(0), nodes(1))
    down_ref[72:144, :] = pack(nodes(2), nodes(3))
    down_ref[144:168, :] = pack(dens(0), dens(1))
    down_ref[168:192, :] = dens(2)
    sort_sides("gz", up_ref, down_ref, zodd_ref, zeven_ref)


def edge_kernel(own_ref, xl_ref, xh_ref, edge_ref, lhs_ref, el_ref, eh_ref, w_ref, b_ref, s_ref):
    s_ref[...] = jnp.zeros(s_ref.shape, F32)
    lhs = lhs_ref[0]
    pad = jnp.zeros((3, EZ), F32)

    def low(c, p):
        mine = x_plane(own_ref, xl_ref, xh_ref, c, p)
        return jnp.concatenate([edge_ref[c * XN + p, 0:4, :], mine[1:2], pad], axis=0)

    def high(c, p):
        mine = x_plane(own_ref, xl_ref, xh_ref, c, p)
        return jnp.concatenate([mine[EY - 1 : EY], edge_ref[c * XN + p, 4:8, :], pad], axis=0)

    for side, e_ref in ((low, el_ref), (high, eh_ref)):
        build_nodes(side, range(XN), 8, w_ref, b_ref)
        energy_planes(lhs, w_ref, b_ref, s_ref, e_ref, 0, XE, 8, (0, 2), 0, XE)


def triangle(value, axis):
    size = value.shape[axis]
    value = value + pltpu.roll(value, size - 1, axis)
    value = value + pltpu.roll(value, size - 2, axis)
    value = value + pltpu.roll(value, 1, axis)
    return value + pltpu.roll(value, 2, axis)


def weights(distance):
    return jnp.maximum(4 - jnp.abs(distance), 0).astype(F32)


def three_parts(value):
    high = value.astype(BF16)
    rest = value - high.astype(F32)
    middle = rest.astype(BF16)
    return high, middle, (rest - middle.astype(F32)).astype(BF16)


def exact_dot(value, right):
    parts = [jnp.dot(part, right, preferred_element_type=F32) for part in three_parts(value)]
    return parts[0] + parts[1] + parts[2]


def edge_total(count, position, parts):
    total = None
    for offset in range(-RADIUS, RADIUS + 1):
        place = position + offset
        term = float(RADIUS + 1 - abs(offset)) * one_hot((place >= 0) & (place < count * parts))
        total = term if total is None else total + term
    return total


def field_kernel(ea_ref, eb_ref, el_ref, eh_ref, dens_ref, lowx_ref, highx_ref, lowy_ref, highy_ref, g_ref, f_ref):
    rows = iota((QROWS, EZ), 0)
    lanes = iota((QROWS, EZ), 1)
    ok = (rows >= 5) & (rows < 55) & (lanes > 0) & (lanes < EZ - 1)
    row = iota((8, EZ), 0)
    for x in range(XE):
        if x < 4:
            middle = eb_ref[x]
        elif x < 18:
            middle = ea_ref[x - 4]
        else:
            middle = eb_ref[x - 14]
        low = pltpu.roll(el_ref[x], 5, 0)
        high = pltpu.roll(eh_ref[x], 3, 0)
        start = jnp.where(row < 1, low, middle[0:8])
        end = jnp.where(row < 3, middle[40:48], high)
        energy = jnp.concatenate([low, start, middle[8:40], end], axis=0)
        at = 3 * XN * 4 + x * 4
        pad = jnp.zeros((5, EZ), F32)
        d = jnp.concatenate(
            [pad, lowy_ref[at : at + 3, :], x_density(dens_ref, lowx_ref, highx_ref, x), highy_ref[at : at + 3, :], pad[0:1]], axis=0)
        f_ref[0, x] = jnp.where(ok, (SCALE * d) * d * d * energy, 0.0)
        f_ref[1, x] = jnp.where(ok, d, 0.0)

    for f in range(2):
        for t in range(QROWS // 8):
            at = slice(t * 8, t * 8 + 8)
            line = [f_ref[f, x, at, :] for x in range(XE)]
            for step in (1, 2, 1, 2):
                line = [line[i] + line[i + step] for i in range(len(line) - step)]
            for x in range(EX):
                f_ref[f, x, at, :] = line[x]
    for f in range(2):
        for x in range(EX):
            g_ref[f, x] = triangle(f_ref[f, x], 0)[8:QROWS]


def last_kernel(g_ref, dens_ref, oa_ref, ob_ref, od_ref, even_ref, odd_ref, lhs_ref,
                sens_ref, smooth_ref, w_ref, b_ref, s_ref, ez_ref, c_ref, zl_ref, zh_ref):
    sort_sides("gz", even_ref, odd_ref, zl_ref, zh_ref)
    lower, upper = has_lower("gz"), has_upper("gz")

    def swap(value):
        return pltpu.roll(value, 64, 1)

    is_low = iota((3 * XR, EZ), 1) < 64
    oa, ob = oa_ref[...], ob_ref[...]
    zl0, zl1 = zl_ref[0:72, :], zl_ref[72:144, :]
    zh0, zh1 = zh_ref[0:72, :], zh_ref[72:144, :]
    nodes = (
        jnp.where(is_low, zl0, ob),
        jnp.where(is_low, swap(zl0), average(upper, oa, swap(zh0), oa)),
        jnp.where(is_low, zl1, zh0),
        jnp.where(is_low, average(lower, swap(zl1), oa, oa), swap(zh1)),
        jnp.where(is_low, ob, zh1),
    )
    build_nodes(lambda c, k: nodes[k][c * XR : (c + 1) * XR], range(5), XR, w_ref, b_ref)
    s_ref[...] = jnp.zeros(s_ref.shape, F32)
    energy_planes(lhs_ref[1], w_ref, b_ref, s_ref, ez_ref, 0, 4, XR, range(0, XE, 2), 0, 4)

    lane = iota((XR, EZ), 1)
    low_side = lane < 64
    od = od_ref[...]
    dl0, dl1 = zl_ref[144:168, :], zl_ref[168:192, :]
    dh0, dh1 = zh_ref[144:168, :], zh_ref[168:192, :]
    dens = (
        jnp.where(low_side, dl0, od),
        jnp.where(low_side, swap(dl0), swap(dh0)),
        jnp.where(low_side, dl1, dh0),
        jnp.where(low_side, od, swap(dh1)),
    )
    inside = (lane % 64 >= 5) & (lane % 64 < 55) & (iota((XR, EZ), 0) < XE)
    for j in range(4):
        d = dens[j]
        for f, value in ((0, (SCALE * d) * d * d * ez_ref[j]), (1, d)):
            value = triangle_forward(jnp.where(inside, value, 0.0))
            c_ref[f, j * EX : (j + 1) * EX, :] = value[0:EX]
    row, col = iota((EZ, EZ), 0), iota((EZ, EZ), 1)
    along_y = jnp.where(row // 64 == col // 64, weights(row - col), 0.0).astype(BF16)

    k = iota((EZ, EZ), 0)
    j = (k % 64) // EX
    place = jnp.where(k < 64, j - 3, EZ - 1 + j)
    z = iota((EZ, EZ), 1)
    right = jnp.concatenate([weights(k - z), weights(place - z)], axis=0).astype(BF16)

    ends = []
    for f in range(2):
        turned = exact_dot(c_ref[f], along_y)
        turned = jnp.concatenate([turned, jnp.zeros((EZ - 4 * EX, EZ), F32)], axis=0).T
        ends.append(turned[8:56] + pltpu.roll(turned[72:120], 64, 1))

    base_x, base_y, base_z = lax.axis_index("gx") * EX, lax.axis_index("gy") * EY, lax.axis_index("gz") * EZ
    norm_y = edge_total(EY, base_y + iota((ROWS, EZ), 0), lax.axis_size("gy"))
    norm_z = edge_total(EZ, base_z + iota((ROWS, EZ), 1), lax.axis_size("gz"))
    norm_yz = norm_y * norm_z
    lanes = iota((ROWS, EZ), 1)
    for x in range(EX):
        sums = []
        for f in range(2):
            tail = jnp.where(lanes % EX == x, ends[f], 0.0)
            sums.append(exact_dot(jnp.concatenate([g_ref[f, x], tail], axis=1), right)[0:EY])
        norm = (norm_yz * edge_total(EX, base_x + x, lax.axis_size("gx")))[0:EY]
        d = dens_ref[pl.ds(x, EY, stride=EX), :]
        sens_ref[pl.ds(x, EY, stride=EX), :] = sums[0] / (d * norm)
        smooth_ref[pl.ds(x, EY, stride=EX), :] = sums[1] / norm


def triangle_forward(value):
    size = value.shape[0]
    for step in (1, 2, 1, 2):
        value = value + pltpu.roll(value, size - step, 0)
    return value


def call(kernel, outs, ins, scratch=(), limit=16, micros=1.0):
    return pl.pallas_call(
        kernel,
        out_shape=[jax.ShapeDtypeStruct(shape, dtype) for shape, dtype in outs],
        in_specs=[pl.BlockSpec(memory_space=space) for space in ins],
        out_specs=[pl.BlockSpec(memory_space=VM)] * len(outs),
        scratch_shapes=[pltpu.VMEM(item[0], item[1]) if isinstance(item, tuple) else item for item in scratch],
        compiler_params=pltpu.CompilerParams(vmem_limit_bytes=limit * 2**20),
        cost_estimate=pl.CostEstimate(flops=0, bytes_accessed=int(micros * 3.6e6), transcendentals=0),
    )


def exchange(even, odd, axis):
    count = lax.axis_size(axis)
    results = []
    for value, first in ((even, 0), (odd, 1)):
        pairs = [(i, i + 1) for i in range(first, count - 1, 2)]
        if pairs:
            results.append(lax.ppermute(value, axis, pairs + [(j, i) for i, j in pairs]))
        else:
            results.append(jnp.zeros_like(value))
    return results


def local(local_solution, top_nodes, coarse_solution, corner_dofs, density, element_stiffness):
    dens = jnp.transpose(density, (1, 0, 2)).reshape(EY * EX, EZ)
    dofs = corner_dofs.reshape(8)
    shared = lax.axis_size("gz") == 2
    if shared:
        other = lax.ppermute(coarse_solution, "gz", [(0, 1), (1, 0)])
        coarse = jnp.stack([coarse_solution, other])
    else:
        coarse = lax.all_gather(coarse_solution, "gz")

    message = ((15, ROWS, EZ), F32)
    even, odd, tops = call(
        pack_kernel,
        [message, message, ((3, XR, EZ), F32)],
        [pltpu.HBM] * 4,
        [((2, 3, 4, NY, EZ), F32), ((3, NX, 1, NY), F32), ((EY * EX, EZ), F32), ((1, 8), jnp.int32), pltpu.SemaphoreType.DMA((9,))],
    )(*[
        pltpu.with_memory_space_constraint(value, pltpu.HBM)
        for value in (local_solution, jnp.transpose(top_nodes, (0, 1, 3, 2)), dens, dofs.reshape(1, 8))
    ])
    even_x, odd_x = exchange(even, odd, "gx")

    def nodes(count):
        return [((count * 8, EZ), F32), ((count * 16, EZ), BF16)]

    own, ea, lhs = call(
        functools.partial(own_kernel, shared),
        [((3 * NX, ROWS, EZ), F32), ((EX - 2, ROWS, EZ), F32), ((2, 64, 64), BF16)],
        [VM, VM, SM, SM],
        nodes((EX - 1) * ROWS) + [(((EX - 2) * ROWS * 8, EZ), F32)],
        micros=6.0,
    )(local_solution, element_stiffness, coarse, dofs)

    face = ((12, ROWS, EZ), F32)
    y_message = ((Y_MESSAGE, EZ), F32)
    xl, xh, tx, even, odd, low_x, high_x = call(
        functools.partial(x_kernel, shared),
        [face, face, ((3, XR, EZ), F32), y_message, y_message, message, message],
        [VM, VM, VM, VM, VM, SM, SM],
        [y_message, y_message, ((4, XR, EZ), F32)],
        micros=2.0,
    )(own, tops, dens, even_x, odd_x, coarse, dofs)
    even_y, odd_y = exchange(even, odd, "gy")

    (eb,) = call(
        side_kernel, [((8, ROWS, EZ), F32)], [VM] * 4, nodes(10 * ROWS) + [((4 * ROWS * 8, EZ), F32)], micros=2.6
    )(own, xl, xh, lhs)

    (zo,) = call(turn_kernel, [((TILES, 8, EZ), F32)], [VM] * 6, micros=1.5)(own, xl, xh, dens, low_x, high_x)

    z_message = ((Z_MESSAGE, EZ), F32)
    edge, low_y, high_y, oa, ob, od, even, odd = call(
        y_kernel,
        [((TILES, 8, EZ), F32), y_message, y_message, ((72, EZ), F32), ((72, EZ), F32), ((XR, EZ), F32), z_message, z_message],
        [VM] * 8,
        [((8 * 3 * XR, EZ), F32), ((8 * XR, EZ), F32), z_message, z_message],
        micros=1.0,
    )(own, xl, xh, tx, zo, eb, even_y, odd_y)
    even_z, odd_z = exchange(even, odd, "gz")

    el, eh = call(
        edge_kernel,
        [((XE, 8, EZ), F32)] * 2,
        [VM] * 5,
        nodes(XN * 8) + [((XE * 8 * 8, EZ), F32)],
        micros=2.3,
    )(own, xl, xh, edge, lhs)

    (filtered,) = call(
        field_kernel, [((2, EX, ROWS, EZ), F32)], [VM] * 9, [((2, XE, QROWS, EZ), F32)], micros=1.5
    )(ea, eb, el, eh, dens, low_x, high_x, low_y, high_y)

    sens, smooth = call(
        last_kernel,
        [((EY * EX, EZ), F32)] * 2,
        [VM] * 8,
        nodes(5 * XR) + [((4 * XR * 8, EZ), F32), ((4, XR, EZ), F32), ((2, 4 * EX, EZ), F32), z_message, z_message],
        micros=2.5,
    )(filtered, dens, oa, ob, od, even_z, odd_z, lhs)

    def grid(value):
        return jnp.transpose(value.reshape(EY, EX, EZ), (1, 0, 2))

    return grid(sens), grid(smooth)


def solution(mesh):
    in_specs = (
        P(None, "gx", "gy", "gz"),
        P(None, "gx", "gy", "gz"),
        P(None, "gz"),
        P("gx", "gy", "gz", None),
        P("gx", "gy", "gz"),
        P(),
    )
    out_specs = (P("gx", "gy", "gz"), P("gx", "gy", "gz"))
    return jax.shard_map(local, mesh=mesh, in_specs=in_specs, out_specs=out_specs, check_vma=False)
```

```python
import functools

import jax
import jax.numpy as jnp
from jax import lax
from jax.experimental import pallas as pl
from jax.experimental.pallas import tpu as pltpu
from jax.sharding import PartitionSpec as P

RADIUS = 3
F32 = jnp.float32
BF16 = jnp.bfloat16
SCALE = -3.0 / 96.0
HIGHEST = lax.Precision.HIGHEST
VM = pltpu.VMEM
SM = pltpu.SMEM

EX, EY, EZ = 16, 44, 128
NX, NY = EX + 1, EY + 1
XN, XE = NX + 2 * RADIUS, EX + 2 * RADIUS
ROWS = 48
QROWS = 56
XR = 24


def iota(shape, dim):
    return lax.broadcasted_iota(jnp.int32, shape, dim)


def one_hot(mask):
    return jnp.where(mask, 1.0, 0.0).astype(F32)


def halves(value):
    high = value.astype(BF16)
    return high, (value - high.astype(F32)).astype(BF16)


def corner_scalars(coarse_ref, dof_of, shared):
    width = coarse_ref.shape[2]
    own = lax.axis_index("gz")
    out = [[None] * 8 for _ in range(3)]
    for k in range(8):
        dof = dof_of(k)
        part = dof // width
        place = dof - part * width
        if shared:
            part = jnp.where(part == own, 0, 1)
        for c in range(3):
            out[c][k] = coarse_ref[part, c, place]
    return out


def corner_rows(corners, c):
    rz = iota((8, EZ), 1).astype(F32) * (1.0 / EZ)
    other = 1.0 - rz
    return [[corners[c][4 * kx + 2 * ky] * other + corners[c][4 * kx + 2 * ky + 1] * rz for ky in (0, 1)] for kx in (0, 1)]


def plane_interp(edges, i, rows):
    wx = i / EX
    first, second = [((1.0 - wx) * edges[0][ky] + wx * edges[1][ky])[0:1] for ky in (0, 1)]
    ry = iota((rows, EZ), 0).astype(F32) * (1.0 / EY)
    return (1.0 - ry) * first + ry * second


def block_rows(block):
    nodes = block + 1
    return 2 * (16 * nodes + 16 * ((nodes + 1) // 2))


def stiffness_rows(stiff, block, in_lanes):
    def target(h, t, r):
        s, c = r // 4, r % 4
        place = 4 * t + 2 * s + h if in_lanes else 4 * h + 2 * t + s
        return jnp.where(c < 3, 8 * c + place, -1)

    row = iota((32, 24), 0)
    left = one_hot(iota((32, 24), 1) == target(row // 16, row // 8 % 2, row % 8))
    full = jnp.dot(left, stiff, precision=HIGHEST, preferred_element_type=F32)
    nodes, width = block + 1, block_rows(block)
    split = 32 * nodes
    half = (width - split) // 2
    col = iota((24, width), 1)
    again = col >= split
    h = jnp.where(again, (col - split) // half, col // (16 * nodes))
    node = jnp.where(again, (col - split) % half // 8, col % (16 * nodes) // 16)
    wide = iota((32, width), 1) >= split
    rows = []
    for e in range(block):
        t = node - e
        right = one_hot((iota((24, width), 0) == target(h, t, col % 8)) & (t >= 0) & (t < 2))
        part = jnp.dot(full, right, precision=HIGHEST, preferred_element_type=F32)
        high = part.astype(BF16).astype(F32)
        rows.append(jnp.where(wide, part - high, high))
    return jnp.concatenate(rows, axis=0).astype(BF16)


def build_nodes(plane_of, planes, rows, refs, first=0):
    w_ref, b_ref, h_ref, _ = refs
    for p in planes:
        base = (first + p) * rows * 8
        zero = jnp.zeros((rows, EZ), F32)
        for c in range(3):
            value = plane_of(c, p)
            w_ref[pl.ds(base + c, rows, stride=8), :] = value
            w_ref[pl.ds(base + 4 + c, rows, stride=8), :] = pltpu.roll(value, EZ - 1, 1)
        w_ref[pl.ds(base + 3, rows, stride=8), :] = zero
        w_ref[pl.ds(base + 7, rows, stride=8), :] = zero

    def split(p, _):
        base = (first + p) * rows
        last = None
        for r in range(rows):
            value = w_ref[pl.ds(pl.multiple_of((base + r) * 8, 8), 8), :]
            high = value.astype(BF16).astype(F32)
            at = pl.ds(pl.multiple_of((base + r) * 16, 16), 16)
            b_ref[at, :] = jnp.concatenate([high, value - high], axis=0).astype(BF16)
            if last is not None:
                h_ref[pl.ds(pl.multiple_of((base + r - 1) * 16, 16), 16), :] = jnp.concatenate([last, high], axis=0).astype(BF16)
            last = high
        h_ref[at, :] = jnp.concatenate([last, last], axis=0).astype(BF16)
        return 0

    lax.fori_loop(0, len(planes), split, 0)


def energy_planes(lhs, block, refs, e_ref, first, count, rows, blocks, out_first):
    w_ref, b_ref, h_ref, s_ref = refs
    nodes = block + 1
    for i in range(0, len(blocks), 2):
        pair = [((first + p) * rows + r, p * rows + r) for p, r in blocks[i : i + 2]]
        right = []
        for at, _ in pair:
            parts = [b_ref[(at + far) * 16 : (at + far + nodes) * 16, :] for far in (0, rows)]
            for far in (0, rows):
                parts += [h_ref[(at + far + t) * 16 : (at + far + t + 1) * 16, :] for t in range(0, nodes, 2)]
            right.append(jnp.concatenate(parts, axis=0))
        product = jnp.dot(lhs, jnp.concatenate(right, axis=1), preferred_element_type=F32)
        for u, (at, out) in enumerate(pair):
            for e in range(block):
                part = product[32 * e : 32 * e + 32, u * EZ : (u + 1) * EZ]
                low = w_ref[(at + e) * 8 : (at + e + 2) * 8, :] * part[0:16]
                high = w_ref[(at + rows + e) * 8 : (at + rows + e + 2) * 8, :] * part[16:32]
                both = low + high
                s_ref[(out + e) * 8 : (out + e + 1) * 8, :] = both[0:8] + both[8:16]
    for p in range(count):
        total = None
        for s in (0, 1, 2, 4, 5, 6):
            term = s_ref[pl.ds(p * rows * 8 + s, rows, stride=8), :]
            total = term if total is None else total + term
        e_ref[out_first + p] = total


def node_buffers(count, energies):
    return [((count * 8, EZ), F32), ((count * 16, EZ), BF16), ((count * 16, EZ), BF16), ((energies * 8, EZ), F32)]


def odd_place(axis):
    return lax.axis_index(axis) % 2 == 1


def pack_kernel(local_ref, top_ref, dens_ref, dofs_ref, even_ref, odd_ref, tops_ref, l_ref, t_ref, d_ref, c_ref, sem):
    copies = [pltpu.make_async_copy(top_ref, t_ref, sem.at[0]), pltpu.make_async_copy(dens_ref, d_ref, sem.at[1]),
              pltpu.make_async_copy(dofs_ref, c_ref, sem.at[2])]
    for side, node in ((0, EX - RADIUS), (1, 0)):
        for c in range(3):
            copies.append(pltpu.make_async_copy(local_ref.at[c, node : node + 4], l_ref.at[side, c], sem.at[len(copies)]))
    for copy in copies:
        copy.start()
    even_ref[...] = jnp.zeros(even_ref.shape, F32)
    odd_ref[...] = jnp.zeros(odd_ref.shape, F32)
    tops_ref[...] = jnp.zeros(tops_ref.shape, F32)
    for copy in copies:
        copy.wait()
    for c in range(3):
        for i in range(NX):
            tops_ref[c, i : i + 1, 0:NY] = t_ref[c, i]
    odd = odd_place("gx")
    for out_ref, flip in ((even_ref, odd), (odd_ref, jnp.logical_not(odd))):
        side = flip.astype(jnp.int32)
        for c in range(3):
            for j in range(4):
                out_ref[c * 4 + j, 0:NY, :] = l_ref[side, c, j]
                out_ref[c * 4 + j, NY : NY + 1, :] = jnp.where(
                    flip, tops_ref[c, j : j + 1, :], tops_ref[c, EX - RADIUS + j : EX - RADIUS + j + 1, :])
        for j in range(3):
            out_ref[12 + j, 0:EY, :] = jnp.where(
                flip, d_ref[pl.ds(j, EY, stride=EX), :], d_ref[pl.ds(EX - RADIUS + j, EY, stride=EX), :])
        out_ref[12, EY : EY + 1, 0:8] = c_ref[...].astype(F32)


def sort_sides(axis, even_ref, odd_ref, low_ref, high_ref):
    odd = odd_place(axis)
    even, other = even_ref[...], odd_ref[...]
    low_ref[...] = jnp.where(odd, even, other)
    high_ref[...] = jnp.where(odd, other, even)


def prepare_kernel(stiff_ref, dens_ref, lhs_ref, lhs_edge_ref, lhs_z_ref, od_ref, rs_ref, rd_ref):
    stiff = stiff_ref[...]
    lhs_ref[...] = stiffness_rows(stiff, 3, False)
    lhs_edge_ref[...] = stiffness_rows(stiff, 4, False)
    lhs_z_ref[...] = stiffness_rows(stiff, 4, True)
    base_x, base_y, base_z = lax.axis_index("gx") * EX, lax.axis_index("gy") * EY, lax.axis_index("gz") * EZ
    inside = iota((ROWS, EZ), 0) < EY
    norm_y = edge_total(EY, base_y + iota((ROWS, EZ), 0), lax.axis_size("gy"))
    norm_z = edge_total(EZ, base_z + iota((ROWS, EZ), 1), lax.axis_size("gz"))
    inverse = 1.0 / jnp.where(inside, norm_y * norm_z, 1.0)
    place = base_x + iota((8, EZ), 0)
    inverse_x = [1.0 / edge_total(EX, place + t, lax.axis_size("gx")) for t in (0, 8)]
    for x in range(EX):
        d = dens_ref[pl.ds(x, EY, stride=EX), :]
        od_ref[x, 0:EY, :] = d
        od_ref[x, EY:ROWS, :] = jnp.ones((ROWS - EY, EZ), F32)
        both = inverse * inverse_x[x // 8][x % 8 : x % 8 + 1, :]
        rd_ref[x] = both
        rs_ref[x] = both / od_ref[x]


def own_kernel(shared, local_ref, lhs_ref, coarse_ref, dofs_ref, own_ref, e_ref, *refs):
    corners = corner_scalars(coarse_ref, lambda k: dofs_ref[k], shared)
    for c in range(3):
        edges = corner_rows(corners, c)
        for i in range(NX):
            own_ref[c * NX + i, 0:NY, :] = local_ref[c, i] + plane_interp(edges, i, NY)
            own_ref[c * NX + i, NY:ROWS, :] = jnp.zeros((ROWS - NY, EZ), F32)
    clear(refs[3])
    build_nodes(lambda c, p: own_ref[c * NX + p + 1], range(EX - 1), ROWS, refs)
    blocks = [(p, r) for p in range(EX - 2) for r in range(1, EY - 1, 3)]
    energy_planes(lhs_ref[...], 3, refs, e_ref, 0, EX - 2, ROWS, blocks, 0)


def clear(ref):
    ref[...] = jnp.zeros(ref.shape, ref.dtype)


def average(flag, low, high, own):
    return jnp.where(flag, 0.5 * low + 0.5 * high, own)


def has_lower(axis):
    return lax.axis_index(axis) > 0


def has_upper(axis):
    return lax.axis_index(axis) < lax.axis_size(axis) - 1


def message_dofs(message_ref):
    row = message_ref[12, EY : EY + 1, :]
    lane = iota((1, EZ), 1)
    return lambda k: jnp.sum(jnp.where(lane == k, row, 0.0)).astype(jnp.int32)


def top_interp(corners, c, rows):
    rx = iota((rows, EZ), 0).astype(F32) * (1.0 / EX)
    ry = iota((rows, EZ), 1).astype(F32) * (1.0 / EY)
    low = (1.0 - ry) * corners[c][1] + ry * corners[c][3]
    high = (1.0 - ry) * corners[c][5] + ry * corners[c][7]
    return (1.0 - rx) * low + rx * high


TOP_AT = 368
Y_MESSAGE = 392


def x_kernel(shared, own_ref, top_ref, dens_ref, even_ref, odd_ref, coarse_ref, dofs_ref,
             xl_ref, xh_ref, tx_ref, yeven_ref, yodd_ref, low_ref, high_ref, up_ref, down_ref, t_ref):
    sort_sides("gx", even_ref, odd_ref, low_ref, high_ref)
    corners = corner_scalars(coarse_ref, lambda k: dofs_ref[k], shared)
    corners_low = corner_scalars(coarse_ref, message_dofs(low_ref), shared)
    corners_high = corner_scalars(coarse_ref, message_dofs(high_ref), shared)
    lower, upper = has_lower("gx"), has_upper("gx")
    for c in range(3):
        edges_low, edges_high = corner_rows(corners_low, c), corner_rows(corners_high, c)
        for j in range(4):
            value = low_ref[c * 4 + j] + plane_interp(edges_low, EX - RADIUS + j, ROWS)
            if j == 3:
                mine = own_ref[c * NX]
                value = average(lower, value, mine, mine)
            xl_ref[c * 4 + j] = value
            value = high_ref[c * 4 + j] + plane_interp(edges_high, j, ROWS)
            if j == 0:
                mine = own_ref[c * NX + EX]
                value = average(upper, mine, value, mine)
            xh_ref[c * 4 + j] = value

    t_ref[...] = jnp.zeros(t_ref.shape, F32)
    for c in range(3):
        t_ref[0] = top_ref[c] + top_interp(corners, c, XR)
        for j in range(4):
            t_ref[1, j : j + 1, 0:NY] = low_ref[c * 4 + j, NY : NY + 1, 0:NY]
            t_ref[2, j : j + 1, 0:NY] = high_ref[c * 4 + j, NY : NY + 1, 0:NY]
        t_low = t_ref[1, 0:8, :] + pltpu.roll(top_interp(corners_low, c, 24), 24 - (EX - RADIUS), 0)[0:8]
        t_high = t_ref[2, 0:8, :] + top_interp(corners_high, c, 8)
        first = average(lower, t_low[3:4], t_ref[0, 0:1, :], t_ref[0, 0:1, :])
        last = average(upper, t_ref[0, EX : EX + 1, :], t_high[0:1], t_ref[0, EX : EX + 1, :])
        t_ref[3, 0:3, :] = t_low[0:3]
        t_ref[3, 3:4, :] = first
        t_ref[3, 4:19, :] = t_ref[0, 1:EX, :]
        t_ref[3, 19:20, :] = last
        t_ref[3, 20:23, :] = t_high[1:4]
        lane = iota((XR, EZ), 1)
        tx_ref[c] = jnp.where(lane < NY + 8, pltpu.roll(t_ref[3], 8, 1), 0.0)

    for out_ref, node, elem, lane_at in ((up_ref, EY - RADIUS, EY - RADIUS, EY - RADIUS + 8), (down_ref, 0, 0, 8)):
        for c in range(3):
            for p in range(XN):
                at = (c * XN + p) * 4
                out_ref[at : at + 4, :] = x_plane(own_ref, xl_ref, xh_ref, c, p)[node : node + 4]
        for x in range(XE):
            at = 3 * XN * 4 + x * 4
            out_ref[at : at + 3, :] = x_density(dens_ref, low_ref, high_ref, x)[elem : elem + 3]
            out_ref[at + 3 : at + 4, :] = jnp.zeros((1, EZ), F32)
        out_ref[364:TOP_AT, :] = jnp.zeros((TOP_AT - 364, EZ), F32)
        lane = iota((XR, EZ), 1)
        total = jnp.zeros((XR, EZ), F32)
        for c in range(3):
            moved = pltpu.roll(tx_ref[c], (4 * c - lane_at) % EZ, 1)
            total = jnp.where((lane >= 4 * c) & (lane < 4 * c + 4), moved, total)
        out_ref[TOP_AT:Y_MESSAGE, :] = total
    sort_sides("gy", up_ref, down_ref, yodd_ref, yeven_ref)


def side_kernel(own_ref, xl_ref, xh_ref, lhs_ref, e_ref, *refs):
    clear(refs[3])

    def plane(c, p):
        if p < 4:
            return xl_ref[c * 4 + p]
        if p == 4:
            return own_ref[c * NX + 1]
        if p == 5:
            return own_ref[c * NX + EX - 1]
        return xh_ref[c * 4 + p - 6]

    build_nodes(plane, range(10), ROWS, refs)
    blocks = [(p, r) for p in range(4) for r in range(1, EY - 1, 3)]
    for first, out_first in ((0, 0), (5, 4)):
        energy_planes(lhs_ref[...], 3, refs, e_ref, first, 4, ROWS, blocks, out_first)


Z_MESSAGE = 192
TILES = 3 * XN + XE


def x_plane(own_ref, xl_ref, xh_ref, c, p):
    if p < 4:
        return xl_ref[c * 4 + p]
    if p < 19:
        return own_ref[c * NX + p - 3]
    return xh_ref[c * 4 + p - 19]


def x_density(dens_ref, low_ref, high_ref, x, rows=EY):
    if x < 3:
        return low_ref[12 + x, 0:rows, :]
    if x < 19:
        return dens_ref[x - 3, 0:rows, :]
    return high_ref[12 + x - 19, 0:rows, :]


def end_planes(turned):
    return jnp.concatenate([turned[0:4], turned[EZ - 4 : EZ]], axis=0)


def turn_kernel(own_ref, xl_ref, xh_ref, dens_ref, lowx_ref, highx_ref, z_ref):
    head = jnp.zeros((8, EZ), F32)

    def padded(i):
        if i < 3 * XN:
            return [head, x_plane(own_ref, xl_ref, xh_ref, i // XN, i % XN), head]
        return [head, x_density(dens_ref, lowx_ref, highx_ref, i - 3 * XN, ROWS), head]

    lane = iota((8, EZ), 1)
    for i in range(0, TILES, 2):
        both = end_planes(jnp.concatenate(padded(i) + padded(min(i + 1, TILES - 1)), axis=0).T)
        z_ref[i] = jnp.where(lane < 64, both, 0.0)
        if i + 1 < TILES:
            z_ref[i + 1] = jnp.where(lane < 64, pltpu.roll(both, 64, 1), 0.0)


def y_kernel(tx_ref, zo_ref, eb_ref, even_ref, odd_ref,
             low_ref, high_ref, oa_ref, ob_ref, od_ref, *refs):
    del eb_ref
    z_ref, d_ref, up_ref, down_ref = refs[-4:]
    sort_sides("gy", even_ref, odd_ref, low_ref, high_ref)
    lower, upper = has_lower("gy"), has_upper("gy")
    clear(z_ref)
    clear(d_ref)
    lane = iota((8, EZ), 1)
    for first in range(0, TILES, 32):
        count = min(32, TILES - first)
        turned = []
        for ref in (low_ref, high_ref):
            block = ref[first * 4 : (first + count) * 4, :]
            if count < 32:
                block = jnp.concatenate([block, jnp.zeros(((32 - count) * 4, EZ), F32)], axis=0)
            turned.append(end_planes(block.T))
        for t in range(count):
            i = first + t
            low = pltpu.roll(turned[0], (5 - 4 * t) % EZ, 1)
            high = pltpu.roll(turned[1], (52 - 4 * t) % EZ, 1)
            mine = zo_ref[i]
            if i < 3 * XN:
                at = (i // XN) * XR + i % XN
                value = jnp.where((lane >= 5) & (lane < 8), low, mine)
                value = jnp.where((lane == 8) & lower, 0.5 * low + 0.5 * mine, value)
                value = jnp.where((lane == 52) & upper, 0.5 * mine + 0.5 * high, value)
                z_ref[at * 8 : at * 8 + 8, :] = jnp.where((lane > 52) & (lane < 56), high, value)
            else:
                at = i - 3 * XN
                value = jnp.where((lane >= 5) & (lane < 8), low, mine)
                d_ref[at * 8 : at * 8 + 8, :] = jnp.where((lane >= 52) & (lane < 55), high, value)

    lane = iota((XR, EZ), 1)
    tops = []
    for c in range(3):
        mine = tx_ref[c]
        low = pltpu.roll(low_ref[TOP_AT:Y_MESSAGE, :], (5 - 4 * c) % EZ, 1)
        high = pltpu.roll(high_ref[TOP_AT:Y_MESSAGE, :], (52 - 4 * c) % EZ, 1)
        value = jnp.where((lane >= 5) & (lane < 8), low, mine)
        value = jnp.where(lane == 8, average(lower, low, mine, mine), value)
        value = jnp.where(lane == 52, average(upper, mine, high, mine), value)
        tops.append(jnp.where((lane > 52) & (lane < 56), high, value))
    top = jnp.concatenate(tops, axis=0)

    def nodes(k):
        return z_ref[pl.ds(k, 3 * XR, stride=8), :]

    def dens(k):
        return d_ref[pl.ds(k, XR, stride=8), :]

    def pack(low, high):
        return low + pltpu.roll(high, 64, 1)

    oa_ref[...] = pack(nodes(0), top)
    ob_ref[...] = pack(nodes(1), nodes(7))
    od_ref[...] = pack(dens(0), dens(7))
    up_ref[0:72, :] = pack(nodes(5), nodes(6))
    up_ref[72:144, :] = pack(nodes(7), top)
    up_ref[144:168, :] = pack(dens(5), dens(6))
    up_ref[168:192, :] = dens(7)
    down_ref[0:72, :] = pack(nodes(0), nodes(1))
    down_ref[72:144, :] = pack(nodes(2), nodes(3))
    down_ref[144:168, :] = pack(dens(0), dens(1))
    down_ref[168:192, :] = dens(2)
    odd = odd_place("gz")
    refs[0][...] = jnp.where(odd, down_ref[...], up_ref[...])
    if len(refs) > 5:
        refs[1][...] = jnp.where(odd, up_ref[...], down_ref[...])


def edge_kernel(own_ref, xl_ref, xh_ref, lowy_ref, highy_ref, lhs_ref, el_ref, eh_ref, *refs):
    clear(refs[3])
    lower, upper = has_lower("gy"), has_upper("gy")
    row = iota((8, EZ), 0)

    def low(c, p):
        mine = pltpu.roll(x_plane(own_ref, xl_ref, xh_ref, c, p)[0:8], 3, 0)
        other = lowy_ref[(c * XN + p) * 4 : (c * XN + p) * 4 + 4, :]
        other = jnp.concatenate([other, other], axis=0)
        value = jnp.where(row == 3, average(lower, other, mine, mine), jnp.where(row < 3, other, mine))
        return jnp.where(row < 5, value, 0.0)

    def high(c, p):
        mine = pltpu.roll(x_plane(own_ref, xl_ref, xh_ref, c, p)[EY - 4 : EY + 4], 5, 0)
        other = highy_ref[(c * XN + p) * 4 : (c * XN + p) * 4 + 4, :]
        other = pltpu.roll(jnp.concatenate([other, other], axis=0), 1, 0)
        value = jnp.where(row == 1, average(upper, mine, other, mine), jnp.where(row < 1, mine, other))
        return jnp.where(row < 5, value, 0.0)

    for side, e_ref in ((low, el_ref), (high, eh_ref)):
        build_nodes(side, range(XN), 8, refs)
        energy_planes(lhs_ref[...], 4, refs, e_ref, 0, XE, 8, [(p, 0) for p in range(XE)], 0)


def triangle(value, axis):
    size = value.shape[axis]
    value = value + pltpu.roll(value, size - 1, axis)
    value = value + pltpu.roll(value, size - 2, axis)
    value = value + pltpu.roll(value, 1, axis)
    return value + pltpu.roll(value, 2, axis)


def weights(distance):
    return jnp.maximum(4 - jnp.abs(distance), 0).astype(F32)


def split_dot(value, right):
    rows = value.shape[0]
    product = jnp.dot(jnp.concatenate(halves(value), axis=0), right, preferred_element_type=F32)
    return product[0:rows] + product[rows:]


def edge_total(count, position, parts):
    total = None
    for offset in range(-RADIUS, RADIUS + 1):
        place = position + offset
        term = float(RADIUS + 1 - abs(offset)) * one_hot((place >= 0) & (place < count * parts))
        total = term if total is None else total + term
    return total


def field_kernel(ea_ref, eb_ref, el_ref, eh_ref, dens_ref, lowx_ref, highx_ref, lowy_ref, highy_ref,
                 g_ref, along_ref, right_ref, f_ref):
    rows = iota((QROWS, EZ), 0)
    lanes = iota((QROWS, EZ), 1)
    ok = (rows >= 5) & (rows < 55) & (lanes > 0) & (lanes < EZ - 1)
    row = iota((8, EZ), 0)
    for x in range(XE):
        if x < 4:
            middle = eb_ref[x]
        elif x < 18:
            middle = ea_ref[x - 4]
        else:
            middle = eb_ref[x - 14]
        low = pltpu.roll(el_ref[x], 5, 0)
        high = pltpu.roll(eh_ref[x], 3, 0)
        start = jnp.where(row < 1, low, middle[0:8])
        end = jnp.where(row < 3, middle[40:48], high)
        energy = jnp.concatenate([low, start, middle[8:40], end], axis=0)
        at = 3 * XN * 4 + x * 4
        pad = jnp.zeros((5, EZ), F32)
        d = jnp.concatenate(
            [pad, lowy_ref[at : at + 3, :], x_density(dens_ref, lowx_ref, highx_ref, x), highy_ref[at : at + 3, :], pad[0:1]], axis=0)
        f_ref[0, x] = jnp.where(ok, (SCALE * d) * d * d * energy, 0.0)
        f_ref[1, x] = jnp.where(ok, d, 0.0)

    for f in range(2):
        for t in range(QROWS // 8):
            at = slice(t * 8, t * 8 + 8)
            line = [f_ref[f, x, at, :] for x in range(XE)]
            for step in (1, 2, 1, 2):
                line = [line[i] + line[i + step] for i in range(len(line) - step)]
            for x in range(EX):
                f_ref[f, x, at, :] = line[x]
    k, col = iota((EZ, EZ), 0), iota((EZ, EZ), 1)
    along_ref[...] = jnp.where(k // 64 == col // 64, weights(k - col), 0.0).astype(BF16)
    j = (k % 64) // EX
    place = jnp.where(k < 64, j - 3, EZ - 1 + j)
    z = jnp.where(col % 8 < 4, EZ - 4 + col % 8, col % 8 - 4)
    right_ref[...] = jnp.where(k % EX == col // 8, weights(place - z), 0.0).astype(BF16)
    right = weights(k - col).astype(BF16)
    for f in range(2):
        for x in range(EX):
            g_ref[f, x] = split_dot(triangle(f_ref[f, x], 0)[8:QROWS], right)


def last_kernel(g_ref, along_ref, right_ref, rs_ref, rd_ref, oa_ref, ob_ref, od_ref, lhs_ref, *refs):
    messages, refs = refs[:-12], refs[-12:]
    outs, (ez_ref, c_ref, zl_ref, zh_ref, o_ref, sem), refs = refs[:2], refs[2:8], refs[8:]
    if len(messages) > 1:
        sort_sides("gz", *messages, zl_ref, zh_ref)
    else:
        odd = odd_place("gz")
        zl_ref[...] = jnp.where(odd, messages[0][...], 0.0)
        zh_ref[...] = jnp.where(odd, 0.0, messages[0][...])
    lower, upper = has_lower("gz"), has_upper("gz")

    def swap(value):
        return pltpu.roll(value, 64, 1)

    is_low = iota((3 * XR, EZ), 1) < 64
    oa, ob = oa_ref[...], ob_ref[...]
    zl0, zl1 = zl_ref[0:72, :], zl_ref[72:144, :]
    zh0, zh1 = zh_ref[0:72, :], zh_ref[72:144, :]
    nodes = (
        jnp.where(is_low, zl0, ob),
        jnp.where(is_low, swap(zl0), average(upper, oa, swap(zh0), oa)),
        jnp.where(is_low, zl1, zh0),
        jnp.where(is_low, average(lower, swap(zl1), oa, oa), swap(zh1)),
        jnp.where(is_low, ob, zh1),
    )
    build_nodes(lambda c, k: nodes[k][c * XR : (c + 1) * XR], range(5), XR, refs)
    for ref, step in zip(refs[:3], (8, 16, 16)):
        ref[5 * XR * step : (5 * XR + 8) * step, :] = jnp.zeros((8 * step, EZ), ref.dtype)

    lane = iota((XR, EZ), 1)
    low_side = lane < 64
    od = od_ref[...]
    dl0, dl1 = zl_ref[144:168, :], zl_ref[168:192, :]
    dh0, dh1 = zh_ref[144:168, :], zh_ref[168:192, :]
    dens = (
        jnp.where(low_side, dl0, od),
        jnp.where(low_side, swap(dl0), swap(dh0)),
        jnp.where(low_side, dl1, dh0),
        jnp.where(low_side, od, swap(dh1)),
    )
    inside = (lane % 64 >= 5) & (lane % 64 < 55) & (iota((XR, EZ), 0) < XE)
    lanes = iota((8, EZ), 1)
    at_end = (lanes < 4) | (lanes >= EZ - 4)
    copies = []
    for f in (1, 0):
        if f == 0:
            energy_planes(lhs_ref[...], 4, refs, ez_ref, 0, 4, XR, [(j, x) for j in range(4) for x in range(0, XR, 4)], 0)
        for j in range(4):
            d = dens[j]
            value = d if f == 1 else (SCALE * d) * d * d * ez_ref[j]
            c_ref[f, j * EX : (j + 1) * EX, :] = triangle_forward(jnp.where(inside, value, 0.0))[0:EX]
        turned = split_dot(c_ref[f], along_ref[...])
        turned = jnp.concatenate([turned, jnp.zeros((EZ - 4 * EX, EZ), F32)], axis=0).T
        ends = split_dot(turned[8:56] + pltpu.roll(turned[72:120], 64, 1), right_ref[...])
        inverse_ref = rs_ref if f == 0 else rd_ref
        for y in range(0, EY, 8):
            count = min(8, EY - y)
            for x in range(EX):
                end = jnp.where(at_end, pltpu.roll(ends[y : y + 8], (EZ - 4 - 8 * x) % EZ, 1), 0.0)
                value = (g_ref[f, x, y : y + 8, :] + end) * inverse_ref[x, y : y + 8, :]
                o_ref[f, pl.ds(y * EX + x, count, stride=EX), :] = value[0:count]
            block = pl.ds(y * EX, count * EX)
            copies.append(pltpu.make_async_copy(o_ref.at[f, block], outs[f].at[block], sem.at[len(copies)]))
            copies[-1].start()
    for copy in copies:
        copy.wait()


def triangle_forward(value):
    size = value.shape[0]
    for step in (1, 2, 1, 2):
        value = value + pltpu.roll(value, size - step, 0)
    return value


def call(kernel, outs, ins, scratch=(), limit=16, micros=1.0, space=VM):
    return pl.pallas_call(
        kernel,
        out_shape=[jax.ShapeDtypeStruct(shape, dtype) for shape, dtype in outs],
        in_specs=[pl.BlockSpec(memory_space=space) for space in ins],
        out_specs=[pl.BlockSpec(memory_space=space)] * len(outs),
        scratch_shapes=[pltpu.VMEM(item[0], item[1]) if isinstance(item, tuple) else item for item in scratch],
        compiler_params=pltpu.CompilerParams(vmem_limit_bytes=limit * 2**20),
        cost_estimate=pl.CostEstimate(flops=0, bytes_accessed=int(micros * 3.6e6), transcendentals=0),
    )


def exchange(axis, *values):
    count = lax.axis_size(axis)
    results = []
    for first, value in enumerate(values):
        pairs = [(i, i + 1) for i in range(first, count - 1, 2)]
        results.append(lax.ppermute(value, axis, pairs + [(j, i) for i, j in pairs]))
    return results


def local(local_solution, top_nodes, coarse_solution, corner_dofs, density, element_stiffness):
    dens = jnp.transpose(density, (1, 0, 2)).reshape(EY * EX, EZ)
    dofs = corner_dofs.reshape(8)
    shared = lax.axis_size("gz") == 2
    if shared:
        other = lax.ppermute(coarse_solution, "gz", [(0, 1), (1, 0)])
        coarse = jnp.stack([coarse_solution, other])
    else:
        coarse = lax.all_gather(coarse_solution, "gz")

    message = ((15, ROWS, EZ), F32)
    even, odd, tops = call(
        pack_kernel,
        [message, message, ((3, XR, EZ), F32)],
        [pltpu.HBM] * 4,
        [((2, 3, 4, NY, EZ), F32), ((3, NX, 1, NY), F32), ((EY * EX, EZ), F32), ((1, 8), jnp.int32), pltpu.SemaphoreType.DMA((9,))],
    )(*[
        pltpu.with_memory_space_constraint(value, pltpu.HBM)
        for value in (local_solution, jnp.transpose(top_nodes, (0, 1, 3, 2)), dens, dofs.reshape(1, 8))
    ])
    even_x, odd_x = exchange("gx", even, odd)

    own_planes = ((EX, ROWS, EZ), F32)
    rows3, rows4 = ((96, block_rows(3)), BF16), ((128, block_rows(4)), BF16)
    lhs, lhs_edge, lhs_z, dens, inverse_sens, inverse_smooth = call(
        prepare_kernel, [rows3, rows4, rows4, own_planes, own_planes, own_planes], [VM, VM], micros=1.0
    )(element_stiffness, dens)

    own, ea = call(
        functools.partial(own_kernel, shared),
        [((3 * NX, ROWS, EZ), F32), ((EX - 2, ROWS, EZ), F32)],
        [VM, VM, SM, SM],
        node_buffers((EX - 1) * ROWS, (EX - 2) * ROWS),
        micros=6.0,
    )(local_solution, lhs, coarse, dofs)

    face = ((12, ROWS, EZ), F32)
    y_message = ((Y_MESSAGE, EZ), F32)
    xl, xh, tx, even, odd, low_x, high_x = call(
        functools.partial(x_kernel, shared),
        [face, face, ((3, XR, EZ), F32), y_message, y_message, message, message],
        [VM, VM, VM, VM, VM, SM, SM],
        [y_message, y_message, ((4, XR, EZ), F32)],
        micros=2.0,
    )(own, tops, dens, even_x, odd_x, coarse, dofs)
    even_y, odd_y = exchange("gy", even, odd)

    (eb,) = call(
        side_kernel, [((8, ROWS, EZ), F32)], [VM] * 4, node_buffers(10 * ROWS, 4 * ROWS), micros=2.6
    )(own, xl, xh, lhs)

    (zo,) = call(turn_kernel, [((TILES, 8, EZ), F32)], [VM] * 6, micros=1.5)(own, xl, xh, dens, low_x, high_x)

    z_message = ((Z_MESSAGE, EZ), F32)
    low_y, high_y, oa, ob, od, *messages = call(
        y_kernel,
        [y_message, y_message, ((72, EZ), F32), ((72, EZ), F32), ((XR, EZ), F32)] + [z_message] * (1 if shared else 2),
        [VM] * 5,
        [((8 * 3 * XR, EZ), F32), ((8 * XR, EZ), F32), z_message, z_message],
        micros=1.0,
    )(tx, zo, eb, even_y, odd_y)
    received_z = exchange("gz", *messages)

    el, eh = call(
        edge_kernel,
        [((XE, 8, EZ), F32)] * 2,
        [VM] * 6,
        node_buffers(XN * 8, XE * 8),
        micros=2.3,
    )(own, xl, xh, low_y, high_y, lhs_edge)

    square = ((EZ, EZ), BF16)
    filtered, along_y, ends = call(
        field_kernel, [((2, EX, ROWS, EZ), F32), square, square], [VM] * 9, [((2, XE, QROWS, EZ), F32)], micros=1.5
    )(ea, eb, el, eh, dens, low_x, high_x, low_y, high_y)

    sens, smooth = call(
        last_kernel,
        [((EY * EX, EZ), F32)] * 2,
        [VM] * (9 + len(received_z)),
        [((4, XR, EZ), F32), ((2, 4 * EX, EZ), F32), z_message, z_message, ((2, EY * EX, EZ), F32),
         pltpu.SemaphoreType.DMA((12,))] + node_buffers(5 * XR + 8, 4 * XR),
        space=pltpu.HBM,
        micros=2.5,
    )(filtered, along_y, ends, inverse_sens, inverse_smooth, oa, ob, od, lhs_z, *received_z)

    def grid(value):
        return jnp.transpose(value.reshape(EY, EX, EZ), (1, 0, 2))

    return grid(sens), grid(smooth)


def solution(mesh):
    in_specs = (
        P(None, "gx", "gy", "gz"),
        P(None, "gx", "gy", "gz"),
        P(None, "gz"),
        P("gx", "gy", "gz", None),
        P("gx", "gy", "gz"),
        P(),
    )
    out_specs = (P("gx", "gy", "gz"), P("gx", "gy", "gz"))
    return jax.shard_map(local, mesh=mesh, in_specs=in_specs, out_specs=out_specs, check_vma=False)
```

```python
import functools

import jax
import jax.numpy as jnp
from jax import lax
from jax.experimental import pallas as pl
from jax.experimental.pallas import tpu as pltpu
from jax.sharding import PartitionSpec as P

RADIUS = 3
F32 = jnp.float32
BF16 = jnp.bfloat16
SCALE = -3.0 / 96.0
HIGHEST = lax.Precision.HIGHEST
VM = pltpu.VMEM
SM = pltpu.SMEM

EX, EY, EZ = 16, 44, 128
NX, NY = EX + 1, EY + 1
XN, XE = NX + 2 * RADIUS, EX + 2 * RADIUS
ROWS = 48
QROWS = 56
OWN = 12
XR = 24


def iota(shape, dim):
    return lax.broadcasted_iota(jnp.int32, shape, dim)


def one_hot(mask):
    return jnp.where(mask, 1.0, 0.0).astype(F32)


def halves(value):
    high = value.astype(BF16)
    return high, (value - high.astype(F32)).astype(BF16)


def corner_scalars(coarse_ref, dof_of, shared):
    width = coarse_ref.shape[2]
    own = lax.axis_index("gz")
    out = [[None] * 8 for _ in range(3)]
    for k in range(8):
        dof = dof_of(k)
        part = dof // width
        place = dof - part * width
        if shared:
            part = jnp.where(part == own, 0, 1)
        for c in range(3):
            out[c][k] = coarse_ref[part, c, place]
    return out


def corner_rows(corners, c):
    rz = iota((8, EZ), 1).astype(F32) * (1.0 / EZ)
    other = 1.0 - rz
    return [[corners[c][4 * kx + 2 * ky] * other + corners[c][4 * kx + 2 * ky + 1] * rz for ky in (0, 1)] for kx in (0, 1)]


def plane_interp(edges, i, rows):
    wx = i / EX
    first, second = [((1.0 - wx) * edges[0][ky] + wx * edges[1][ky])[0:1] for ky in (0, 1)]
    ry = iota((rows, EZ), 0).astype(F32) * (1.0 / EY)
    return (1.0 - ry) * first + ry * second


def block_rows(block):
    nodes = block + 1
    return 2 * (16 * nodes + 16 * ((nodes + 1) // 2))


def stiffness_rows(stiff, block, in_lanes):
    def target(h, t, r):
        s, c = r // 4, r % 4
        place = 4 * t + 2 * s + h if in_lanes else 4 * h + 2 * t + s
        return jnp.where(c < 3, 8 * c + place, -1)

    row = iota((32, 24), 0)
    left = one_hot(iota((32, 24), 1) == target(row // 16, row // 8 % 2, row % 8))
    full = jnp.dot(left, stiff, precision=HIGHEST, preferred_element_type=F32)
    nodes, width = block + 1, block_rows(block)
    split = 32 * nodes
    half = (width - split) // 2
    col = iota((24, width), 1)
    again = col >= split
    h = jnp.where(again, (col - split) // half, col // (16 * nodes))
    node = jnp.where(again, (col - split) % half // 8, col % (16 * nodes) // 16)
    wide = iota((32, width), 1) >= split
    rows = []
    for e in range(block):
        t = node - e
        right = one_hot((iota((24, width), 0) == target(h, t, col % 8)) & (t >= 0) & (t < 2))
        part = jnp.dot(full, right, precision=HIGHEST, preferred_element_type=F32)
        high = part.astype(BF16).astype(F32)
        rows.append(jnp.where(wide, part - high, high))
    return jnp.concatenate(rows, axis=0).astype(BF16)


def build_nodes(plane_of, planes, rows, refs, first=0):
    w_ref, b_ref, h_ref, _ = refs
    for p in planes:
        base = (first + p) * rows * 8
        zero = jnp.zeros((rows, EZ), F32)
        for c in range(3):
            value = plane_of(c, p)
            w_ref[pl.ds(base + c, rows, stride=8), :] = value
            w_ref[pl.ds(base + 4 + c, rows, stride=8), :] = pltpu.roll(value, EZ - 1, 1)
        w_ref[pl.ds(base + 3, rows, stride=8), :] = zero
        w_ref[pl.ds(base + 7, rows, stride=8), :] = zero

    def split(p, _):
        base = (first + p) * rows
        last = None
        for r in range(rows):
            value = w_ref[pl.ds(pl.multiple_of((base + r) * 8, 8), 8), :]
            high = value.astype(BF16).astype(F32)
            at = pl.ds(pl.multiple_of((base + r) * 16, 16), 16)
            b_ref[at, :] = jnp.concatenate([high, value - high], axis=0).astype(BF16)
            if last is not None:
                h_ref[pl.ds(pl.multiple_of((base + r - 1) * 16, 16), 16), :] = jnp.concatenate([last, high], axis=0).astype(BF16)
            last = high
        h_ref[at, :] = jnp.concatenate([last, last], axis=0).astype(BF16)
        return 0

    lax.fori_loop(0, len(planes), split, 0)


def energy_planes(lhs, block, refs, e_ref, first, count, rows, blocks, out_first):
    w_ref, b_ref, h_ref, s_ref = refs
    nodes = block + 1
    for i in range(0, len(blocks), 2):
        pair = [((first + p) * rows + r, p * rows + r) for p, r in blocks[i : i + 2]]
        right = []
        for at, _ in pair:
            parts = [b_ref[(at + far) * 16 : (at + far + nodes) * 16, :] for far in (0, rows)]
            for far in (0, rows):
                parts += [h_ref[(at + far + t) * 16 : (at + far + t + 1) * 16, :] for t in range(0, nodes, 2)]
            right.append(jnp.concatenate(parts, axis=0))
        product = jnp.dot(lhs, jnp.concatenate(right, axis=1), preferred_element_type=F32)
        for u, (at, out) in enumerate(pair):
            for e in range(block):
                part = product[32 * e : 32 * e + 32, u * EZ : (u + 1) * EZ]
                low = w_ref[(at + e) * 8 : (at + e + 2) * 8, :] * part[0:16]
                high = w_ref[(at + rows + e) * 8 : (at + rows + e + 2) * 8, :] * part[16:32]
                both = low + high
                s_ref[(out + e) * 8 : (out + e + 1) * 8, :] = both[0:8] + both[8:16]
    for p in range(count):
        total = None
        for s in (0, 1, 2, 4, 5, 6):
            term = s_ref[pl.ds(p * rows * 8 + s, rows, stride=8), :]
            total = term if total is None else total + term
        e_ref[out_first + p] = total


def node_buffers(count, energies):
    return [((count * 8, EZ), F32), ((count * 16, EZ), BF16), ((count * 16, EZ), BF16), ((energies * 8, EZ), F32)]


def odd_place(axis):
    return lax.axis_index(axis) % 2 == 1


X_MESSAGE = 688
X_DENSITY, X_TOP, X_DOFS = 576, 672, 684


def third_rows():
    spare = [(48 * i + NY, 3 * i, 3) for i in range(12)]
    return spare + [(X_DENSITY + EY, 36, 4), (X_DENSITY + ROWS + EY, 40, 4)]


def pack_kernel(local_ref, top_ref, dens_ref, dofs_ref, even_ref, odd_ref, tops_ref, l_ref, t_ref, d_ref, c_ref, sem):
    copies = []
    for side, node in ((0, EX - RADIUS), (1, 0)):
        for c in range(3):
            copies.append(pltpu.make_async_copy(local_ref.at[c, node : node + 4], l_ref.at[side, c], sem.at[len(copies)]))
    for source, dest in ((top_ref, t_ref), (dofs_ref, c_ref), (dens_ref, d_ref)):
        copies.append(pltpu.make_async_copy(source, dest, sem.at[len(copies)]))
    for copy in copies:
        copy.start()
    for out_ref in (even_ref, odd_ref):
        out_ref[X_TOP:X_MESSAGE, :] = jnp.zeros((X_MESSAGE - X_TOP, EZ), F32)
    clear(tops_ref)
    odd = odd_place("gx")
    outs = ((even_ref, odd), (odd_ref, jnp.logical_not(odd)))
    for copy in copies[:6]:
        copy.wait()
    for out_ref, flip in outs:
        side = flip.astype(jnp.int32)
        for c in range(3):
            for j in range(4):
                out_ref[(c * 4 + j) * ROWS : (c * 4 + j) * ROWS + NY, :] = l_ref[side, c, j]
    for copy in copies[6:]:
        copy.wait()
    for c in range(3):
        for i in range(NX):
            tops_ref[c, i : i + 1, 0:NY] = t_ref[c, i]
    for out_ref, flip in outs:
        for c in range(3):
            out_ref[X_TOP + 4 * c : X_TOP + 4 * c + 4, :] = jnp.where(
                flip, tops_ref[c, 0:4, :], tops_ref[c, EX - RADIUS : EX - RADIUS + 4, :])
        for j in range(3):
            value = jnp.where(flip, d_ref[pl.ds(j, EY, stride=EX), :], d_ref[pl.ds(EX - RADIUS + j, EY, stride=EX), :])
            if j < 2:
                out_ref[X_DENSITY + j * ROWS : X_DENSITY + j * ROWS + EY, :] = value
            else:
                for at, first, count in third_rows():
                    out_ref[at : at + count, :] = value[first : first + count]
        out_ref[X_DOFS : X_DOFS + 1, 0:8] = c_ref[...].astype(F32)


def sort_sides(axis, even_ref, odd_ref, low_ref, high_ref):
    odd = odd_place(axis)
    even, other = even_ref[...], odd_ref[...]
    low_ref[...] = jnp.where(has_lower(axis), jnp.where(odd, even, other), 0.0)
    high_ref[...] = jnp.where(has_upper(axis), jnp.where(odd, other, even), 0.0)


def prepare_kernel(stiff_ref, dens_ref, lhs_ref, lhs_edge_ref, lhs_z_ref, od_ref, rs_ref, rd_ref):
    stiff = stiff_ref[...]
    lhs_ref[...] = stiffness_rows(stiff, 3, False)
    lhs_edge_ref[...] = stiffness_rows(stiff, 4, False)
    lhs_z_ref[...] = stiffness_rows(stiff, 4, True)
    base_x, base_y, base_z = lax.axis_index("gx") * EX, lax.axis_index("gy") * EY, lax.axis_index("gz") * EZ
    inside = iota((ROWS, EZ), 0) < EY
    norm_y = edge_total(EY, base_y + iota((ROWS, EZ), 0), lax.axis_size("gy"))
    norm_z = edge_total(EZ, base_z + iota((ROWS, EZ), 1), lax.axis_size("gz"))
    inverse = 1.0 / jnp.where(inside, norm_y * norm_z, 1.0)
    place = base_x + iota((8, EZ), 0)
    inverse_x = [1.0 / edge_total(EX, place + t, lax.axis_size("gx")) for t in (0, 8)]
    for x in range(EX):
        d = dens_ref[pl.ds(x, EY, stride=EX), :]
        od_ref[x, 0:EY, :] = d
        od_ref[x, EY:ROWS, :] = jnp.ones((ROWS - EY, EZ), F32)
        both = inverse * inverse_x[x // 8][x % 8 : x % 8 + 1, :]
        rd_ref[x] = both
        rs_ref[x] = both / od_ref[x]


def own_kernel(shared, local_ref, lhs_ref, coarse_ref, dofs_ref, own_ref, e_ref, *refs):
    corners = corner_scalars(coarse_ref, lambda k: dofs_ref[k], shared)
    for c in range(3):
        edges = corner_rows(corners, c)
        for i in range(NX):
            own_ref[c * NX + i, 0:NY, :] = local_ref[c, i] + plane_interp(edges, i, NY)
            own_ref[c * NX + i, NY:ROWS, :] = jnp.zeros((ROWS - NY, EZ), F32)
    clear(refs[3])
    build_nodes(lambda c, p: own_ref[c * NX + p + 1], range(OWN + 1), ROWS, refs)
    blocks = [(p, r) for p in range(OWN) for r in range(1, EY - 1, 3)]
    energy_planes(lhs_ref[...], 3, refs, e_ref, 0, OWN, ROWS, blocks, 0)


def clear(ref):
    ref[...] = jnp.zeros(ref.shape, ref.dtype)


def average(flag, low, high, own):
    return jnp.where(flag, 0.5 * low + 0.5 * high, own)


def has_lower(axis):
    return lax.axis_index(axis) > 0


def has_upper(axis):
    return lax.axis_index(axis) < lax.axis_size(axis) - 1


def message_dofs(row):
    lane = iota((1, EZ), 1)
    return lambda k: jnp.sum(jnp.where(lane == k, row, 0.0)).astype(jnp.int32)


def top_interp(corners, c, rows):
    rx = iota((rows, EZ), 0).astype(F32) * (1.0 / EX)
    ry = iota((rows, EZ), 1).astype(F32) * (1.0 / EY)
    low = (1.0 - ry) * corners[c][1] + ry * corners[c][3]
    high = (1.0 - ry) * corners[c][5] + ry * corners[c][7]
    return (1.0 - rx) * low + rx * high


TOP_AT = 368
Y_MESSAGE = 392


def x_kernel(shared, own_ref, top_ref, dens_ref, even_ref, odd_ref, coarse_ref, dofs_ref,
             xl_ref, xh_ref, tx_ref, yeven_ref, yodd_ref, hd_ref, up_ref, down_ref, t_ref):
    odd = odd_place("gx")

    def low_rows(at, count):
        return jnp.where(odd, even_ref[at : at + count, :], odd_ref[at : at + count, :])

    def high_rows(at, count):
        return jnp.where(odd, odd_ref[at : at + count, :], even_ref[at : at + count, :])

    corners = corner_scalars(coarse_ref, lambda k: dofs_ref[k], shared)
    corners_low = corner_scalars(coarse_ref, message_dofs(low_rows(X_DOFS, 1)), shared)
    corners_high = corner_scalars(coarse_ref, message_dofs(high_rows(X_DOFS, 1)), shared)
    lower, upper = has_lower("gx"), has_upper("gx")
    for side, side_rows, there in ((0, low_rows, lower), (3, high_rows, upper)):
        for j in range(2):
            hd_ref[side + j] = jnp.where(there, side_rows(X_DENSITY + j * ROWS, ROWS), 0.0)
        hd_ref[side + 2, EY:ROWS, :] = jnp.zeros((ROWS - EY, EZ), F32)
        for at, first, count in third_rows():
            hd_ref[side + 2, first : first + count, :] = jnp.where(there, side_rows(at, count), 0.0)
    for c in range(3):
        edges_low, edges_high = corner_rows(corners_low, c), corner_rows(corners_high, c)
        for j in range(4):
            value = low_rows((c * 4 + j) * ROWS, ROWS) + plane_interp(edges_low, EX - RADIUS + j, ROWS)
            if j == 3:
                mine = own_ref[c * NX]
                value = average(lower, value, mine, mine)
            xl_ref[c * 4 + j] = value
            value = high_rows((c * 4 + j) * ROWS, ROWS) + plane_interp(edges_high, j, ROWS)
            if j == 0:
                mine = own_ref[c * NX + EX]
                value = average(upper, mine, value, mine)
            xh_ref[c * 4 + j] = value

    t_ref[...] = jnp.zeros(t_ref.shape, F32)
    for c in range(3):
        t_ref[0] = top_ref[c] + top_interp(corners, c, XR)
        t_ref[1, 0:4, :] = low_rows(X_TOP + 4 * c, 4)
        t_ref[2, 0:4, :] = high_rows(X_TOP + 4 * c, 4)
        t_low = t_ref[1, 0:8, :] + pltpu.roll(top_interp(corners_low, c, 24), 24 - (EX - RADIUS), 0)[0:8]
        t_high = t_ref[2, 0:8, :] + top_interp(corners_high, c, 8)
        first = average(lower, t_low[3:4], t_ref[0, 0:1, :], t_ref[0, 0:1, :])
        last = average(upper, t_ref[0, EX : EX + 1, :], t_high[0:1], t_ref[0, EX : EX + 1, :])
        t_ref[3, 0:3, :] = t_low[0:3]
        t_ref[3, 3:4, :] = first
        t_ref[3, 4:19, :] = t_ref[0, 1:EX, :]
        t_ref[3, 19:20, :] = last
        t_ref[3, 20:23, :] = t_high[1:4]
        lane = iota((XR, EZ), 1)
        tx_ref[c] = jnp.where(lane < NY + 8, pltpu.roll(t_ref[3], 8, 1), 0.0)

    for out_ref, node, elem, lane_at in ((up_ref, EY - RADIUS, EY - RADIUS, EY - RADIUS + 8), (down_ref, 0, 0, 8)):
        for c in range(3):
            for p in range(XN):
                at = (c * XN + p) * 4
                out_ref[at : at + 4, :] = x_plane(own_ref, xl_ref, xh_ref, c, p)[node : node + 4]
        for x in range(XE):
            at = 3 * XN * 4 + x * 4
            out_ref[at : at + 3, :] = x_density(dens_ref, hd_ref, x)[elem : elem + 3]
            out_ref[at + 3 : at + 4, :] = jnp.zeros((1, EZ), F32)
        out_ref[364:TOP_AT, :] = jnp.zeros((TOP_AT - 364, EZ), F32)
        lane = iota((XR, EZ), 1)
        total = jnp.zeros((XR, EZ), F32)
        for c in range(3):
            moved = pltpu.roll(tx_ref[c], (4 * c - lane_at) % EZ, 1)
            total = jnp.where((lane >= 4 * c) & (lane < 4 * c + 4), moved, total)
        out_ref[TOP_AT:Y_MESSAGE, :] = total
    odd = odd_place("gy")
    up, down = up_ref[...], down_ref[...]
    yeven_ref[...] = jnp.where(odd, down, up)
    yodd_ref[...] = jnp.where(odd, up, down)


def side_kernel(own_ref, xl_ref, xh_ref, lhs_ref, e_ref, *refs):
    clear(refs[3])
    high = XE - 4 - OWN

    def plane(c, p):
        if p < 5:
            return x_plane(own_ref, xl_ref, xh_ref, c, p)
        return x_plane(own_ref, xl_ref, xh_ref, c, p - 5 + 4 + OWN)

    build_nodes(plane, range(5 + high + 1), ROWS, refs)
    for first, count, out_first in ((0, 4, 0), (5, high, 4)):
        blocks = [(p, r) for p in range(count) for r in range(1, EY - 1, 3)]
        energy_planes(lhs_ref[...], 3, refs, e_ref, first, count, ROWS, blocks, out_first)


Z_MESSAGE = 192
TILES = 3 * XN + XE


def x_plane(own_ref, xl_ref, xh_ref, c, p):
    if p < 4:
        return xl_ref[c * 4 + p]
    if p < 19:
        return own_ref[c * NX + p - 3]
    return xh_ref[c * 4 + p - 19]


def x_density(dens_ref, hd_ref, x, rows=EY):
    if x < 3:
        return hd_ref[x, 0:rows, :]
    if x < 19:
        return dens_ref[x - 3, 0:rows, :]
    return hd_ref[x - 16, 0:rows, :]


def end_planes(turned):
    return jnp.concatenate([turned[0:4], turned[EZ - 4 : EZ]], axis=0)


def turn_kernel(own_ref, xl_ref, xh_ref, dens_ref, hd_ref, z_ref):
    head = jnp.zeros((8, EZ), F32)

    def padded(i):
        if i < 3 * XN:
            return [head, x_plane(own_ref, xl_ref, xh_ref, i // XN, i % XN), head]
        return [head, x_density(dens_ref, hd_ref, i - 3 * XN, ROWS), head]

    lane = iota((8, EZ), 1)
    for i in range(0, TILES, 2):
        both = end_planes(jnp.concatenate(padded(i) + padded(min(i + 1, TILES - 1)), axis=0).T)
        z_ref[i] = jnp.where(lane < 64, both, 0.0)
        if i + 1 < TILES:
            z_ref[i + 1] = jnp.where(lane < 64, pltpu.roll(both, 64, 1), 0.0)


def y_kernel(tx_ref, zo_ref, eb_ref, even_ref, odd_ref,
             low_ref, high_ref, oa_ref, ob_ref, od_ref, *refs):
    del eb_ref
    z_ref, d_ref, up_ref, down_ref = refs[-4:]
    sort_sides("gy", even_ref, odd_ref, low_ref, high_ref)
    lower, upper = has_lower("gy"), has_upper("gy")
    clear(z_ref)
    clear(d_ref)
    lane = iota((8, EZ), 1)
    for first in range(0, TILES, 32):
        count = min(32, TILES - first)
        turned = []
        for ref in (low_ref, high_ref):
            block = ref[first * 4 : (first + count) * 4, :]
            if count < 32:
                block = jnp.concatenate([block, jnp.zeros(((32 - count) * 4, EZ), F32)], axis=0)
            turned.append(end_planes(block.T))
        for t in range(count):
            i = first + t
            low = pltpu.roll(turned[0], (5 - 4 * t) % EZ, 1)
            high = pltpu.roll(turned[1], (52 - 4 * t) % EZ, 1)
            mine = zo_ref[i]
            if i < 3 * XN:
                at = (i // XN) * XR + i % XN
                value = jnp.where((lane >= 5) & (lane < 8), low, mine)
                value = jnp.where((lane == 8) & lower, 0.5 * low + 0.5 * mine, value)
                value = jnp.where((lane == 52) & upper, 0.5 * mine + 0.5 * high, value)
                z_ref[at * 8 : at * 8 + 8, :] = jnp.where((lane > 52) & (lane < 56), high, value)
            else:
                at = i - 3 * XN
                value = jnp.where((lane >= 5) & (lane < 8), low, mine)
                d_ref[at * 8 : at * 8 + 8, :] = jnp.where((lane >= 52) & (lane < 55), high, value)

    lane = iota((XR, EZ), 1)
    tops = []
    for c in range(3):
        mine = tx_ref[c]
        low = pltpu.roll(low_ref[TOP_AT:Y_MESSAGE, :], (5 - 4 * c) % EZ, 1)
        high = pltpu.roll(high_ref[TOP_AT:Y_MESSAGE, :], (52 - 4 * c) % EZ, 1)
        value = jnp.where((lane >= 5) & (lane < 8), low, mine)
        value = jnp.where(lane == 8, average(lower, low, mine, mine), value)
        value = jnp.where(lane == 52, average(upper, mine, high, mine), value)
        tops.append(jnp.where((lane > 52) & (lane < 56), high, value))
    top = jnp.concatenate(tops, axis=0)

    def nodes(k):
        return z_ref[pl.ds(k, 3 * XR, stride=8), :]

    def dens(k):
        return d_ref[pl.ds(k, XR, stride=8), :]

    def pack(low, high):
        return low + pltpu.roll(high, 64, 1)

    oa_ref[...] = pack(nodes(0), top)
    ob_ref[...] = pack(nodes(1), nodes(7))
    od_ref[...] = pack(dens(0), dens(7))
    up_ref[0:72, :] = pack(nodes(5), nodes(6))
    up_ref[72:144, :] = pack(nodes(7), top)
    up_ref[144:168, :] = pack(dens(5), dens(6))
    up_ref[168:192, :] = dens(7)
    down_ref[0:72, :] = pack(nodes(0), nodes(1))
    down_ref[72:144, :] = pack(nodes(2), nodes(3))
    down_ref[144:168, :] = pack(dens(0), dens(1))
    down_ref[168:192, :] = dens(2)
    odd = odd_place("gz")
    refs[0][...] = jnp.where(odd, down_ref[...], up_ref[...])
    if len(refs) > 5:
        refs[1][...] = jnp.where(odd, up_ref[...], down_ref[...])


def edge_kernel(own_ref, xl_ref, xh_ref, lowy_ref, highy_ref, lhs_ref, el_ref, eh_ref, *refs):
    clear(refs[3])
    lower, upper = has_lower("gy"), has_upper("gy")
    row = iota((8, EZ), 0)

    def low(c, p):
        mine = pltpu.roll(x_plane(own_ref, xl_ref, xh_ref, c, p)[0:8], 3, 0)
        other = lowy_ref[(c * XN + p) * 4 : (c * XN + p) * 4 + 4, :]
        other = jnp.concatenate([other, other], axis=0)
        value = jnp.where(row == 3, average(lower, other, mine, mine), jnp.where(row < 3, other, mine))
        return jnp.where(row < 5, value, 0.0)

    def high(c, p):
        mine = pltpu.roll(x_plane(own_ref, xl_ref, xh_ref, c, p)[EY - 4 : EY + 4], 5, 0)
        other = highy_ref[(c * XN + p) * 4 : (c * XN + p) * 4 + 4, :]
        other = pltpu.roll(jnp.concatenate([other, other], axis=0), 1, 0)
        value = jnp.where(row == 1, average(upper, mine, other, mine), jnp.where(row < 1, mine, other))
        return jnp.where(row < 5, value, 0.0)

    for side, e_ref in ((low, el_ref), (high, eh_ref)):
        build_nodes(side, range(XN), 8, refs)
        energy_planes(lhs_ref[...], 4, refs, e_ref, 0, XE, 8, [(p, 0) for p in range(XE)], 0)


def triangle(value, axis):
    size = value.shape[axis]
    value = value + pltpu.roll(value, size - 1, axis)
    value = value + pltpu.roll(value, size - 2, axis)
    value = value + pltpu.roll(value, 1, axis)
    return value + pltpu.roll(value, 2, axis)


def weights(distance):
    return jnp.maximum(4 - jnp.abs(distance), 0).astype(F32)


def split_dot(value, right):
    rows = value.shape[0]
    product = jnp.dot(jnp.concatenate(halves(value), axis=0), right, preferred_element_type=F32)
    return product[0:rows] + product[rows:]


def edge_total(count, position, parts):
    total = None
    for offset in range(-RADIUS, RADIUS + 1):
        place = position + offset
        term = float(RADIUS + 1 - abs(offset)) * one_hot((place >= 0) & (place < count * parts))
        total = term if total is None else total + term
    return total


def field_kernel(ea_ref, eb_ref, el_ref, eh_ref, dens_ref, hd_ref, lowy_ref, highy_ref,
                 g_ref, along_ref, right_ref, f_ref):
    rows = iota((QROWS, EZ), 0)
    lanes = iota((QROWS, EZ), 1)
    ok = (rows >= 5) & (rows < 55) & (lanes > 0) & (lanes < EZ - 1)
    row = iota((8, EZ), 0)
    for x in range(XE):
        if x < 4:
            middle = eb_ref[x]
        elif x < 4 + OWN:
            middle = ea_ref[x - 4]
        else:
            middle = eb_ref[x - OWN]
        low = pltpu.roll(el_ref[x], 5, 0)
        high = pltpu.roll(eh_ref[x], 3, 0)
        start = jnp.where(row < 1, low, middle[0:8])
        end = jnp.where(row < 3, middle[40:48], high)
        energy = jnp.concatenate([low, start, middle[8:40], end], axis=0)
        at = 3 * XN * 4 + x * 4
        pad = jnp.zeros((5, EZ), F32)
        d = jnp.concatenate(
            [pad, lowy_ref[at : at + 3, :], x_density(dens_ref, hd_ref, x), highy_ref[at : at + 3, :], pad[0:1]], axis=0)
        f_ref[0, x] = jnp.where(ok, (SCALE * d) * d * d * energy, 0.0)
        f_ref[1, x] = jnp.where(ok, d, 0.0)

    for f in range(2):
        for t in range(QROWS // 8):
            at = slice(t * 8, t * 8 + 8)
            line = [f_ref[f, x, at, :] for x in range(XE)]
            for step in (1, 2, 1, 2):
                line = [line[i] + line[i + step] for i in range(len(line) - step)]
            for x in range(EX):
                f_ref[f, x, at, :] = line[x]
    k, col = iota((EZ, EZ), 0), iota((EZ, EZ), 1)
    along_ref[...] = jnp.where(k // 64 == col // 64, weights(k - col), 0.0).astype(BF16)
    j = (k % 64) // EX
    place = jnp.where(k < 64, j - 3, EZ - 1 + j)
    z = jnp.where(col % 8 < 4, EZ - 4 + col % 8, col % 8 - 4)
    right_ref[...] = jnp.where(k % EX == col // 8, weights(place - z), 0.0).astype(BF16)
    right = weights(k - col).astype(BF16)
    for f in range(2):
        for x in range(EX):
            g_ref[f, x] = split_dot(triangle(f_ref[f, x], 0)[8:QROWS], right)


def last_kernel(g_ref, along_ref, right_ref, rs_ref, rd_ref, oa_ref, ob_ref, od_ref, lhs_ref, *refs):
    messages, refs = refs[:-12], refs[-12:]
    outs, (ez_ref, c_ref, zl_ref, zh_ref, o_ref, sem), refs = refs[:2], refs[2:8], refs[8:]
    if len(messages) > 1:
        sort_sides("gz", *messages, zl_ref, zh_ref)
    else:
        odd = odd_place("gz")
        zl_ref[...] = jnp.where(odd, messages[0][...], 0.0)
        zh_ref[...] = jnp.where(odd, 0.0, messages[0][...])
    lower, upper = has_lower("gz"), has_upper("gz")

    def swap(value):
        return pltpu.roll(value, 64, 1)

    is_low = iota((3 * XR, EZ), 1) < 64
    oa, ob = oa_ref[...], ob_ref[...]
    zl0, zl1 = zl_ref[0:72, :], zl_ref[72:144, :]
    zh0, zh1 = zh_ref[0:72, :], zh_ref[72:144, :]
    nodes = (
        jnp.where(is_low, zl0, ob),
        jnp.where(is_low, swap(zl0), average(upper, oa, swap(zh0), oa)),
        jnp.where(is_low, zl1, zh0),
        jnp.where(is_low, average(lower, swap(zl1), oa, oa), swap(zh1)),
        jnp.where(is_low, ob, zh1),
    )
    build_nodes(lambda c, k: nodes[k][c * XR : (c + 1) * XR], range(5), XR, refs)
    for ref, step in zip(refs[:3], (8, 16, 16)):
        ref[5 * XR * step : (5 * XR + 8) * step, :] = jnp.zeros((8 * step, EZ), ref.dtype)

    lane = iota((XR, EZ), 1)
    low_side = lane < 64
    od = od_ref[...]
    dl0, dl1 = zl_ref[144:168, :], zl_ref[168:192, :]
    dh0, dh1 = zh_ref[144:168, :], zh_ref[168:192, :]
    dens = (
        jnp.where(low_side, dl0, od),
        jnp.where(low_side, swap(dl0), swap(dh0)),
        jnp.where(low_side, dl1, dh0),
        jnp.where(low_side, od, swap(dh1)),
    )
    inside = (lane % 64 >= 5) & (lane % 64 < 55) & (iota((XR, EZ), 0) < XE)
    lanes = iota((16, EZ), 1)
    at_end = (lanes < 4) | (lanes >= EZ - 4)
    energy_planes(lhs_ref[...], 4, refs, ez_ref, 0, 4, XR, [(j, x) for j in range(4) for x in range(0, XR, 4)], 0)
    ends = []
    for f in range(2):
        for j in range(4):
            d = dens[j]
            value = d if f == 1 else (SCALE * d) * d * d * ez_ref[j]
            c_ref[f, j * EX : (j + 1) * EX, :] = triangle_forward(jnp.where(inside, value, 0.0))[0:EX]
        turned = split_dot(c_ref[f], along_ref[...])
        turned = jnp.concatenate([turned, jnp.zeros((EZ - 4 * EX, EZ), F32)], axis=0).T
        ends.append(split_dot(turned[8:56] + pltpu.roll(turned[72:120], 64, 1), right_ref[...]))
    copies = []
    for y in (0, 16, 32):
        count = min(16, EY - y)
        for f, inverse_ref in ((0, rs_ref), (1, rd_ref)):
            for x in range(EX):
                end = jnp.where(at_end, pltpu.roll(ends[f][y : y + 16], (EZ - 4 - 8 * x) % EZ, 1), 0.0)
                value = (g_ref[f, x, y : y + 16, :] + end) * inverse_ref[x, y : y + 16, :]
                o_ref[f, pl.ds(y * EX + x, count, stride=EX), :] = value[0:count]
            block = pl.ds(y * EX, count * EX)
            copies.append(pltpu.make_async_copy(o_ref.at[f, block], outs[f].at[block], sem.at[len(copies)]))
            copies[-1].start()
    for copy in copies:
        copy.wait()


def triangle_forward(value):
    size = value.shape[0]
    for step in (1, 2, 1, 2):
        value = value + pltpu.roll(value, size - step, 0)
    return value


def call(kernel, outs, ins, scratch=(), limit=16, micros=1.0, space=VM):
    return pl.pallas_call(
        kernel,
        out_shape=[jax.ShapeDtypeStruct(shape, dtype) for shape, dtype in outs],
        in_specs=[pl.BlockSpec(memory_space=space) for space in ins],
        out_specs=[pl.BlockSpec(memory_space=space)] * len(outs),
        scratch_shapes=[pltpu.VMEM(item[0], item[1]) if isinstance(item, tuple) else item for item in scratch],
        compiler_params=pltpu.CompilerParams(vmem_limit_bytes=limit * 2**20),
        cost_estimate=pl.CostEstimate(flops=0, bytes_accessed=int(micros * 3.6e6), transcendentals=0),
    )


def exchange(axis, spare, *values):
    count, others = lax.axis_size(axis), lax.axis_size(spare)
    names = tuple(sorted((axis, spare)))
    step, spare_step = (others, 1) if names[0] == axis else (1, count)
    results = []
    for first, value in enumerate(values):
        moves = []
        for i in range(count):
            j = i + 1 if i % 2 == first else i - 1
            for o in range(others):
                target = (j, o) if 0 <= j < count else (i, o ^ 1)
                moves.append((i * step + o * spare_step, target[0] * step + target[1] * spare_step))
        results.append(lax.ppermute(value, names, moves))
    return results


def local(local_solution, top_nodes, coarse_solution, corner_dofs, density, element_stiffness):
    dens = jnp.transpose(density, (1, 0, 2)).reshape(EY * EX, EZ)
    dofs = corner_dofs.reshape(8)
    shared = lax.axis_size("gz") == 2
    if shared:
        other = lax.ppermute(coarse_solution, "gz", [(0, 1), (1, 0)])
        coarse = jnp.stack([coarse_solution, other])
    else:
        coarse = lax.all_gather(coarse_solution, "gz")

    message = ((X_MESSAGE, EZ), F32)
    even, odd, tops = call(
        pack_kernel,
        [message, message, ((3, XR, EZ), F32)],
        [pltpu.HBM] * 4,
        [((2, 3, 4, NY, EZ), F32), ((3, NX, 1, NY), F32), ((EY * EX, EZ), F32), ((1, 8), jnp.int32), pltpu.SemaphoreType.DMA((9,))],
    )(*[
        pltpu.with_memory_space_constraint(value, pltpu.HBM)
        for value in (local_solution, jnp.transpose(top_nodes, (0, 1, 3, 2)), dens, dofs.reshape(1, 8))
    ])
    even_x, odd_x = exchange("gx", "gy", even, odd)

    own_planes = ((EX, ROWS, EZ), F32)
    rows3, rows4 = ((96, block_rows(3)), BF16), ((128, block_rows(4)), BF16)
    lhs, lhs_edge, lhs_z, dens, inverse_sens, inverse_smooth = call(
        prepare_kernel, [rows3, rows4, rows4, own_planes, own_planes, own_planes], [VM, VM], micros=1.0
    )(element_stiffness, dens)

    own, ea = call(
        functools.partial(own_kernel, shared),
        [((3 * NX, ROWS, EZ), F32), ((OWN, ROWS, EZ), F32)],
        [VM, VM, SM, SM],
        node_buffers((OWN + 1) * ROWS, OWN * ROWS),
        micros=6.0,
    )(local_solution, lhs, coarse, dofs)

    face = ((12, ROWS, EZ), F32)
    y_message = ((Y_MESSAGE, EZ), F32)
    xl, xh, tx, even, odd, halo_dens = call(
        functools.partial(x_kernel, shared),
        [face, face, ((3, XR, EZ), F32), y_message, y_message, ((6, ROWS, EZ), F32)],
        [VM, VM, VM, VM, VM, SM, SM],
        [y_message, y_message, ((4, XR, EZ), F32)],
        micros=2.0,
    )(own, tops, dens, even_x, odd_x, coarse, dofs)
    even_y, odd_y = exchange("gy", "gz", even, odd)

    (eb,) = call(
        side_kernel, [((XE - OWN, ROWS, EZ), F32)], [VM] * 4, node_buffers((XE - OWN + 2) * ROWS, (XE - 4 - OWN) * ROWS), micros=2.6
    )(own, xl, xh, lhs)

    (zo,) = call(turn_kernel, [((TILES, 8, EZ), F32)], [VM] * 5, micros=1.5)(own, xl, xh, dens, halo_dens)

    z_message = ((Z_MESSAGE, EZ), F32)
    low_y, high_y, oa, ob, od, *messages = call(
        y_kernel,
        [y_message, y_message, ((72, EZ), F32), ((72, EZ), F32), ((XR, EZ), F32)] + [z_message] * (1 if shared else 2),
        [VM] * 5,
        [((8 * 3 * XR, EZ), F32), ((8 * XR, EZ), F32), z_message, z_message],
        micros=1.0,
    )(tx, zo, eb, even_y, odd_y)
    received_z = exchange("gz", "gy", *messages)

    el, eh = call(
        edge_kernel,
        [((XE, 8, EZ), F32)] * 2,
        [VM] * 6,
        node_buffers(XN * 8, XE * 8),
        micros=2.3,
    )(own, xl, xh, low_y, high_y, lhs_edge)

    square = ((EZ, EZ), BF16)
    filtered, along_y, ends = call(
        field_kernel, [((2, EX, ROWS, EZ), F32), square, square], [VM] * 8, [((2, XE, QROWS, EZ), F32)], micros=1.5
    )(ea, eb, el, eh, dens, halo_dens, low_y, high_y)

    sens, smooth = call(
        last_kernel,
        [((EY * EX, EZ), F32)] * 2,
        [VM] * (9 + len(received_z)),
        [((4, XR, EZ), F32), ((2, 4 * EX, EZ), F32), z_message, z_message, ((2, EY * EX, EZ), F32),
         pltpu.SemaphoreType.DMA((6,))] + node_buffers(5 * XR + 8, 4 * XR),
        space=pltpu.HBM,
        micros=2.5,
    )(filtered, along_y, ends, inverse_sens, inverse_smooth, oa, ob, od, lhs_z, *received_z)

    def grid(value):
        return jnp.transpose(value.reshape(EY, EX, EZ), (1, 0, 2))

    return grid(sens), grid(smooth)


def solution(mesh):
    in_specs = (
        P(None, "gx", "gy", "gz"),
        P(None, "gx", "gy", "gz"),
        P(None, "gz"),
        P("gx", "gy", "gz", None),
        P("gx", "gy", "gz"),
        P(),
    )
    out_specs = (P("gx", "gy", "gz"), P("gx", "gy", "gz"))
    return jax.shard_map(local, mesh=mesh, in_specs=in_specs, out_specs=out_specs, check_vma=False)
```

```python
import functools

import jax
import jax.numpy as jnp
from jax import lax
from jax.experimental import pallas as pl
from jax.experimental.pallas import tpu as pltpu
from jax.sharding import PartitionSpec as P

RADIUS = 3
F32 = jnp.float32
BF16 = jnp.bfloat16
SCALE = -3.0 / 96.0
HIGHEST = lax.Precision.HIGHEST
VM = pltpu.VMEM

EX, EY, EZ = 16, 44, 128
NX, NY = EX + 1, EY + 1
XN, XE = NX + 2 * RADIUS, EX + 2 * RADIUS
ROWS = 48
QROWS = 56
OWN = 12
XR = 24


def iota(shape, dim):
    return lax.broadcasted_iota(jnp.int32, shape, dim)


def one_hot(mask):
    return jnp.where(mask, 1.0, 0.0).astype(F32)


def halves(value):
    high = value.astype(BF16)
    return high, (value - high.astype(F32)).astype(BF16)


def as_column(row):
    lane, sub = iota((8, EZ), 1), iota((8, EZ), 0)
    return jnp.sum(jnp.where(lane == sub, row, 0.0), axis=1, keepdims=True)


def corner_values(coarse_ref, dofs, shared):
    parts, _, width = coarse_ref.shape
    dofs = dofs.astype(jnp.int32)
    own = lax.axis_index("gz")
    lane = iota((8, width), 1)
    totals = [0.0] * 3
    for part in range(parts):
        place = part if not shared else own if part == 0 else 1 - own
        found = lane + place * width == dofs
        for c in range(3):
            totals[c] = totals[c] + jnp.where(found, coarse_ref[part, c : c + 1, :], 0.0)
    return [jnp.broadcast_to(jnp.sum(total, axis=1, keepdims=True), (8, EZ)) for total in totals]


def corner_rows(corners, c):
    rz = iota((8, EZ), 1).astype(F32) * (1.0 / EZ)
    other = 1.0 - rz
    value = [corners[c][k : k + 1] for k in range(8)]
    return [[value[4 * kx + 2 * ky] * other + value[4 * kx + 2 * ky + 1] * rz for ky in (0, 1)] for kx in (0, 1)]


def plane_interp(edges, i, rows, start=0):
    wx = i / EX
    first, second = [((1.0 - wx) * edges[0][ky] + wx * edges[1][ky])[0:1] for ky in (0, 1)]
    ry = (start + iota((rows, EZ), 0)).astype(F32) * (1.0 / EY)
    return (1.0 - ry) * first + ry * second


def block_rows(block):
    nodes = block + 1
    return 2 * (16 * nodes + 16 * ((nodes + 1) // 2))


def stiffness_rows(stiff, block, in_lanes):
    def target(h, t, r):
        s, c = r // 4, r % 4
        place = 4 * t + 2 * s + h if in_lanes else 4 * h + 2 * t + s
        return jnp.where(c < 3, 8 * c + place, -1)

    row = iota((32, 24), 0)
    left = one_hot(iota((32, 24), 1) == target(row // 16, row // 8 % 2, row % 8))
    full = jnp.dot(left, stiff, precision=HIGHEST, preferred_element_type=F32)
    nodes, width = block + 1, block_rows(block)
    split = 32 * nodes
    half = (width - split) // 2
    col = iota((24, width), 1)
    again = col >= split
    h = jnp.where(again, (col - split) // half, col // (16 * nodes))
    node = jnp.where(again, (col - split) % half // 8, col % (16 * nodes) // 16)
    wide = iota((32, width), 1) >= split
    rows = []
    for e in range(block):
        t = node - e
        right = one_hot((iota((24, width), 0) == target(h, t, col % 8)) & (t >= 0) & (t < 2))
        part = jnp.dot(full, right, precision=HIGHEST, preferred_element_type=F32)
        high = part.astype(BF16).astype(F32)
        rows.append(jnp.where(wide, part - high, high))
    return jnp.concatenate(rows, axis=0).astype(BF16)


def build_nodes(plane_of, planes, rows, refs, first=0):
    w_ref, b_ref, h_ref = refs
    for p in planes:
        base = (first + p) * rows * 8
        zero = jnp.zeros((rows, EZ), F32)
        for c in range(3):
            value = plane_of(c, p)
            w_ref[pl.ds(base + c, rows, stride=8), :] = value
            w_ref[pl.ds(base + 4 + c, rows, stride=8), :] = pltpu.roll(value, EZ - 1, 1)
        w_ref[pl.ds(base + 3, rows, stride=8), :] = zero
        w_ref[pl.ds(base + 7, rows, stride=8), :] = zero

    def split(p, _):
        base = (first + p) * rows
        last = None
        for r in range(rows):
            value = w_ref[pl.ds(pl.multiple_of((base + r) * 8, 8), 8), :]
            high = value.astype(BF16).astype(F32)
            at = pl.ds(pl.multiple_of((base + r) * 16, 16), 16)
            b_ref[at, :] = jnp.concatenate([high, value - high], axis=0).astype(BF16)
            if last is not None:
                h_ref[pl.ds(pl.multiple_of((base + r - 1) * 16, 16), 16), :] = jnp.concatenate([last, high], axis=0).astype(BF16)
            last = high
        h_ref[at, :] = jnp.concatenate([last, last], axis=0).astype(BF16)
        return 0

    lax.fori_loop(0, len(planes), split, 0)


def sum_rows(values):
    row = iota((8, EZ), 0)
    for step in (1, 2, 4):
        first = row % (2 * step) < step
        values = [
            jnp.where(first, a, b) + pltpu.roll(jnp.where(first, b, a), step, 0)
            for a, b in zip(values[::2], values[1::2])
        ]
    return values[0]


def energy_planes(lhs, block, refs, e_ref, first, count, rows, blocks, out_first):
    w_ref, b_ref, h_ref = refs
    nodes = block + 1
    zero = jnp.zeros((8, EZ), F32)
    found, left = {}, {(p, t) for p in range(count) for t in range(0, rows, 8)}

    def store(before):
        for p, t in sorted(left):
            if (p, t + 7) < before:
                values = [found.pop((p, t + i), zero) for i in range(8)]
                e_ref[out_first + p, t : t + 8, :] = zero if all(v is zero for v in values) else sum_rows(values)
                left.remove((p, t))

    for i in range(0, len(blocks), 2):
        pair = blocks[i : i + 2]
        right = []
        for p, r in pair:
            at = (first + p) * rows + r
            parts = [b_ref[(at + far) * 16 : (at + far + nodes) * 16, :] for far in (0, rows)]
            for far in (0, rows):
                parts += [h_ref[(at + far + t) * 16 : (at + far + t + 1) * 16, :] for t in range(0, nodes, 2)]
            right.append(jnp.concatenate(parts, axis=0))
        product = jnp.dot(lhs, jnp.concatenate(right, axis=1), preferred_element_type=F32)
        for u, (p, r) in enumerate(pair):
            at = (first + p) * rows + r
            for e in range(min(block, rows - r)):
                part = product[32 * e : 32 * e + 32, u * EZ : (u + 1) * EZ]
                low = w_ref[(at + e) * 8 : (at + e + 2) * 8, :] * part[0:16]
                high = w_ref[(at + rows + e) * 8 : (at + rows + e + 2) * 8, :] * part[16:32]
                both = low + high
                found[p, r + e] = both[0:8] + both[8:16]
        store(blocks[i + 2] if i + 2 < len(blocks) else (count, 0))


def node_buffers(count):
    return [((count * 8, EZ), F32), ((count * 16, EZ), BF16), ((count * 16, EZ), BF16)]


def odd_place(axis):
    return lax.axis_index(axis) % 2 == 1


X_MESSAGE = 688
X_DENSITY, X_TOP, X_DOFS = 576, 672, 684


def third_rows():
    spare = [(48 * i + NY, 3 * i, 3) for i in range(12)]
    return spare + [(X_DENSITY + EY, 36, 4), (X_DENSITY + ROWS + EY, 40, 4)]


def pack_kernel(local_ref, top_ref, dens_ref, dofs_ref, even_ref, odd_ref, tops_ref, dofs_out_ref, l_ref, t_ref, d_ref, c_ref, sem):
    copies = []
    for side, node in ((0, EX - RADIUS), (1, 0)):
        for c in range(3):
            copies.append(pltpu.make_async_copy(local_ref.at[c, node : node + 4], l_ref.at[side, c], sem.at[len(copies)]))
    for source, dest in ((top_ref, t_ref), (dofs_ref, c_ref), (dens_ref, d_ref)):
        copies.append(pltpu.make_async_copy(source, dest, sem.at[len(copies)]))
    for copy in copies:
        copy.start()
    for out_ref in (even_ref, odd_ref):
        out_ref[X_TOP:X_MESSAGE, :] = jnp.zeros((X_MESSAGE - X_TOP, EZ), F32)
    clear(tops_ref)
    odd = odd_place("gx")
    outs = ((even_ref, odd), (odd_ref, jnp.logical_not(odd)))
    for copy in copies[:6]:
        copy.wait()
    for out_ref, flip in outs:
        side = flip.astype(jnp.int32)
        for c in range(3):
            for j in range(4):
                out_ref[(c * 4 + j) * ROWS : (c * 4 + j) * ROWS + NY, :] = l_ref[side, c, j]
    for copy in copies[6:]:
        copy.wait()
    for c in range(3):
        for i in range(NX):
            tops_ref[c, i : i + 1, 0:NY] = t_ref[c, i]
    for out_ref, flip in outs:
        for c in range(3):
            out_ref[X_TOP + 4 * c : X_TOP + 4 * c + 4, :] = jnp.where(
                flip, tops_ref[c, 0:4, :], tops_ref[c, EX - RADIUS : EX - RADIUS + 4, :])
        for j in range(3):
            value = jnp.where(flip, d_ref[pl.ds(j, EY, stride=EX), :], d_ref[pl.ds(EX - RADIUS + j, EY, stride=EX), :])
            if j < 2:
                out_ref[X_DENSITY + j * ROWS : X_DENSITY + j * ROWS + EY, :] = value
            else:
                for at, first, count in third_rows():
                    out_ref[at : at + count, :] = value[first : first + count]
        out_ref[X_DOFS : X_DOFS + 1, 0:8] = c_ref[...].astype(F32)
    dofs_out_ref[...] = jnp.broadcast_to(as_column(even_ref[X_DOFS : X_DOFS + 1, :]), (8, EZ))


def sort_sides(axis, even_ref, odd_ref, low_ref, high_ref):
    odd = odd_place(axis)
    even, other = even_ref[...], odd_ref[...]
    low_ref[...] = jnp.where(has_lower(axis), jnp.where(odd, even, other), 0.0)
    high_ref[...] = jnp.where(has_upper(axis), jnp.where(odd, other, even), 0.0)


def prepare_kernel(stiff_ref, dens_ref, lhs_ref, lhs_edge_ref, lhs_z_ref, od_ref, rs_ref, rd_ref):
    stiff = stiff_ref[...]
    lhs_ref[...] = stiffness_rows(stiff, 3, False)
    lhs_edge_ref[...] = stiffness_rows(stiff, 4, False)
    lhs_z_ref[...] = stiffness_rows(stiff, 4, True)
    base_x, base_y, base_z = lax.axis_index("gx") * EX, lax.axis_index("gy") * EY, lax.axis_index("gz") * EZ
    inside = iota((ROWS, EZ), 0) < EY
    norm_y = edge_total(EY, base_y + iota((ROWS, EZ), 0), lax.axis_size("gy"))
    norm_z = edge_total(EZ, base_z + iota((ROWS, EZ), 1), lax.axis_size("gz"))
    inverse = 1.0 / jnp.where(inside, norm_y * norm_z, 1.0)
    place = base_x + iota((8, EZ), 0)
    inverse_x = [1.0 / edge_total(EX, place + t, lax.axis_size("gx")) for t in (0, 8)]
    for x in range(EX):
        d = dens_ref[pl.ds(x, EY, stride=EX), :]
        od_ref[x, 0:EY, :] = d
        od_ref[x, EY:ROWS, :] = jnp.ones((ROWS - EY, EZ), F32)
        both = inverse * inverse_x[x // 8][x % 8 : x % 8 + 1, :]
        rd_ref[x] = both
        rs_ref[x] = both / od_ref[x]


def own_kernel(shared, local_ref, lhs_ref, dens_ref, coarse_ref, dofs_ref, own_ref, e_ref, up_ref, down_ref, *refs):
    corners = corner_values(coarse_ref, dofs_ref[:, 0:1], shared)
    for c in range(3):
        edges = corner_rows(corners, c)
        for i in range(NX):
            own_ref[c * NX + i, 0:NY, :] = local_ref[c, i] + plane_interp(edges, i, NY)
            own_ref[c * NX + i, NY:ROWS, :] = jnp.zeros((ROWS - NY, EZ), F32)
    for out_ref, first in ((up_ref, EY - RADIUS), (down_ref, 0)):
        out_ref[61 * 4 : OWN_SLOTS * 4, :] = jnp.zeros((4, EZ), F32)
        for slot in range(61):
            kind, c, p = SLOTS[slot]
            if kind == "node":
                out_ref[slot * 4 : slot * 4 + 4, :] = own_ref[c * NX + p - 3, first : first + 4, :]
            else:
                out_ref[slot * 4 : slot * 4 + 3, :] = dens_ref[c - 3, first : first + 3, :]
                out_ref[slot * 4 + 3 : slot * 4 + 4, :] = jnp.zeros((1, EZ), F32)
    build_nodes(lambda c, p: own_ref[c * NX + p + 1], range(OWN + 1), ROWS, refs)
    blocks = [(p, r) for p in range(OWN) for r in range(1, EY - 1, 3)]
    energy_planes(lhs_ref[...], 3, refs, e_ref, 0, OWN, ROWS, blocks, 0)


def clear(ref):
    ref[...] = jnp.zeros(ref.shape, ref.dtype)


def average(flag, low, high, own):
    return jnp.where(flag, 0.5 * low + 0.5 * high, own)


OWN_SLOTS = 62


def node_slot(c, p):
    if 4 <= p < 19:
        return c * 15 + p - 4
    return OWN_SLOTS + c * 8 + (p if p < 4 else p - 15)


def dens_slot(x):
    if 3 <= x < 19:
        return 45 + x - 3
    return OWN_SLOTS + 24 + (x if x < 3 else x - 16)


SLOTS = [None] * (OWN_SLOTS + 30)
for _x in range(XE):
    SLOTS[dens_slot(_x)] = ("density", _x, 0)
for _p in range(XN):
    for _c in range(3):
        SLOTS[node_slot(_c, _p)] = ("node", _c, _p)
TOP_AT = 4 * len(SLOTS)
Y_MESSAGE = TOP_AT + XR


def has_lower(axis):
    return lax.axis_index(axis) > 0


def has_upper(axis):
    return lax.axis_index(axis) < lax.axis_size(axis) - 1


def top_interp(corners, c, rows):
    rx = iota((rows, EZ), 0).astype(F32) * (1.0 / EX)
    ry = iota((rows, EZ), 1).astype(F32) * (1.0 / EY)
    value = [corners[c][k : k + 1] for k in range(8)]
    low = (1.0 - ry) * value[1] + ry * value[3]
    high = (1.0 - ry) * value[5] + ry * value[7]
    return (1.0 - rx) * low + rx * high


def x_sides(even_ref, odd_ref):
    odd = odd_place("gx")

    def low(at, count):
        return jnp.where(odd, even_ref[at : at + count, :], odd_ref[at : at + count, :])

    def high(at, count):
        return jnp.where(odd, odd_ref[at : at + count, :], even_ref[at : at + count, :])

    return low, high


def side_corners(shared, coarse_ref, sides):
    return [corner_values(coarse_ref, as_column(side(X_DOFS, 1)), shared) for side in sides]


def x_faces(own_ref, sides, corners, start, rows):
    lower, upper = has_lower("gx"), has_upper("gx")
    for c in range(3):
        edges = [corner_rows(corner, c) for corner in corners]
        for j in range(4):
            low, high = [
                side((c * 4 + j) * ROWS + start, rows) + plane_interp(edge, i, rows, start)
                for side, edge, i in zip(sides, edges, (EX - RADIUS + j, j))
            ]
            if j == 3:
                mine = own_ref[c * NX, start : start + rows, :]
                low = average(lower, low, mine, mine)
            if j == 0:
                mine = own_ref[c * NX + EX, start : start + rows, :]
                high = average(upper, mine, high, mine)
            yield c, j, low
            yield c, 19 + j, high


def halo_kernel(shared, own_ref, even_ref, odd_ref, coarse_ref, xl_ref, xh_ref, hd_ref):
    sides = x_sides(even_ref, odd_ref)
    for c, p, value in x_faces(own_ref, sides, side_corners(shared, coarse_ref, sides), 0, ROWS):
        if p < 4:
            xl_ref[c * 4 + p] = value
        else:
            xh_ref[c * 4 + p - 19] = value
    for first, side, there in zip((0, 3), sides, (has_lower("gx"), has_upper("gx"))):
        for j in range(2):
            hd_ref[first + j] = jnp.where(there, side(X_DENSITY + j * ROWS, ROWS), 0.0)
        hd_ref[first + 2, EY:ROWS, :] = jnp.zeros((ROWS - EY, EZ), F32)
        for at, row, count in third_rows():
            hd_ref[first + 2, row : row + count, :] = jnp.where(there, side(at, count), 0.0)


def x_kernel(shared, own_ref, up_own_ref, down_own_ref, top_ref, even_ref, odd_ref, coarse_ref, dofs_ref,
             tx_ref, yeven_ref, yodd_ref, up_ref, down_ref, t_ref):
    sides = low_rows, high_rows = x_sides(even_ref, odd_ref)
    corners = corner_values(coarse_ref, dofs_ref[:, 0:1], shared)
    corners_low, corners_high = side_corners(shared, coarse_ref, sides)
    lower, upper = has_lower("gx"), has_upper("gx")
    for out_ref, start, skip in ((up_ref, EY - 4, 1), (down_ref, 0, 0)):
        for c, p, value in x_faces(own_ref, sides, (corners_low, corners_high), start, 8):
            at = (node_slot(c, p) - OWN_SLOTS) * 4
            out_ref[at : at + 4, :] = value[skip : skip + 4]
        for x in (0, 1, 2, 19, 20, 21):
            j, side, there = (x, low_rows, lower) if x < 3 else (x - 19, high_rows, upper)
            row = start + skip
            if j < 2:
                value = side(X_DENSITY + j * ROWS + row, 3)
            else:
                value = side(NY if row == 0 else X_DENSITY + ROWS + EY + 1, 3)
            at = (dens_slot(x) - OWN_SLOTS) * 4
            out_ref[at : at + 3, :] = jnp.where(there, value, 0.0)
            out_ref[at + 3 : at + 4, :] = jnp.zeros((1, EZ), F32)

    t_ref[...] = jnp.zeros(t_ref.shape, F32)
    for c in range(3):
        t_ref[0] = top_ref[c] + top_interp(corners, c, XR)
        t_ref[1, 0:4, :] = low_rows(X_TOP + 4 * c, 4)
        t_ref[2, 0:4, :] = high_rows(X_TOP + 4 * c, 4)
        t_low = t_ref[1, 0:8, :] + pltpu.roll(top_interp(corners_low, c, 24), 24 - (EX - RADIUS), 0)[0:8]
        t_high = t_ref[2, 0:8, :] + top_interp(corners_high, c, 8)
        first = average(lower, t_low[3:4], t_ref[0, 0:1, :], t_ref[0, 0:1, :])
        last = average(upper, t_ref[0, EX : EX + 1, :], t_high[0:1], t_ref[0, EX : EX + 1, :])
        t_ref[3, 0:3, :] = t_low[0:3]
        t_ref[3, 3:4, :] = first
        t_ref[3, 4:19, :] = t_ref[0, 1:EX, :]
        t_ref[3, 19:20, :] = last
        t_ref[3, 20:23, :] = t_high[1:4]
        lane = iota((XR, EZ), 1)
        tx_ref[c] = jnp.where(lane < NY + 8, pltpu.roll(t_ref[3], 8, 1), 0.0)

    lane = iota((XR, EZ), 1)
    for out_ref, lane_at in ((up_ref, EY - RADIUS + 8), (down_ref, 8)):
        total = jnp.zeros((XR, EZ), F32)
        for c in range(3):
            moved = pltpu.roll(tx_ref[c], (4 * c - lane_at) % EZ, 1)
            total = jnp.where((lane >= 4 * c) & (lane < 4 * c + 4), moved, total)
        out_ref[TOP_AT - OWN_SLOTS * 4 :, :] = total
    odd = odd_place("gy")
    for mine, other, out_ref in ((up_own_ref, down_own_ref, yeven_ref), (down_own_ref, up_own_ref, yodd_ref)):
        out_ref[0 : OWN_SLOTS * 4, :] = jnp.where(odd, other[...], mine[...])
    for mine, other, out_ref in ((up_ref, down_ref, yeven_ref), (down_ref, up_ref, yodd_ref)):
        out_ref[OWN_SLOTS * 4 :, :] = jnp.where(odd, other[...], mine[...])


def side_kernel(own_ref, xl_ref, xh_ref, lhs_ref, e_ref, *refs):
    high = XE - 4 - OWN

    def plane(c, p):
        if p < 5:
            return x_plane(own_ref, xl_ref, xh_ref, c, p)
        return x_plane(own_ref, xl_ref, xh_ref, c, p - 5 + 4 + OWN)

    build_nodes(plane, range(5 + high + 1), ROWS, refs)
    for first, count, out_first in ((0, 4, 0), (5, high, 4)):
        blocks = [(p, r) for p in range(count) for r in range(1, EY - 1, 3)]
        energy_planes(lhs_ref[...], 3, refs, e_ref, first, count, ROWS, blocks, out_first)


Z_MESSAGE = 192


def x_plane(own_ref, xl_ref, xh_ref, c, p):
    if p < 4:
        return xl_ref[c * 4 + p]
    if p < 19:
        return own_ref[c * NX + p - 3]
    return xh_ref[c * 4 + p - 19]


def x_density(dens_ref, hd_ref, x, rows=EY):
    if x < 3:
        return hd_ref[x, 0:rows, :]
    if x < 19:
        return dens_ref[x - 3, 0:rows, :]
    return hd_ref[x - 16, 0:rows, :]


def end_planes(turned):
    return jnp.concatenate([turned[0:4], turned[EZ - 4 : EZ]], axis=0)


def turn_kernel(own_ref, xl_ref, xh_ref, dens_ref, hd_ref, z_ref):
    head = jnp.zeros((8, EZ), F32)

    def padded(slot):
        kind, c, p = SLOTS[slot] or SLOTS[0]
        if kind == "node":
            return [head, x_plane(own_ref, xl_ref, xh_ref, c, p), head]
        return [head, x_density(dens_ref, hd_ref, c, ROWS), head]

    lane = iota((8, EZ), 1)
    for slot in range(0, len(SLOTS), 2):
        both = end_planes(jnp.concatenate(padded(slot) + padded(slot + 1), axis=0).T)
        z_ref[slot] = jnp.where(lane < 64, both, 0.0)
        z_ref[slot + 1] = jnp.where(lane < 64, pltpu.roll(both, 64, 1), 0.0)


def y_kernel(tx_ref, zo_ref, eb_ref, even_ref, odd_ref,
             low_ref, high_ref, oa_ref, ob_ref, od_ref, *refs):
    del eb_ref
    z_ref, d_ref, up_ref, down_ref = refs[-4:]
    sort_sides("gy", even_ref, odd_ref, low_ref, high_ref)
    lower, upper = has_lower("gy"), has_upper("gy")
    clear(z_ref)
    clear(d_ref)
    lane = iota((8, EZ), 1)
    for first in range(0, len(SLOTS), 32):
        count = min(32, len(SLOTS) - first)
        turned = []
        for ref in (low_ref, high_ref):
            block = ref[first * 4 : (first + count) * 4, :]
            if count < 32:
                block = jnp.concatenate([block, jnp.zeros(((32 - count) * 4, EZ), F32)], axis=0)
            turned.append(end_planes(block.T))
        for t in range(count):
            if SLOTS[first + t] is None:
                continue
            kind, c, p = SLOTS[first + t]
            low = pltpu.roll(turned[0], (5 - 4 * t) % EZ, 1)
            high = pltpu.roll(turned[1], (52 - 4 * t) % EZ, 1)
            mine = zo_ref[first + t]
            value = jnp.where((lane >= 5) & (lane < 8), low, mine)
            if kind == "node":
                at = c * XR + p
                value = jnp.where((lane == 8) & lower, 0.5 * low + 0.5 * mine, value)
                value = jnp.where((lane == 52) & upper, 0.5 * mine + 0.5 * high, value)
                z_ref[at * 8 : at * 8 + 8, :] = jnp.where((lane > 52) & (lane < 56), high, value)
            else:
                d_ref[c * 8 : c * 8 + 8, :] = jnp.where((lane >= 52) & (lane < 55), high, value)

    lane = iota((XR, EZ), 1)
    tops = []
    for c in range(3):
        mine = tx_ref[c]
        low = pltpu.roll(low_ref[TOP_AT:Y_MESSAGE, :], (5 - 4 * c) % EZ, 1)
        high = pltpu.roll(high_ref[TOP_AT:Y_MESSAGE, :], (52 - 4 * c) % EZ, 1)
        value = jnp.where((lane >= 5) & (lane < 8), low, mine)
        value = jnp.where(lane == 8, average(lower, low, mine, mine), value)
        value = jnp.where(lane == 52, average(upper, mine, high, mine), value)
        tops.append(jnp.where((lane > 52) & (lane < 56), high, value))
    top = jnp.concatenate(tops, axis=0)

    def nodes(k):
        return z_ref[pl.ds(k, 3 * XR, stride=8), :]

    def dens(k):
        return d_ref[pl.ds(k, XR, stride=8), :]

    def pack(low, high):
        return low + pltpu.roll(high, 64, 1)

    oa_ref[...] = pack(nodes(0), top)
    ob_ref[...] = pack(nodes(1), nodes(7))
    od_ref[...] = pack(dens(0), dens(7))
    up_ref[0:72, :] = pack(nodes(5), nodes(6))
    up_ref[72:144, :] = pack(nodes(7), top)
    up_ref[144:168, :] = pack(dens(5), dens(6))
    up_ref[168:192, :] = dens(7)
    down_ref[0:72, :] = pack(nodes(0), nodes(1))
    down_ref[72:144, :] = pack(nodes(2), nodes(3))
    down_ref[144:168, :] = pack(dens(0), dens(1))
    down_ref[168:192, :] = dens(2)
    odd = odd_place("gz")
    refs[0][...] = jnp.where(odd, down_ref[...], up_ref[...])
    if len(refs) > 5:
        refs[1][...] = jnp.where(odd, up_ref[...], down_ref[...])


def edge_kernel(own_ref, xl_ref, xh_ref, lowy_ref, highy_ref, lhs_ref, el_ref, eh_ref, *refs):
    lower, upper = has_lower("gy"), has_upper("gy")
    row = iota((8, EZ), 0)

    def low(c, p):
        mine = pltpu.roll(x_plane(own_ref, xl_ref, xh_ref, c, p)[0:8], 3, 0)
        other = lowy_ref[node_slot(c, p) * 4 : node_slot(c, p) * 4 + 4, :]
        other = jnp.concatenate([other, other], axis=0)
        value = jnp.where(row == 3, average(lower, other, mine, mine), jnp.where(row < 3, other, mine))
        return jnp.where(row < 5, value, 0.0)

    def high(c, p):
        mine = pltpu.roll(x_plane(own_ref, xl_ref, xh_ref, c, p)[EY - 4 : EY + 4], 5, 0)
        other = highy_ref[node_slot(c, p) * 4 : node_slot(c, p) * 4 + 4, :]
        other = pltpu.roll(jnp.concatenate([other, other], axis=0), 1, 0)
        value = jnp.where(row == 1, average(upper, mine, other, mine), jnp.where(row < 1, mine, other))
        return jnp.where(row < 5, value, 0.0)

    for side, e_ref in ((low, el_ref), (high, eh_ref)):
        build_nodes(side, range(XN), 8, refs)
        energy_planes(lhs_ref[...], 4, refs, e_ref, 0, XE, 8, [(p, 0) for p in range(XE)], 0)


def triangle(value, axis):
    size = value.shape[axis]
    value = value + pltpu.roll(value, size - 1, axis)
    value = value + pltpu.roll(value, size - 2, axis)
    value = value + pltpu.roll(value, 1, axis)
    return value + pltpu.roll(value, 2, axis)


def weights(distance):
    return jnp.maximum(4 - jnp.abs(distance), 0).astype(F32)


def split_dot(value, right):
    rows = value.shape[0]
    product = jnp.dot(jnp.concatenate(halves(value), axis=0), right, preferred_element_type=F32)
    return product[0:rows] + product[rows:]


def edge_total(count, position, parts):
    total = None
    for offset in range(-RADIUS, RADIUS + 1):
        place = position + offset
        term = float(RADIUS + 1 - abs(offset)) * one_hot((place >= 0) & (place < count * parts))
        total = term if total is None else total + term
    return total


def field_kernel(ea_ref, eb_ref, el_ref, eh_ref, dens_ref, hd_ref, lowy_ref, highy_ref,
                 g_ref, along_ref, right_ref, f_ref):
    rows = iota((QROWS, EZ), 0)
    lanes = iota((QROWS, EZ), 1)
    ok = (rows >= 5) & (rows < 55) & (lanes > 0) & (lanes < EZ - 1)
    row = iota((8, EZ), 0)
    for x in range(XE):
        if x < 4:
            middle = eb_ref[x]
        elif x < 4 + OWN:
            middle = ea_ref[x - 4]
        else:
            middle = eb_ref[x - OWN]
        low = pltpu.roll(el_ref[x], 5, 0)
        high = pltpu.roll(eh_ref[x], 3, 0)
        start = jnp.where(row < 1, low, middle[0:8])
        end = jnp.where(row < 3, middle[40:48], high)
        energy = jnp.concatenate([low, start, middle[8:40], end], axis=0)
        at = dens_slot(x) * 4
        pad = jnp.zeros((5, EZ), F32)
        d = jnp.concatenate(
            [pad, lowy_ref[at : at + 3, :], x_density(dens_ref, hd_ref, x), highy_ref[at : at + 3, :], pad[0:1]], axis=0)
        f_ref[0, x] = jnp.where(ok, (SCALE * d) * d * d * energy, 0.0)
        f_ref[1, x] = jnp.where(ok, d, 0.0)

    for f in range(2):
        for t in range(QROWS // 8):
            at = slice(t * 8, t * 8 + 8)
            line = [f_ref[f, x, at, :] for x in range(XE)]
            for step in (1, 2, 1, 2):
                line = [line[i] + line[i + step] for i in range(len(line) - step)]
            for x in range(EX):
                f_ref[f, x, at, :] = line[x]
    k, col = iota((EZ, EZ), 0), iota((EZ, EZ), 1)
    along_ref[...] = jnp.where(k // 64 == col // 64, weights(k - col), 0.0).astype(BF16)
    j = (k % 64) // EX
    place = jnp.where(k < 64, j - 3, EZ - 1 + j)
    z = jnp.where(col % 8 < 4, EZ - 4 + col % 8, col % 8 - 4)
    right_ref[...] = jnp.where(k % EX == col // 8, weights(place - z), 0.0).astype(BF16)
    right = weights(k - col).astype(BF16)
    for f in range(2):
        for x in range(EX):
            g_ref[f, x] = split_dot(triangle(f_ref[f, x], 0)[8:QROWS], right)


def last_kernel(g_ref, along_ref, right_ref, rs_ref, rd_ref, oa_ref, ob_ref, od_ref, lhs_ref, *refs):
    messages, refs = refs[:-11], refs[-11:]
    outs, (ez_ref, c_ref, zl_ref, zh_ref, o_ref, sem), refs = refs[:2], refs[2:8], refs[8:]
    if len(messages) > 1:
        sort_sides("gz", *messages, zl_ref, zh_ref)
    else:
        odd = odd_place("gz")
        zl_ref[...] = jnp.where(odd, messages[0][...], 0.0)
        zh_ref[...] = jnp.where(odd, 0.0, messages[0][...])
    lower, upper = has_lower("gz"), has_upper("gz")

    def swap(value):
        return pltpu.roll(value, 64, 1)

    is_low = iota((3 * XR, EZ), 1) < 64
    oa, ob = oa_ref[...], ob_ref[...]
    zl0, zl1 = zl_ref[0:72, :], zl_ref[72:144, :]
    zh0, zh1 = zh_ref[0:72, :], zh_ref[72:144, :]
    nodes = (
        jnp.where(is_low, zl0, ob),
        jnp.where(is_low, swap(zl0), average(upper, oa, swap(zh0), oa)),
        jnp.where(is_low, zl1, zh0),
        jnp.where(is_low, average(lower, swap(zl1), oa, oa), swap(zh1)),
        jnp.where(is_low, ob, zh1),
    )
    build_nodes(lambda c, k: nodes[k][c * XR : (c + 1) * XR], range(5), XR, refs)
    for ref, step in zip(refs, (8, 16, 16)):
        ref[5 * XR * step : (5 * XR + 8) * step, :] = jnp.zeros((8 * step, EZ), ref.dtype)

    lane = iota((XR, EZ), 1)
    low_side = lane < 64
    od = od_ref[...]
    dl0, dl1 = zl_ref[144:168, :], zl_ref[168:192, :]
    dh0, dh1 = zh_ref[144:168, :], zh_ref[168:192, :]
    dens = (
        jnp.where(low_side, dl0, od),
        jnp.where(low_side, swap(dl0), swap(dh0)),
        jnp.where(low_side, dl1, dh0),
        jnp.where(low_side, od, swap(dh1)),
    )
    inside = (lane % 64 >= 5) & (lane % 64 < 55) & (iota((XR, EZ), 0) < XE)
    lanes = iota((16, EZ), 1)
    at_end = (lanes < 4) | (lanes >= EZ - 4)
    energy_planes(lhs_ref[...], 4, refs, ez_ref, 0, 4, XR, [(j, x) for j in range(4) for x in range(0, XR, 4)], 0)
    ends = []
    for f in range(2):
        for j in range(4):
            d = dens[j]
            value = d if f == 1 else (SCALE * d) * d * d * ez_ref[j]
            c_ref[f, j * EX : (j + 1) * EX, :] = triangle_forward(jnp.where(inside, value, 0.0))[0:EX]
        turned = split_dot(c_ref[f], along_ref[...])
        turned = jnp.concatenate([turned, jnp.zeros((EZ - 4 * EX, EZ), F32)], axis=0).T
        ends.append(split_dot(turned[8:56] + pltpu.roll(turned[72:120], 64, 1), right_ref[...]))
    copies = []
    for y in (0, 16, 32):
        count = min(16, EY - y)
        for f, inverse_ref in ((0, rs_ref), (1, rd_ref)):
            for x in range(EX):
                end = jnp.where(at_end, pltpu.roll(ends[f][y : y + 16], (EZ - 4 - 8 * x) % EZ, 1), 0.0)
                value = (g_ref[f, x, y : y + 16, :] + end) * inverse_ref[x, y : y + 16, :]
                o_ref[f, pl.ds(y * EX + x, count, stride=EX), :] = value[0:count]
            block = pl.ds(y * EX, count * EX)
            copies.append(pltpu.make_async_copy(o_ref.at[f, block], outs[f].at[block], sem.at[len(copies)]))
            copies[-1].start()
    for copy in copies:
        copy.wait()


def triangle_forward(value):
    size = value.shape[0]
    for step in (1, 2, 1, 2):
        value = value + pltpu.roll(value, size - step, 0)
    return value


def call(kernel, outs, ins, scratch=(), limit=16, micros=1.0, space=VM):
    return pl.pallas_call(
        kernel,
        out_shape=[jax.ShapeDtypeStruct(shape, dtype) for shape, dtype in outs],
        in_specs=[pl.BlockSpec(memory_space=space) for space in ins],
        out_specs=[pl.BlockSpec(memory_space=space)] * len(outs),
        scratch_shapes=[pltpu.VMEM(item[0], item[1]) if isinstance(item, tuple) else item for item in scratch],
        compiler_params=pltpu.CompilerParams(vmem_limit_bytes=limit * 2**20),
        cost_estimate=pl.CostEstimate(flops=0, bytes_accessed=int(micros * 3.6e6), transcendentals=0),
    )


def exchange(axis, spare, *values):
    count, others = lax.axis_size(axis), lax.axis_size(spare)
    names = tuple(sorted((axis, spare)))
    step, spare_step = (others, 1) if names[0] == axis else (1, count)
    results = []
    for first, value in enumerate(values):
        moves = []
        for i in range(count):
            j = i + 1 if i % 2 == first else i - 1
            for o in range(others):
                target = (j, o) if 0 <= j < count else (i, o ^ 1)
                moves.append((i * step + o * spare_step, target[0] * step + target[1] * spare_step))
        results.append(lax.ppermute(value, names, moves))
    return results


def local(local_solution, top_nodes, coarse_solution, corner_dofs, density, element_stiffness):
    dens = jnp.transpose(density, (1, 0, 2)).reshape(EY * EX, EZ)
    shared = lax.axis_size("gz") == 2
    if shared:
        other = lax.ppermute(coarse_solution, "gz", [(0, 1), (1, 0)])
        coarse = jnp.stack([coarse_solution, other])
    else:
        coarse = lax.all_gather(coarse_solution, "gz")

    message = ((X_MESSAGE, EZ), F32)
    even, odd, tops, dofs = call(
        pack_kernel,
        [message, message, ((3, XR, EZ), F32), ((8, EZ), F32)],
        [pltpu.HBM] * 4,
        [((2, 3, 4, NY, EZ), F32), ((3, NX, 1, NY), F32), ((EY * EX, EZ), F32), ((1, 8), jnp.int32), pltpu.SemaphoreType.DMA((9,))],
    )(*[
        pltpu.with_memory_space_constraint(value, pltpu.HBM)
        for value in (local_solution, jnp.transpose(top_nodes, (0, 1, 3, 2)), dens, corner_dofs.reshape(1, 8))
    ])
    even_x, odd_x = exchange("gx", "gy", even, odd)

    own_planes = ((EX, ROWS, EZ), F32)
    rows3, rows4 = ((96, block_rows(3)), BF16), ((128, block_rows(4)), BF16)
    lhs, lhs_edge, lhs_z, dens, inverse_sens, inverse_smooth = call(
        prepare_kernel, [rows3, rows4, rows4, own_planes, own_planes, own_planes], [VM, VM], micros=1.0
    )(element_stiffness, dens)

    own_part = ((OWN_SLOTS * 4, EZ), F32)
    own, ea, up_own, down_own = call(
        functools.partial(own_kernel, shared),
        [((3 * NX, ROWS, EZ), F32), ((OWN, ROWS, EZ), F32), own_part, own_part],
        [VM] * 5,
        node_buffers((OWN + 1) * ROWS),
        micros=6.0,
    )(local_solution, lhs, dens, coarse, dofs)

    face = ((12, ROWS, EZ), F32)
    y_message = ((Y_MESSAGE, EZ), F32)
    halo_part = ((Y_MESSAGE - OWN_SLOTS * 4, EZ), F32)
    tx, even, odd = call(
        functools.partial(x_kernel, shared),
        [((3, XR, EZ), F32), y_message, y_message],
        [VM] * 8,
        [halo_part, halo_part, ((4, XR, EZ), F32)],
        micros=1.0,
    )(own, up_own, down_own, tops, even_x, odd_x, coarse, dofs)
    even_y, odd_y = exchange("gy", "gz", even, odd)

    xl, xh, halo_dens = call(
        functools.partial(halo_kernel, shared), [face, face, ((6, ROWS, EZ), F32)], [VM] * 4, micros=0.7
    )(own, even_x, odd_x, coarse)
    (eb,) = call(
        side_kernel, [((XE - OWN, ROWS, EZ), F32)], [VM] * 4, node_buffers((XE - OWN + 2) * ROWS), micros=2.6
    )(own, xl, xh, lhs)

    (zo,) = call(turn_kernel, [((len(SLOTS), 8, EZ), F32)], [VM] * 5, micros=1.5)(own, xl, xh, dens, halo_dens)

    z_message = ((Z_MESSAGE, EZ), F32)
    low_y, high_y, oa, ob, od, *messages = call(
        y_kernel,
        [y_message, y_message, ((72, EZ), F32), ((72, EZ), F32), ((XR, EZ), F32)] + [z_message] * (1 if shared else 2),
        [VM] * 5,
        [((8 * 3 * XR, EZ), F32), ((8 * XR, EZ), F32), z_message, z_message],
        micros=1.0,
    )(tx, zo, eb, even_y, odd_y)
    received_z = exchange("gz", "gy", *messages)

    el, eh = call(
        edge_kernel,
        [((XE, 8, EZ), F32)] * 2,
        [VM] * 6,
        node_buffers(XN * 8),
        micros=2.3,
    )(own, xl, xh, low_y, high_y, lhs_edge)

    square = ((EZ, EZ), BF16)
    filtered, along_y, ends = call(
        field_kernel, [((2, EX, ROWS, EZ), F32), square, square], [VM] * 8, [((2, XE, QROWS, EZ), F32)], micros=1.5
    )(ea, eb, el, eh, dens, halo_dens, low_y, high_y)

    sens, smooth = call(
        last_kernel,
        [((EY * EX, EZ), F32)] * 2,
        [VM] * (9 + len(received_z)),
        [((4, XR, EZ), F32), ((2, 4 * EX, EZ), F32), z_message, z_message, ((2, EY * EX, EZ), F32),
         pltpu.SemaphoreType.DMA((6,))] + node_buffers(5 * XR + 8),
        space=pltpu.HBM,
        micros=2.5,
    )(filtered, along_y, ends, inverse_sens, inverse_smooth, oa, ob, od, lhs_z, *received_z)

    def grid(value):
        return jnp.transpose(value.reshape(EY, EX, EZ), (1, 0, 2))

    return grid(sens), grid(smooth)


def solution(mesh):
    in_specs = (
        P(None, "gx", "gy", "gz"),
        P(None, "gx", "gy", "gz"),
        P(None, "gz"),
        P("gx", "gy", "gz", None),
        P("gx", "gy", "gz"),
        P(),
    )
    out_specs = (P("gx", "gy", "gz"), P("gx", "gy", "gz"))
    return jax.shard_map(local, mesh=mesh, in_specs=in_specs, out_specs=out_specs, check_vma=False)
```

```python
import functools

import jax
import jax.numpy as jnp
from jax import lax
from jax.experimental import pallas as pl
from jax.experimental.pallas import tpu as pltpu
from jax.sharding import PartitionSpec as P

RADIUS = 3
F32 = jnp.float32
BF16 = jnp.bfloat16
SCALE = -3.0 / 96.0
HIGHEST = lax.Precision.HIGHEST
VM = pltpu.VMEM

EX, EY, EZ = 16, 44, 128
NX, NY = EX + 1, EY + 1
XN, XE = NX + 2 * RADIUS, EX + 2 * RADIUS
ROWS = 48
QROWS = 56
OWN = 12
XR = 24


def iota(shape, dim):
    return lax.broadcasted_iota(jnp.int32, shape, dim)


def one_hot(mask):
    return jnp.where(mask, 1.0, 0.0).astype(F32)


def halves(value):
    high = value.astype(BF16)
    return high, (value - high.astype(F32)).astype(BF16)


def as_column(row):
    lane, sub = iota((8, EZ), 1), iota((8, EZ), 0)
    return jnp.sum(jnp.where(lane == sub, row, 0.0), axis=1, keepdims=True)


def corner_values(coarse_ref, dofs, shared):
    parts, _, width = coarse_ref.shape
    dofs = dofs.astype(jnp.int32)
    own = lax.axis_index("gz")
    lane = iota((8, width), 1)
    totals = [0.0] * 3
    for part in range(parts):
        place = part if not shared else own if part == 0 else 1 - own
        found = lane + place * width == dofs
        for c in range(3):
            totals[c] = totals[c] + jnp.where(found, coarse_ref[part, c : c + 1, :], 0.0)
    return [jnp.broadcast_to(jnp.sum(total, axis=1, keepdims=True), (8, EZ)) for total in totals]


def corner_rows(corners, c):
    rz = iota((8, EZ), 1).astype(F32) * (1.0 / EZ)
    other = 1.0 - rz
    value = [corners[c][k : k + 1] for k in range(8)]
    return [[value[4 * kx + 2 * ky] * other + value[4 * kx + 2 * ky + 1] * rz for ky in (0, 1)] for kx in (0, 1)]


def plane_interp(edges, i, rows, start=0):
    wx = i / EX
    first, second = [((1.0 - wx) * edges[0][ky] + wx * edges[1][ky])[0:1] for ky in (0, 1)]
    ry = (start + iota((rows, EZ), 0)).astype(F32) * (1.0 / EY)
    return (1.0 - ry) * first + ry * second


def block_rows(block):
    nodes = block + 1
    return 2 * (16 * nodes + 16 * ((nodes + 1) // 2))


def stiffness_rows(stiff, block, in_lanes):
    def target(h, t, r):
        s, c = r // 4, r % 4
        place = 4 * t + 2 * s + h if in_lanes else 4 * h + 2 * t + s
        return jnp.where(c < 3, 8 * c + place, -1)

    row = iota((32, 24), 0)
    left = one_hot(iota((32, 24), 1) == target(row // 16, row // 8 % 2, row % 8))
    full = jnp.dot(left, stiff, precision=HIGHEST, preferred_element_type=F32)
    nodes, width = block + 1, block_rows(block)
    split = 32 * nodes
    half = (width - split) // 2
    col = iota((24, width), 1)
    again = col >= split
    h = jnp.where(again, (col - split) // half, col // (16 * nodes))
    node = jnp.where(again, (col - split) % half // 8, col % (16 * nodes) // 16)
    wide = iota((32, width), 1) >= split
    rows = []
    for e in range(block):
        t = node - e
        right = one_hot((iota((24, width), 0) == target(h, t, col % 8)) & (t >= 0) & (t < 2))
        part = jnp.dot(full, right, precision=HIGHEST, preferred_element_type=F32)
        high = part.astype(BF16).astype(F32)
        rows.append(jnp.where(wide, part - high, high))
    return jnp.concatenate(rows, axis=0).astype(BF16)


def build_nodes(plane_of, planes, rows, refs, first=0):
    w_ref, b_ref, h_ref = refs
    for p in planes:
        base = (first + p) * rows * 8
        zero = jnp.zeros((rows, EZ), F32)
        for c in range(3):
            value = plane_of(c, p)
            w_ref[pl.ds(base + c, rows, stride=8), :] = value
            w_ref[pl.ds(base + 4 + c, rows, stride=8), :] = pltpu.roll(value, EZ - 1, 1)
        w_ref[pl.ds(base + 3, rows, stride=8), :] = zero
        w_ref[pl.ds(base + 7, rows, stride=8), :] = zero

    def split(p, _):
        base = (first + p) * rows
        last = None
        for r in range(rows):
            value = w_ref[pl.ds(pl.multiple_of((base + r) * 8, 8), 8), :]
            high = value.astype(BF16).astype(F32)
            at = pl.ds(pl.multiple_of((base + r) * 16, 16), 16)
            b_ref[at, :] = jnp.concatenate([high, value - high], axis=0).astype(BF16)
            if last is not None:
                h_ref[pl.ds(pl.multiple_of((base + r - 1) * 16, 16), 16), :] = jnp.concatenate([last, high], axis=0).astype(BF16)
            last = high
        h_ref[at, :] = jnp.concatenate([last, last], axis=0).astype(BF16)
        return 0

    lax.fori_loop(0, len(planes), split, 0)


def sum_rows(values):
    row = iota((8, EZ), 0)
    for step in (1, 2, 4):
        first = row % (2 * step) < step
        values = [
            jnp.where(first, a, b) + pltpu.roll(jnp.where(first, b, a), step, 0)
            for a, b in zip(values[::2], values[1::2])
        ]
    return values[0]


def energy_planes(lhs, block, refs, e_ref, first, count, rows, blocks, out_first):
    w_ref, b_ref, h_ref = refs
    nodes = block + 1
    zero = jnp.zeros((8, EZ), F32)
    found, left = {}, {(p, t) for p in range(count) for t in range(0, rows, 8)}

    def store(before):
        for p, t in sorted(left):
            if (p, t + 7) < before:
                values = [found.pop((p, t + i), zero) for i in range(8)]
                e_ref[out_first + p, t : t + 8, :] = zero if all(v is zero for v in values) else sum_rows(values)
                left.remove((p, t))

    for i in range(0, len(blocks), 2):
        pair = blocks[i : i + 2]
        right = []
        for p, r in pair:
            at = (first + p) * rows + r
            parts = [b_ref[(at + far) * 16 : (at + far + nodes) * 16, :] for far in (0, rows)]
            for far in (0, rows):
                parts += [h_ref[(at + far + t) * 16 : (at + far + t + 1) * 16, :] for t in range(0, nodes, 2)]
            right.append(jnp.concatenate(parts, axis=0))
        product = jnp.dot(lhs, jnp.concatenate(right, axis=1), preferred_element_type=F32)
        for u, (p, r) in enumerate(pair):
            at = (first + p) * rows + r
            for e in range(min(block, rows - r)):
                part = product[32 * e : 32 * e + 32, u * EZ : (u + 1) * EZ]
                low = w_ref[(at + e) * 8 : (at + e + 2) * 8, :] * part[0:16]
                high = w_ref[(at + rows + e) * 8 : (at + rows + e + 2) * 8, :] * part[16:32]
                both = low + high
                found[p, r + e] = both[0:8] + both[8:16]
        store(blocks[i + 2] if i + 2 < len(blocks) else (count, 0))


def node_buffers(count):
    return [((count * 8, EZ), F32), ((count * 16, EZ), BF16), ((count * 16, EZ), BF16)]


def odd_place(axis):
    return lax.axis_index(axis) % 2 == 1


X_MESSAGE = 688
X_DENSITY, X_TOP, X_DOFS = 576, 672, 684


def third_rows():
    spare = [(48 * i + NY, 3 * i, 3) for i in range(12)]
    return spare + [(X_DENSITY + EY, 36, 4), (X_DENSITY + ROWS + EY, 40, 4)]


def pack_kernel(local_ref, top_ref, dens_ref, dofs_ref, even_ref, odd_ref, tops_ref, l_ref, t_ref, d_ref, c_ref, sem):
    copies = []
    for source, dest in ((top_ref, t_ref), (dofs_ref, c_ref), (dens_ref, d_ref)):
        copies.append(pltpu.make_async_copy(source, dest, sem.at[len(copies)]))
    for c in range(3):
        for side, node in ((0, EX - RADIUS), (1, 0)):
            copies.append(pltpu.make_async_copy(local_ref.at[c, node : node + 4], l_ref.at[side, c], sem.at[len(copies)]))
    for copy in copies:
        copy.start()
    for out_ref in (even_ref, odd_ref):
        out_ref[X_TOP:X_MESSAGE, :] = jnp.zeros((X_MESSAGE - X_TOP, EZ), F32)
    clear(tops_ref)
    flip = odd_place("gx")
    outs = ((even_ref, flip), (odd_ref, jnp.logical_not(flip)))
    for copy in copies[:3]:
        copy.wait()
    for c in range(3):
        for i in range(NX):
            tops_ref[c, i : i + 1, 0:NY] = t_ref[c, i]
    for out_ref, flip in outs:
        for c in range(3):
            out_ref[X_TOP + 4 * c : X_TOP + 4 * c + 4, :] = jnp.where(
                flip, tops_ref[c, 0:4, :], tops_ref[c, EX - RADIUS : EX - RADIUS + 4, :])
        for j in range(3):
            value = jnp.where(flip, d_ref[pl.ds(j, EY, stride=EX), :], d_ref[pl.ds(EX - RADIUS + j, EY, stride=EX), :])
            if j < 2:
                out_ref[X_DENSITY + j * ROWS : X_DENSITY + j * ROWS + EY, :] = value
            else:
                for at, first, count in third_rows():
                    out_ref[at : at + count, :] = value[first : first + count]
        out_ref[X_DOFS : X_DOFS + 1, 0:8] = c_ref[...].astype(F32)
    for c in range(3):
        for copy in copies[3 + 2 * c : 5 + 2 * c]:
            copy.wait()
        for out_ref, flip in outs:
            side = flip.astype(jnp.int32)
            for j in range(4):
                out_ref[(c * 4 + j) * ROWS : (c * 4 + j) * ROWS + NY, :] = l_ref[side, c, j]


def sort_sides(axis, even_ref, odd_ref, low_ref, high_ref):
    odd = odd_place(axis)
    even, other = even_ref[...], odd_ref[...]
    low_ref[...] = jnp.where(has_lower(axis), jnp.where(odd, even, other), 0.0)
    high_ref[...] = jnp.where(has_upper(axis), jnp.where(odd, other, even), 0.0)


def prepare_kernel(stiff_ref, dens_ref, dofs_in_ref, lhs_ref, lhs_edge_ref, lhs_z_ref, od_ref, rs_ref, rd_ref,
                   dofs_ref, along_ref, right_ref, row_ref):
    stiff = stiff_ref[...]
    clear(row_ref)
    row_ref[0:1, 0:8] = dofs_in_ref[...].astype(F32)
    dofs_ref[...] = jnp.broadcast_to(as_column(row_ref[0:1, :]), (8, EZ))
    k, col = iota((EZ, EZ), 0), iota((EZ, EZ), 1)
    along_ref[...] = jnp.where(k // 64 == col // 64, weights(k - col), 0.0).astype(BF16)
    j = (k % 64) // EX
    weight = weights(jnp.where(k < 64, j - 3, EZ - 1 + j) - col)
    for x in range(EX):
        part = jnp.where(k % EX == x, weight, 0.0).astype(BF16)
        right_ref[0:EZ, x * EZ : (x + 1) * EZ] = part
        right_ref[EZ : 2 * EZ, x * EZ : (x + 1) * EZ] = part
    lhs_ref[...] = stiffness_rows(stiff, 3, False)
    lhs_edge_ref[...] = stiffness_rows(stiff, 4, False)
    lhs_z_ref[...] = stiffness_rows(stiff, 4, True)
    base_x, base_y, base_z = lax.axis_index("gx") * EX, lax.axis_index("gy") * EY, lax.axis_index("gz") * EZ
    inside = iota((ROWS, EZ), 0) < EY
    norm_y = edge_total(EY, base_y + iota((ROWS, EZ), 0), lax.axis_size("gy"))
    norm_z = edge_total(EZ, base_z + iota((ROWS, EZ), 1), lax.axis_size("gz"))
    inverse = 1.0 / jnp.where(inside, norm_y * norm_z, 1.0)
    place = base_x + iota((8, EZ), 0)
    inverse_x = [1.0 / edge_total(EX, place + t, lax.axis_size("gx")) for t in (0, 8)]
    for x in range(EX):
        d = dens_ref[pl.ds(x, EY, stride=EX), :]
        od_ref[x, 0:EY, :] = d
        od_ref[x, EY:ROWS, :] = jnp.ones((ROWS - EY, EZ), F32)
        both = inverse * inverse_x[x // 8][x % 8 : x % 8 + 1, :]
        rd_ref[x] = both
        rs_ref[x] = both / od_ref[x]


def own_kernel(shared, local_ref, lhs_ref, dens_ref, coarse_ref, dofs_ref, own_ref, e_ref, up_ref, down_ref, *refs):
    corners = corner_values(coarse_ref, dofs_ref[:, 0:1], shared)
    for c in range(3):
        edges = corner_rows(corners, c)
        for i in range(NX):
            own_ref[c * NX + i, 0:NY, :] = local_ref[c, i] + plane_interp(edges, i, NY)
            own_ref[c * NX + i, NY:ROWS, :] = jnp.zeros((ROWS - NY, EZ), F32)
    for out_ref, first in ((up_ref, EY - RADIUS), (down_ref, 0)):
        out_ref[OWN_ROWS - 4 : OWN_ROWS, :] = jnp.zeros((4, EZ), F32)
        for p in range(4, 19):
            for c in range(3):
                at = node_row(c, p)
                out_ref[at : at + 4, :] = own_ref[c * NX + p - 3, first : first + 4, :]
        for x in range(3, 19):
            out_ref[dens_row(x) : dens_row(x) + 3, :] = dens_ref[x - 3, first : first + 3, :]
    build_nodes(lambda c, p: own_ref[c * NX + p + 1], range(OWN + 1), ROWS, refs)
    blocks = [(p, r) for p in range(OWN) for r in range(1, EY - 1, 3)]
    energy_planes(lhs_ref[...], 3, refs, e_ref, 0, OWN, ROWS, blocks, 0)


def clear(ref):
    ref[...] = jnp.zeros(ref.shape, ref.dtype)


def average(flag, low, high, own):
    return jnp.where(flag, 0.5 * low + 0.5 * high, own)


OWN_ROWS = 232
TOP_AT = 352
Y_MESSAGE = TOP_AT + 8


def node_row(c, p):
    if 4 <= p < 19:
        return 4 * (c * 15 + p - 4)
    return OWN_ROWS + 4 * (c * 8 + (p if p < 4 else p - 15))


def dens_row(x):
    if 3 <= x < 19:
        return 180 + 3 * (x - 3)
    return OWN_ROWS + 96 + 3 * (x if x < 3 else x - 16)


SLOTS = sorted(
    [("node", c, p) for c in range(3) for p in range(XN)] + [("density", x, x) for x in range(XE)],
    key=lambda slot: node_row(*slot[1:]) if slot[0] == "node" else dens_row(slot[1]),
)


def has_lower(axis):
    return lax.axis_index(axis) > 0


def has_upper(axis):
    return lax.axis_index(axis) < lax.axis_size(axis) - 1


def top_interp(corners, c, rows):
    rx = iota((rows, EZ), 0).astype(F32) * (1.0 / EX)
    ry = iota((rows, EZ), 1).astype(F32) * (1.0 / EY)
    value = [corners[c][k : k + 1] for k in range(8)]
    low = (1.0 - ry) * value[1] + ry * value[3]
    high = (1.0 - ry) * value[5] + ry * value[7]
    return (1.0 - rx) * low + rx * high


def x_sides(even_ref, odd_ref):
    flip = odd_place("gx")

    def low(at, count):
        return jnp.where(flip, even_ref[at : at + count, :], odd_ref[at : at + count, :])

    def high(at, count):
        return jnp.where(flip, odd_ref[at : at + count, :], even_ref[at : at + count, :])

    return low, high


def side_corners(shared, coarse_ref, sides):
    return [corner_values(coarse_ref, as_column(side(X_DOFS, 1)), shared) for side in sides]


def x_faces(own_ref, sides, corners, start, rows):
    lower, upper = has_lower("gx"), has_upper("gx")
    for c in range(3):
        edges = [corner_rows(corner, c) for corner in corners]
        for j in range(4):
            low, high = [
                side((c * 4 + j) * ROWS + start, rows) + plane_interp(edge, i, rows, start)
                for side, edge, i in zip(sides, edges, (EX - RADIUS + j, j))
            ]
            if j == 3:
                mine = own_ref[c * NX, start : start + rows, :]
                low = average(lower, low, mine, mine)
            if j == 0:
                mine = own_ref[c * NX + EX, start : start + rows, :]
                high = average(upper, mine, high, mine)
            yield c, j, low
            yield c, 19 + j, high


def halo_kernel(shared, own_ref, even_ref, odd_ref, coarse_ref, xl_ref, xh_ref, hd_ref):
    sides = x_sides(even_ref, odd_ref)
    for c, p, value in x_faces(own_ref, sides, side_corners(shared, coarse_ref, sides), 0, ROWS):
        if p < 4:
            xl_ref[c * 4 + p] = value
        else:
            xh_ref[c * 4 + p - 19] = value
    for first, side, there in zip((0, 3), sides, (has_lower("gx"), has_upper("gx"))):
        for j in range(2):
            hd_ref[first + j] = jnp.where(there, side(X_DENSITY + j * ROWS, ROWS), 0.0)
        hd_ref[first + 2, EY:ROWS, :] = jnp.zeros((ROWS - EY, EZ), F32)
        for at, row, count in third_rows():
            hd_ref[first + 2, row : row + count, :] = jnp.where(there, side(at, count), 0.0)


def x_kernel(shared, own_ref, up_own_ref, down_own_ref, top_ref, even_ref, odd_ref, coarse_ref, dofs_ref,
             tx_ref, yeven_ref, yodd_ref, up_ref, down_ref, t_ref):
    sides = low_rows, high_rows = x_sides(even_ref, odd_ref)
    corners = corner_values(coarse_ref, dofs_ref[:, 0:1], shared)
    corners_low, corners_high = side_corners(shared, coarse_ref, sides)
    lower, upper = has_lower("gx"), has_upper("gx")
    for out_ref, start, skip in ((up_ref, EY - 4, 1), (down_ref, 0, 0)):
        for c, p, value in x_faces(own_ref, sides, (corners_low, corners_high), start, 8):
            at = node_row(c, p) - OWN_ROWS
            out_ref[at : at + 4, :] = value[skip : skip + 4]
        for x in (0, 1, 2, 19, 20, 21):
            j, side, there = (x, low_rows, lower) if x < 3 else (x - 19, high_rows, upper)
            row = start + skip
            if j < 2:
                value = side(X_DENSITY + j * ROWS + row, 3)
            else:
                value = side(NY if row == 0 else X_DENSITY + ROWS + EY + 1, 3)
            at = dens_row(x) - OWN_ROWS
            out_ref[at : at + 3, :] = jnp.where(there, value, 0.0)
        out_ref[TOP_AT - 6 - OWN_ROWS : TOP_AT - OWN_ROWS, :] = jnp.zeros((6, EZ), F32)

    t_ref[...] = jnp.zeros(t_ref.shape, F32)
    for c in range(3):
        t_ref[0] = top_ref[c] + top_interp(corners, c, XR)
        t_ref[1, 0:4, :] = low_rows(X_TOP + 4 * c, 4)
        t_ref[2, 0:4, :] = high_rows(X_TOP + 4 * c, 4)
        t_low = t_ref[1, 0:8, :] + pltpu.roll(top_interp(corners_low, c, 24), 24 - (EX - RADIUS), 0)[0:8]
        t_high = t_ref[2, 0:8, :] + top_interp(corners_high, c, 8)
        first = average(lower, t_low[3:4], t_ref[0, 0:1, :], t_ref[0, 0:1, :])
        last = average(upper, t_ref[0, EX : EX + 1, :], t_high[0:1], t_ref[0, EX : EX + 1, :])
        t_ref[3, 0:3, :] = t_low[0:3]
        t_ref[3, 3:4, :] = first
        t_ref[3, 4:19, :] = t_ref[0, 1:EX, :]
        t_ref[3, 19:20, :] = last
        t_ref[3, 20:23, :] = t_high[1:4]
        lane = iota((XR, EZ), 1)
        tx_ref[c] = jnp.where(lane < NY + 8, pltpu.roll(t_ref[3], 8, 1), 0.0)

    lane = iota((XR, EZ), 1)
    for out_ref, lane_at in ((up_ref, EY - RADIUS + 8), (down_ref, 8)):
        total = jnp.zeros((XR, EZ), F32)
        for c in range(3):
            moved = pltpu.roll(tx_ref[c], (4 * c - lane_at) % EZ, 1)
            total = jnp.where((lane >= 4 * c) & (lane < 4 * c + 4), moved, total)
        out_ref[TOP_AT - OWN_ROWS :, :] = total[0:8] + pltpu.roll(total[8:16], 16, 1) + pltpu.roll(total[16:24], 32, 1)
    odd = odd_place("gy")
    for mine, other, out_ref in ((up_own_ref, down_own_ref, yeven_ref), (down_own_ref, up_own_ref, yodd_ref)):
        out_ref[0:OWN_ROWS, :] = jnp.where(odd, other[...], mine[...])
    for mine, other, out_ref in ((up_ref, down_ref, yeven_ref), (down_ref, up_ref, yodd_ref)):
        out_ref[OWN_ROWS:, :] = jnp.where(odd, other[...], mine[...])


def side_kernel(own_ref, xl_ref, xh_ref, lhs_ref, e_ref, *refs):
    high = XE - 4 - OWN

    def plane(c, p):
        if p < 5:
            return x_plane(own_ref, xl_ref, xh_ref, c, p)
        return x_plane(own_ref, xl_ref, xh_ref, c, p - 5 + 4 + OWN)

    build_nodes(plane, range(5 + high + 1), ROWS, refs)
    for first, count, out_first in ((0, 4, 0), (5, high, 4)):
        blocks = [(p, r) for p in range(count) for r in range(1, EY - 1, 3)]
        energy_planes(lhs_ref[...], 3, refs, e_ref, first, count, ROWS, blocks, out_first)


Z_MESSAGE = 184


def x_plane(own_ref, xl_ref, xh_ref, c, p):
    if p < 4:
        return xl_ref[c * 4 + p]
    if p < 19:
        return own_ref[c * NX + p - 3]
    return xh_ref[c * 4 + p - 19]


def x_density(dens_ref, hd_ref, x, rows=EY):
    if x < 3:
        return hd_ref[x, 0:rows, :]
    if x < 19:
        return dens_ref[x - 3, 0:rows, :]
    return hd_ref[x - 16, 0:rows, :]


def end_planes(turned):
    return jnp.concatenate([turned[0:4], turned[EZ - 4 : EZ]], axis=0)


def turn_kernel(own_ref, xl_ref, xh_ref, dens_ref, hd_ref, z_ref):
    head = jnp.zeros((8, EZ), F32)

    def padded(slot):
        kind, c, p = SLOTS[min(slot, len(SLOTS) - 1)]
        if kind == "node":
            return [head, x_plane(own_ref, xl_ref, xh_ref, c, p), head]
        return [head, x_density(dens_ref, hd_ref, c, ROWS), head]

    lane = iota((8, EZ), 1)
    for slot in range(0, len(SLOTS), 2):
        both = end_planes(jnp.concatenate(padded(slot) + padded(slot + 1), axis=0).T)
        z_ref[slot] = jnp.where(lane < 64, both, 0.0)
        if slot + 1 < len(SLOTS):
            z_ref[slot + 1] = jnp.where(lane < 64, pltpu.roll(both, 64, 1), 0.0)


def y_kernel(tx_ref, zo_ref, eb_ref, even_ref, odd_ref,
             low_ref, high_ref, oa_ref, ob_ref, od_ref, *refs):
    del eb_ref
    z_ref, d_ref, up_ref, down_ref = refs[-4:]
    sort_sides("gy", even_ref, odd_ref, low_ref, high_ref)
    lower, upper = has_lower("gy"), has_upper("gy")
    clear(z_ref)
    clear(d_ref)
    lane = iota((8, EZ), 1)
    turned = []
    for first in range(0, TOP_AT, EZ):
        turned.append([])
        for ref in (low_ref, high_ref):
            block = ref[first : min(first + EZ, TOP_AT), :]
            if block.shape[0] < EZ:
                block = jnp.concatenate([block, jnp.zeros((EZ - block.shape[0], EZ), F32)], axis=0)
            turned[-1].append(end_planes(block.T))
    for slot, (kind, c, p) in enumerate(SLOTS):
        at = node_row(c, p) if kind == "node" else dens_row(c)
        low = pltpu.roll(turned[at // EZ][0], (5 - at) % EZ, 1)
        high = pltpu.roll(turned[at // EZ][1], (52 - at) % EZ, 1)
        mine = zo_ref[slot]
        value = jnp.where((lane >= 5) & (lane < 8), low, mine)
        if kind == "node":
            at = c * XR + p
            value = jnp.where((lane == 8) & lower, 0.5 * low + 0.5 * mine, value)
            value = jnp.where((lane == 52) & upper, 0.5 * mine + 0.5 * high, value)
            z_ref[at * 8 : at * 8 + 8, :] = jnp.where((lane > 52) & (lane < 56), high, value)
        else:
            d_ref[c * 8 : c * 8 + 8, :] = jnp.where((lane >= 52) & (lane < 55), high, value)

    lane = iota((XR, EZ), 1)
    tops = []
    for c in range(3):
        mine = tx_ref[c]
        low, high = [
            jnp.concatenate([pltpu.roll(ref[TOP_AT:Y_MESSAGE, :], (to - 4 * c - 16 * g) % EZ, 1) for g in range(3)], axis=0)
            for ref, to in ((low_ref, 5), (high_ref, 52))
        ]
        value = jnp.where((lane >= 5) & (lane < 8), low, mine)
        value = jnp.where(lane == 8, average(lower, low, mine, mine), value)
        value = jnp.where(lane == 52, average(upper, mine, high, mine), value)
        tops.append(jnp.where((lane > 52) & (lane < 56), high, value))
    top = jnp.concatenate(tops, axis=0)

    def nodes(k):
        return z_ref[pl.ds(k, 3 * XR, stride=8), :]

    def dens(k):
        return d_ref[pl.ds(k, XR, stride=8), :]

    def pack(low, high):
        return low + pltpu.roll(high, 64, 1)

    def fold(value):
        return jnp.concatenate([pack(value[0:8], value[8:16]), value[16:24]], axis=0)

    oa_ref[...] = pack(nodes(0), top)
    ob_ref[...] = pack(nodes(1), nodes(7))
    od_ref[...] = pack(dens(0), dens(7))
    up_ref[0:72, :] = pack(nodes(5), nodes(6))
    up_ref[72:144, :] = pack(nodes(7), top)
    up_ref[144:168, :] = pack(dens(5), dens(6))
    up_ref[168:184, :] = fold(dens(7))
    down_ref[0:72, :] = pack(nodes(0), nodes(1))
    down_ref[72:144, :] = pack(nodes(2), nodes(3))
    down_ref[144:168, :] = pack(dens(0), dens(1))
    down_ref[168:184, :] = fold(dens(2))
    odd = odd_place("gz")
    refs[0][...] = jnp.where(odd, down_ref[...], up_ref[...])
    if len(refs) > 5:
        refs[1][...] = jnp.where(odd, up_ref[...], down_ref[...])


def edge_kernel(own_ref, xl_ref, xh_ref, lowy_ref, highy_ref, lhs_ref, el_ref, eh_ref, *refs):
    lower, upper = has_lower("gy"), has_upper("gy")
    row = iota((8, EZ), 0)

    def low(c, p):
        mine = pltpu.roll(x_plane(own_ref, xl_ref, xh_ref, c, p)[0:8], 3, 0)
        other = lowy_ref[node_row(c, p) : node_row(c, p) + 4, :]
        other = jnp.concatenate([other, other], axis=0)
        value = jnp.where(row == 3, average(lower, other, mine, mine), jnp.where(row < 3, other, mine))
        return jnp.where(row < 5, value, 0.0)

    def high(c, p):
        mine = pltpu.roll(x_plane(own_ref, xl_ref, xh_ref, c, p)[EY - 4 : EY + 4], 5, 0)
        other = highy_ref[node_row(c, p) : node_row(c, p) + 4, :]
        other = pltpu.roll(jnp.concatenate([other, other], axis=0), 1, 0)
        value = jnp.where(row == 1, average(upper, mine, other, mine), jnp.where(row < 1, mine, other))
        return jnp.where(row < 5, value, 0.0)

    for side, e_ref in ((low, el_ref), (high, eh_ref)):
        build_nodes(side, range(XN), 8, refs)
        energy_planes(lhs_ref[...], 4, refs, e_ref, 0, XE, 8, [(p, 0) for p in range(XE)], 0)


def triangle(value, axis):
    size = value.shape[axis]
    value = value + pltpu.roll(value, size - 1, axis)
    value = value + pltpu.roll(value, size - 2, axis)
    value = value + pltpu.roll(value, 1, axis)
    return value + pltpu.roll(value, 2, axis)


def weights(distance):
    return jnp.maximum(4 - jnp.abs(distance), 0).astype(F32)


def split_dot(value, right):
    rows = value.shape[0]
    product = jnp.dot(jnp.concatenate(halves(value), axis=0), right, preferred_element_type=F32)
    return product[0:rows] + product[rows:]


def edge_total(count, position, parts):
    total = None
    for offset in range(-RADIUS, RADIUS + 1):
        place = position + offset
        term = float(RADIUS + 1 - abs(offset)) * one_hot((place >= 0) & (place < count * parts))
        total = term if total is None else total + term
    return total


def field_kernel(ea_ref, eb_ref, el_ref, eh_ref, dens_ref, hd_ref, lowy_ref, highy_ref, g_ref, f_ref):
    rows = iota((QROWS, EZ), 0)
    lanes = iota((QROWS, EZ), 1)
    ok = (rows >= 5) & (rows < 55) & (lanes > 0) & (lanes < EZ - 1)
    row = iota((8, EZ), 0)
    for x in range(XE):
        if x < 4:
            middle = eb_ref[x]
        elif x < 4 + OWN:
            middle = ea_ref[x - 4]
        else:
            middle = eb_ref[x - OWN]
        low = pltpu.roll(el_ref[x], 5, 0)
        high = pltpu.roll(eh_ref[x], 3, 0)
        start = jnp.where(row < 1, low, middle[0:8])
        end = jnp.where(row < 3, middle[40:48], high)
        energy = jnp.concatenate([low, start, middle[8:40], end], axis=0)
        at = dens_row(x)
        pad = jnp.zeros((5, EZ), F32)
        d = jnp.concatenate(
            [pad, lowy_ref[at : at + 3, :], x_density(dens_ref, hd_ref, x), highy_ref[at : at + 3, :], pad[0:1]], axis=0)
        f_ref[0, x] = jnp.where(ok, (SCALE * d) * d * d * energy, 0.0)
        f_ref[1, x] = jnp.where(ok, d, 0.0)

    for f in range(2):
        for t in range(QROWS // 8):
            at = slice(t * 8, t * 8 + 8)
            line = [f_ref[f, x, at, :] for x in range(XE)]
            for step in (1, 2, 1, 2):
                line = [line[i] + line[i + step] for i in range(len(line) - step)]
            for x in range(EX):
                f_ref[f, x, at, :] = line[x]
    k, col = iota((EZ, EZ), 0), iota((EZ, EZ), 1)
    right = weights(k - col).astype(BF16)
    for f in range(2):
        for x in range(EX):
            g_ref[f, x] = split_dot(triangle(f_ref[f, x], 0)[8:QROWS], right)


def last_kernel(g_ref, along_ref, right_ref, rs_ref, rd_ref, oa_ref, ob_ref, od_ref, lhs_ref, *refs):
    messages, refs = refs[:-12], refs[-12:]
    outs, (ez_ref, c_ref, zl_ref, zh_ref, e_ref, o_ref, sem), refs = refs[:2], refs[2:9], refs[9:]
    if len(messages) > 1:
        sort_sides("gz", *messages, zl_ref, zh_ref)
    else:
        odd = odd_place("gz")
        zl_ref[...] = jnp.where(odd, messages[0][...], 0.0)
        zh_ref[...] = jnp.where(odd, 0.0, messages[0][...])
    lower, upper = has_lower("gz"), has_upper("gz")

    def swap(value):
        return pltpu.roll(value, 64, 1)

    is_low = iota((3 * XR, EZ), 1) < 64
    oa, ob = oa_ref[...], ob_ref[...]
    zl0, zl1 = zl_ref[0:72, :], zl_ref[72:144, :]
    zh0, zh1 = zh_ref[0:72, :], zh_ref[72:144, :]
    nodes = (
        jnp.where(is_low, zl0, ob),
        jnp.where(is_low, swap(zl0), average(upper, oa, swap(zh0), oa)),
        jnp.where(is_low, zl1, zh0),
        jnp.where(is_low, average(lower, swap(zl1), oa, oa), swap(zh1)),
        jnp.where(is_low, ob, zh1),
    )
    build_nodes(lambda c, k: nodes[k][c * XR : (c + 1) * XR], range(5), XR, refs)
    for ref, step in zip(refs, (8, 16, 16)):
        ref[5 * XR * step : (5 * XR + 8) * step, :] = jnp.zeros((8 * step, EZ), ref.dtype)

    lane = iota((XR, EZ), 1)
    low_side = lane < 64
    od = od_ref[...]
    dl0, dh0 = zl_ref[144:168, :], zh_ref[144:168, :]
    dl1, dh1 = [
        jnp.concatenate([ref[168:176, :], swap(ref[168:176, :]), ref[176:184, :]], axis=0) for ref in (zl_ref, zh_ref)
    ]
    dens = (
        jnp.where(low_side, dl0, od),
        jnp.where(low_side, swap(dl0), swap(dh0)),
        jnp.where(low_side, dl1, dh0),
        jnp.where(low_side, od, swap(dh1)),
    )
    inside = (lane % 64 >= 5) & (lane % 64 < 55) & (iota((XR, EZ), 0) < XE)
    energy_planes(lhs_ref[...], 4, refs, ez_ref, 0, 4, XR, [(j, x) for j in range(4) for x in range(0, XR, 4)], 0)
    parts = []
    for f in range(2):
        for j in range(4):
            d = dens[j]
            value = d if f == 1 else (SCALE * d) * d * d * ez_ref[j]
            c_ref[f, j * EX : (j + 1) * EX, :] = triangle_forward(jnp.where(inside, value, 0.0))[0:EX]
        turned = split_dot(c_ref[f], along_ref[...])
        turned = jnp.concatenate([turned, jnp.zeros((EZ - 4 * EX, EZ), F32)], axis=0).T
        parts.append(jnp.concatenate(halves(turned[8:56] + pltpu.roll(turned[72:120], 64, 1)), axis=1))
    both = jnp.concatenate(parts, axis=0)
    for x in range(0, EX, 2):
        e_ref[:, x * EZ : (x + 2) * EZ] = jnp.dot(both, right_ref[:, x * EZ : (x + 2) * EZ], preferred_element_type=F32)
    copies = []
    for y in (0, 16, 32):
        count = min(16, EY - y)
        for f, inverse_ref in ((0, rs_ref), (1, rd_ref)):
            for x in range(EX):
                end = e_ref[f * ROWS + y : f * ROWS + y + 16, x * EZ : (x + 1) * EZ]
                value = (g_ref[f, x, y : y + 16, :] + end) * inverse_ref[x, y : y + 16, :]
                o_ref[f, pl.ds(y * EX + x, count, stride=EX), :] = value[0:count]
            block = pl.ds(y * EX, count * EX)
            copies.append(pltpu.make_async_copy(o_ref.at[f, block], outs[f].at[block], sem.at[len(copies)]))
            copies[-1].start()
    for copy in copies:
        copy.wait()


def triangle_forward(value):
    size = value.shape[0]
    for step in (1, 2, 1, 2):
        value = value + pltpu.roll(value, size - step, 0)
    return value


def call(kernel, outs, ins, scratch=(), limit=16, micros=1.0, space=VM):
    return pl.pallas_call(
        kernel,
        out_shape=[jax.ShapeDtypeStruct(shape, dtype) for shape, dtype in outs],
        in_specs=[pl.BlockSpec(memory_space=space) for space in ins],
        out_specs=[pl.BlockSpec(memory_space=space)] * len(outs),
        scratch_shapes=[pltpu.VMEM(item[0], item[1]) if isinstance(item, tuple) else item for item in scratch],
        compiler_params=pltpu.CompilerParams(vmem_limit_bytes=limit * 2**20),
        cost_estimate=pl.CostEstimate(flops=0, bytes_accessed=int(micros * 3.6e6), transcendentals=0),
    )


def exchange(axis, spare, *values):
    count, others = lax.axis_size(axis), lax.axis_size(spare)
    names = tuple(sorted((axis, spare)))
    step, spare_step = (others, 1) if names[0] == axis else (1, count)
    results = []
    for first, value in enumerate(values):
        moves = []
        for i in range(count):
            j = i + 1 if i % 2 == first else i - 1
            for o in range(others):
                target = (j, o) if 0 <= j < count else (i, o ^ 1)
                moves.append((i * step + o * spare_step, target[0] * step + target[1] * spare_step))
        results.append(lax.ppermute(value, names, moves))
    return results


def local(local_solution, top_nodes, coarse_solution, corner_dofs, density, element_stiffness):
    dens = jnp.transpose(density, (1, 0, 2)).reshape(EY * EX, EZ)
    shared = lax.axis_size("gz") == 2
    if shared:
        other = lax.ppermute(coarse_solution, "gz", [(0, 1), (1, 0)])
        coarse = jnp.stack([coarse_solution, other])
    else:
        coarse = lax.all_gather(coarse_solution, "gz")

    message = ((X_MESSAGE, EZ), F32)
    even, odd, tops = call(
        pack_kernel,
        [message, message, ((3, XR, EZ), F32)],
        [pltpu.HBM] * 4,
        [((2, 3, 4, NY, EZ), F32), ((3, NX, 1, NY), F32), ((EY * EX, EZ), F32), ((1, 8), jnp.int32), pltpu.SemaphoreType.DMA((9,))],
    )(*[
        pltpu.with_memory_space_constraint(value, pltpu.HBM)
        for value in (local_solution, jnp.transpose(top_nodes, (0, 1, 3, 2)), dens, corner_dofs.reshape(1, 8))
    ])
    even_x, odd_x = exchange("gx", "gy", even, odd)

    own_planes = ((EX, ROWS, EZ), F32)
    rows3, rows4 = ((96, block_rows(3)), BF16), ((128, block_rows(4)), BF16)
    lhs, lhs_edge, lhs_z, dens, inverse_sens, inverse_smooth, dofs, along_y, ends = call(
        prepare_kernel,
        [rows3, rows4, rows4, own_planes, own_planes, own_planes, ((8, EZ), F32), ((EZ, EZ), BF16), ((2 * EZ, EX * EZ), BF16)],
        [VM] * 3,
        [((8, EZ), F32)],
        micros=1.0,
    )(element_stiffness, dens, corner_dofs.reshape(1, 8))

    own_part = ((OWN_ROWS, EZ), F32)
    own, ea, up_own, down_own = call(
        functools.partial(own_kernel, shared),
        [((3 * NX, ROWS, EZ), F32), ((OWN, ROWS, EZ), F32), own_part, own_part],
        [VM] * 5,
        node_buffers((OWN + 1) * ROWS),
        micros=6.0,
    )(local_solution, lhs, dens, coarse, dofs)

    face = ((12, ROWS, EZ), F32)
    y_message = ((Y_MESSAGE, EZ), F32)
    halo_part = ((Y_MESSAGE - OWN_ROWS, EZ), F32)
    tx, even, odd = call(
        functools.partial(x_kernel, shared),
        [((3, XR, EZ), F32), y_message, y_message],
        [VM] * 8,
        [halo_part, halo_part, ((4, XR, EZ), F32)],
        micros=1.0,
    )(own, up_own, down_own, tops, even_x, odd_x, coarse, dofs)
    even_y, odd_y = exchange("gy", "gz", even, odd)

    xl, xh, halo_dens = call(
        functools.partial(halo_kernel, shared), [face, face, ((6, ROWS, EZ), F32)], [VM] * 4, micros=0.7
    )(own, even_x, odd_x, coarse)
    (eb,) = call(
        side_kernel, [((XE - OWN, ROWS, EZ), F32)], [VM] * 4, node_buffers((XE - OWN + 2) * ROWS), micros=2.6
    )(own, xl, xh, lhs)

    (zo,) = call(turn_kernel, [((len(SLOTS), 8, EZ), F32)], [VM] * 5, micros=1.5)(own, xl, xh, dens, halo_dens)

    z_message = ((Z_MESSAGE, EZ), F32)
    low_y, high_y, oa, ob, od, *messages = call(
        y_kernel,
        [y_message, y_message, ((72, EZ), F32), ((72, EZ), F32), ((XR, EZ), F32)] + [z_message] * (1 if shared else 2),
        [VM] * 5,
        [((8 * 3 * XR, EZ), F32), ((8 * XR, EZ), F32), z_message, z_message],
        micros=1.0,
    )(tx, zo, eb, even_y, odd_y)
    received_z = exchange("gz", "gy", *messages)

    el, eh = call(
        edge_kernel,
        [((XE, 8, EZ), F32)] * 2,
        [VM] * 6,
        node_buffers(XN * 8),
        micros=2.3,
    )(own, xl, xh, low_y, high_y, lhs_edge)

    (filtered,) = call(
        field_kernel, [((2, EX, ROWS, EZ), F32)], [VM] * 8, [((2, XE, QROWS, EZ), F32)], micros=1.5
    )(ea, eb, el, eh, dens, halo_dens, low_y, high_y)

    sens, smooth = call(
        last_kernel,
        [((EY * EX, EZ), F32)] * 2,
        [VM] * (9 + len(received_z)),
        [((4, XR, EZ), F32), ((2, 4 * EX, EZ), F32), z_message, z_message, ((2 * ROWS, EX * EZ), F32), ((2, EY * EX, EZ), F32),
         pltpu.SemaphoreType.DMA((6,))] + node_buffers(5 * XR + 8),
        space=pltpu.HBM,
        micros=2.5,
    )(filtered, along_y, ends, inverse_sens, inverse_smooth, oa, ob, od, lhs_z, *received_z)

    def grid(value):
        return jnp.transpose(value.reshape(EY, EX, EZ), (1, 0, 2))

    return grid(sens), grid(smooth)


def solution(mesh):
    in_specs = (
        P(None, "gx", "gy", "gz"),
        P(None, "gx", "gy", "gz"),
        P(None, "gz"),
        P("gx", "gy", "gz", None),
        P("gx", "gy", "gz"),
        P(),
    )
    out_specs = (P("gx", "gy", "gz"), P("gx", "gy", "gz"))
    return jax.shard_map(local, mesh=mesh, in_specs=in_specs, out_specs=out_specs, check_vma=False)
```

```python
import functools

import jax
import jax.numpy as jnp
from jax import lax
from jax.experimental import pallas as pl
from jax.experimental.pallas import tpu as pltpu
from jax.sharding import PartitionSpec as P

RADIUS = 3
F32 = jnp.float32
BF16 = jnp.bfloat16
SCALE = -3.0 / 96.0
HIGHEST = lax.Precision.HIGHEST
VM = pltpu.VMEM

EX, EY, EZ = 16, 44, 128
NX, NY = EX + 1, EY + 1
XN, XE = NX + 2 * RADIUS, EX + 2 * RADIUS
ROWS = 48
QROWS = 56
OWN = 12
XR = 24


def iota(shape, dim):
    return lax.broadcasted_iota(jnp.int32, shape, dim)


def one_hot(mask):
    return jnp.where(mask, 1.0, 0.0).astype(F32)


def halves(value):
    high = value.astype(BF16)
    return high, (value - high.astype(F32)).astype(BF16)


def as_column(row):
    lane, sub = iota((8, EZ), 1), iota((8, EZ), 0)
    return jnp.sum(jnp.where(lane == sub, row, 0.0), axis=1, keepdims=True)


def corner_values(coarse_ref, dofs, shared):
    parts, _, width = coarse_ref.shape
    dofs = dofs.astype(jnp.int32)
    own = lax.axis_index("gz")
    lane = iota((8, width), 1)
    totals = [0.0] * 3
    for part in range(parts):
        place = part if not shared else own if part == 0 else 1 - own
        found = lane + place * width == dofs
        for c in range(3):
            totals[c] = totals[c] + jnp.where(found, coarse_ref[part, c : c + 1, :], 0.0)
    return [jnp.broadcast_to(jnp.sum(total, axis=1, keepdims=True), (8, EZ)) for total in totals]


def corner_rows(corners, c):
    rz = iota((8, EZ), 1).astype(F32) * (1.0 / EZ)
    other = 1.0 - rz
    value = [corners[c][k : k + 1] for k in range(8)]
    return [[value[4 * kx + 2 * ky] * other + value[4 * kx + 2 * ky + 1] * rz for ky in (0, 1)] for kx in (0, 1)]


def plane_interp(edges, i, rows, start=0):
    wx = i / EX
    first, second = [((1.0 - wx) * edges[0][ky] + wx * edges[1][ky])[0:1] for ky in (0, 1)]
    ry = (start + iota((rows, EZ), 0)).astype(F32) * (1.0 / EY)
    return (1.0 - ry) * first + ry * second


def block_rows(block):
    nodes = block + 1
    return 2 * (16 * nodes + 16 * ((nodes + 1) // 2))


def stiffness_rows(stiff, block, in_lanes):
    def target(h, t, r):
        s, c = r // 4, r % 4
        place = 4 * t + 2 * s + h if in_lanes else 4 * h + 2 * t + s
        return jnp.where(c < 3, 8 * c + place, -1)

    row = iota((32, 24), 0)
    left = one_hot(iota((32, 24), 1) == target(row // 16, row // 8 % 2, row % 8))
    full = jnp.dot(left, stiff, precision=HIGHEST, preferred_element_type=F32)
    nodes, width = block + 1, block_rows(block)
    split = 32 * nodes
    half = (width - split) // 2
    col = iota((24, width), 1)
    again = col >= split
    h = jnp.where(again, (col - split) // half, col // (16 * nodes))
    node = jnp.where(again, (col - split) % half // 8, col % (16 * nodes) // 16)
    wide = iota((32, width), 1) >= split
    rows = []
    for e in range(block):
        t = node - e
        right = one_hot((iota((24, width), 0) == target(h, t, col % 8)) & (t >= 0) & (t < 2))
        part = jnp.dot(full, right, precision=HIGHEST, preferred_element_type=F32)
        high = part.astype(BF16).astype(F32)
        rows.append(jnp.where(wide, part - high, high))
    return jnp.concatenate(rows, axis=0).astype(BF16)


def build_nodes(plane_of, planes, rows, refs, first=0):
    w_ref, b_ref, h_ref = refs
    for p in planes:
        base = (first + p) * rows * 8
        zero = jnp.zeros((rows, EZ), F32)
        for c in range(3):
            value = plane_of(c, p)
            w_ref[pl.ds(base + c, rows, stride=8), :] = value
            w_ref[pl.ds(base + 4 + c, rows, stride=8), :] = pltpu.roll(value, EZ - 1, 1)
        w_ref[pl.ds(base + 3, rows, stride=8), :] = zero
        w_ref[pl.ds(base + 7, rows, stride=8), :] = zero

    def split(p, _):
        base = (first + p) * rows
        last = None
        for r in range(rows):
            value = w_ref[pl.ds(pl.multiple_of((base + r) * 8, 8), 8), :]
            high = value.astype(BF16).astype(F32)
            at = pl.ds(pl.multiple_of((base + r) * 16, 16), 16)
            b_ref[at, :] = jnp.concatenate([high, value - high], axis=0).astype(BF16)
            if last is not None:
                h_ref[pl.ds(pl.multiple_of((base + r - 1) * 16, 16), 16), :] = jnp.concatenate([last, high], axis=0).astype(BF16)
            last = high
        h_ref[at, :] = jnp.concatenate([last, last], axis=0).astype(BF16)
        return 0

    lax.fori_loop(0, len(planes), split, 0)


def sum_rows(values):
    row = iota((8, EZ), 0)
    for step in (1, 2, 4):
        first = row % (2 * step) < step
        values = [
            jnp.where(first, a, b) + pltpu.roll(jnp.where(first, b, a), step, 0)
            for a, b in zip(values[::2], values[1::2])
        ]
    return values[0]


def energy_planes(lhs, block, refs, e_ref, first, count, rows, blocks, out_first):
    w_ref, b_ref, h_ref = refs
    nodes = block + 1
    zero = jnp.zeros((8, EZ), F32)
    found, left = {}, {(p, t) for p in range(count) for t in range(0, rows, 8)}

    def store(before):
        for p, t in sorted(left):
            if (p, t + 7) < before:
                values = [found.pop((p, t + i), zero) for i in range(8)]
                e_ref[out_first + p, t : t + 8, :] = zero if all(v is zero for v in values) else sum_rows(values)
                left.remove((p, t))

    for i in range(0, len(blocks), 2):
        pair = blocks[i : i + 2]
        right = []
        for p, r in pair:
            at = (first + p) * rows + r
            parts = [b_ref[(at + far) * 16 : (at + far + nodes) * 16, :] for far in (0, rows)]
            for far in (0, rows):
                parts += [h_ref[(at + far + t) * 16 : (at + far + t + 1) * 16, :] for t in range(0, nodes, 2)]
            right.append(jnp.concatenate(parts, axis=0))
        product = jnp.dot(lhs, jnp.concatenate(right, axis=1), preferred_element_type=F32)
        for u, (p, r) in enumerate(pair):
            at = (first + p) * rows + r
            for e in range(min(block, rows - r)):
                part = product[32 * e : 32 * e + 32, u * EZ : (u + 1) * EZ]
                low = w_ref[(at + e) * 8 : (at + e + 2) * 8, :] * part[0:16]
                high = w_ref[(at + rows + e) * 8 : (at + rows + e + 2) * 8, :] * part[16:32]
                both = low + high
                found[p, r + e] = both[0:8] + both[8:16]
        store(blocks[i + 2] if i + 2 < len(blocks) else (count, 0))


def node_buffers(count):
    return [((count * 8, EZ), F32), ((count * 16, EZ), BF16), ((count * 16, EZ), BF16)]


def odd_place(axis):
    return lax.axis_index(axis) % 2 == 1


X_MESSAGE = 680
X_DENSITY, X_TOP, X_DOFS = 576, 672, 678


def third_rows():
    spare = [(48 * i + NY, 3 * i, 3) for i in range(12)]
    return spare + [(X_DENSITY + EY, 36, 4), (X_DENSITY + ROWS + EY, 40, 4)]


def pack_kernel(local_ref, top_ref, dens_ref, dofs_ref, even_ref, odd_ref, tops_ref, l_ref, t_ref, d_ref, c_ref, sem):
    copies = []
    for source, dest in ((top_ref, t_ref), (dofs_ref, c_ref), (dens_ref, d_ref)):
        copies.append(pltpu.make_async_copy(source, dest, sem.at[len(copies)]))
    for c in range(3):
        for side, node in ((0, EX - RADIUS), (1, 0)):
            copies.append(pltpu.make_async_copy(local_ref.at[c, node : node + 4], l_ref.at[side, c], sem.at[len(copies)]))
    for copy in copies:
        copy.start()
    for out_ref in (even_ref, odd_ref):
        out_ref[X_TOP:X_MESSAGE, :] = jnp.zeros((X_MESSAGE - X_TOP, EZ), F32)
    clear(tops_ref)
    flip = odd_place("gx")
    outs = ((even_ref, flip), (odd_ref, jnp.logical_not(flip)))
    for copy in copies[:3]:
        copy.wait()
    for c in range(3):
        for i in range(NX):
            tops_ref[c, i : i + 1, 0:NY] = t_ref[c, i]
    for out_ref, flip in outs:
        faces = [jnp.where(flip, tops_ref[c, 0:4, :], tops_ref[c, EX - RADIUS : EX - RADIUS + 4, :]) for c in range(3)]
        faces = jnp.concatenate(faces, axis=0)
        out_ref[X_TOP : X_TOP + 6, :] = faces[0:6] + pltpu.roll(faces[6:12], 64, 1)
        for j in range(3):
            value = jnp.where(flip, d_ref[pl.ds(j, EY, stride=EX), :], d_ref[pl.ds(EX - RADIUS + j, EY, stride=EX), :])
            if j < 2:
                out_ref[X_DENSITY + j * ROWS : X_DENSITY + j * ROWS + EY, :] = value
            else:
                for at, first, count in third_rows():
                    out_ref[at : at + count, :] = value[first : first + count]
        out_ref[X_DOFS : X_DOFS + 1, 0:8] = c_ref[...].astype(F32)
    for c in range(3):
        for copy in copies[3 + 2 * c : 5 + 2 * c]:
            copy.wait()
        for out_ref, flip in outs:
            side = flip.astype(jnp.int32)
            for j in range(4):
                out_ref[(c * 4 + j) * ROWS : (c * 4 + j) * ROWS + NY, :] = l_ref[side, c, j]


def sort_sides(axis, even_ref, odd_ref, low_ref, high_ref):
    odd = odd_place(axis)
    even, other = even_ref[...], odd_ref[...]
    low_ref[...] = jnp.where(has_lower(axis), jnp.where(odd, even, other), 0.0)
    high_ref[...] = jnp.where(has_upper(axis), jnp.where(odd, other, even), 0.0)


def prepare_kernel(stiff_ref, dens_ref, dofs_in_ref, lhs_ref, lhs_edge_ref, lhs_z_ref, od_ref, rs_ref, rd_ref,
                   dofs_ref, along_ref, right_ref, row_ref):
    stiff = stiff_ref[...]
    clear(row_ref)
    row_ref[0:1, 0:8] = dofs_in_ref[...].astype(F32)
    dofs_ref[...] = jnp.broadcast_to(as_column(row_ref[0:1, :]), (8, EZ))
    k, col = iota((EZ, EZ), 0), iota((EZ, EZ), 1)
    along_ref[...] = jnp.where(k // 64 == col // 64, weights(k - col), 0.0).astype(BF16)
    j = (k % 64) // EX
    weight = weights(jnp.where(k < 64, j - 3, EZ - 1 + j) - col)
    for x in range(EX):
        part = jnp.where(k % EX == x, weight, 0.0).astype(BF16)
        right_ref[0:EZ, x * EZ : (x + 1) * EZ] = part
        right_ref[EZ : 2 * EZ, x * EZ : (x + 1) * EZ] = part
    lhs_ref[...] = stiffness_rows(stiff, 3, False)
    lhs_edge_ref[...] = stiffness_rows(stiff, 4, False)
    lhs_z_ref[...] = stiffness_rows(stiff, 4, True)
    base_x, base_y, base_z = lax.axis_index("gx") * EX, lax.axis_index("gy") * EY, lax.axis_index("gz") * EZ
    inside = iota((ROWS, EZ), 0) < EY
    norm_y = edge_total(EY, base_y + iota((ROWS, EZ), 0), lax.axis_size("gy"))
    norm_z = edge_total(EZ, base_z + iota((ROWS, EZ), 1), lax.axis_size("gz"))
    inverse = 1.0 / jnp.where(inside, norm_y * norm_z, 1.0)
    place = base_x + iota((8, EZ), 0)
    inverse_x = [1.0 / edge_total(EX, place + t, lax.axis_size("gx")) for t in (0, 8)]
    for x in range(EX):
        d = dens_ref[pl.ds(x, EY, stride=EX), :]
        od_ref[x, 0:EY, :] = d
        od_ref[x, EY:ROWS, :] = jnp.ones((ROWS - EY, EZ), F32)
        both = inverse * inverse_x[x // 8][x % 8 : x % 8 + 1, :]
        rd_ref[x] = both
        rs_ref[x] = both / od_ref[x]


def own_kernel(shared, local_ref, lhs_ref, dens_ref, coarse_ref, dofs_ref, own_ref, e_ref, even_ref, odd_ref, *refs):
    corners = corner_values(coarse_ref, dofs_ref[:, 0:1], shared)
    for c in range(3):
        edges = corner_rows(corners, c)
        for i in range(NX):
            own_ref[c * NX + i, 0:NY, :] = local_ref[c, i] + plane_interp(edges, i, NY)
            own_ref[c * NX + i, NY:ROWS, :] = jnp.zeros((ROWS - NY, EZ), F32)
    odd = odd_place("gy")
    for out_ref, first, second in ((even_ref, EY - RADIUS, 0), (odd_ref, 0, EY - RADIUS)):
        out_ref[OWN_ROWS - 4 : OWN_ROWS, :] = jnp.zeros((4, EZ), F32)
        for p in range(4, 19):
            for c in range(3):
                at = node_row(c, p)
                plane = own_ref[c * NX + p - 3]
                out_ref[at : at + 4, :] = jnp.where(odd, plane[second : second + 4], plane[first : first + 4])
        for x in range(3, 19):
            plane = dens_ref[x - 3]
            out_ref[dens_row(x) : dens_row(x) + 3, :] = jnp.where(odd, plane[second : second + 3], plane[first : first + 3])
    build_nodes(lambda c, p: own_ref[c * NX + p + 1], range(OWN + 1), ROWS, refs)
    blocks = [(p, r) for p in range(OWN) for r in range(1, EY - 1, 3)]
    energy_planes(lhs_ref[...], 3, refs, e_ref, 0, OWN, ROWS, blocks, 0)


def clear(ref):
    ref[...] = jnp.zeros(ref.shape, ref.dtype)


def average(flag, low, high, own):
    return jnp.where(flag, 0.5 * low + 0.5 * high, own)


OWN_ROWS = 232
TOP_AT = 352
Y_MESSAGE = TOP_AT + 8


def node_row(c, p):
    if 4 <= p < 19:
        return 4 * (c * 15 + p - 4)
    return OWN_ROWS + 4 * (c * 8 + (p if p < 4 else p - 15))


def dens_row(x):
    if 3 <= x < 19:
        return 180 + 3 * (x - 3)
    return OWN_ROWS + 96 + 3 * (x if x < 3 else x - 16)


SLOTS = sorted(
    [("node", c, p) for c in range(3) for p in range(XN)] + [("density", x, x) for x in range(XE)],
    key=lambda slot: node_row(*slot[1:]) if slot[0] == "node" else dens_row(slot[1]),
)


def has_lower(axis):
    return lax.axis_index(axis) > 0


def has_upper(axis):
    return lax.axis_index(axis) < lax.axis_size(axis) - 1


def top_interp(corners, c, rows):
    rx = iota((rows, EZ), 0).astype(F32) * (1.0 / EX)
    ry = iota((rows, EZ), 1).astype(F32) * (1.0 / EY)
    value = [corners[c][k : k + 1] for k in range(8)]
    low = (1.0 - ry) * value[1] + ry * value[3]
    high = (1.0 - ry) * value[5] + ry * value[7]
    return (1.0 - rx) * low + rx * high


def x_sides(even_ref, odd_ref):
    flip = odd_place("gx")

    def low(at, count):
        return jnp.where(flip, even_ref[at : at + count, :], odd_ref[at : at + count, :])

    def high(at, count):
        return jnp.where(flip, odd_ref[at : at + count, :], even_ref[at : at + count, :])

    return low, high


def side_corners(shared, coarse_ref, sides):
    return [corner_values(coarse_ref, as_column(side(X_DOFS, 1)), shared) for side in sides]


def x_faces(own_ref, sides, corners, start, rows):
    lower, upper = has_lower("gx"), has_upper("gx")
    for c in range(3):
        edges = [corner_rows(corner, c) for corner in corners]
        for j in range(4):
            low, high = [
                side((c * 4 + j) * ROWS + start, rows) + plane_interp(edge, i, rows, start)
                for side, edge, i in zip(sides, edges, (EX - RADIUS + j, j))
            ]
            if j == 3:
                mine = own_ref[c * NX, start : start + rows, :]
                low = average(lower, low, mine, mine)
            if j == 0:
                mine = own_ref[c * NX + EX, start : start + rows, :]
                high = average(upper, mine, high, mine)
            yield c, j, low
            yield c, 19 + j, high


def halo_kernel(shared, own_ref, even_ref, odd_ref, coarse_ref, xl_ref, xh_ref, hd_ref):
    sides = x_sides(even_ref, odd_ref)
    for c, p, value in x_faces(own_ref, sides, side_corners(shared, coarse_ref, sides), 0, ROWS):
        if p < 4:
            xl_ref[c * 4 + p] = value
        else:
            xh_ref[c * 4 + p - 19] = value
    for first, side, there in zip((0, 3), sides, (has_lower("gx"), has_upper("gx"))):
        for j in range(2):
            hd_ref[first + j] = jnp.where(there, side(X_DENSITY + j * ROWS, ROWS), 0.0)
        hd_ref[first + 2, EY:ROWS, :] = jnp.zeros((ROWS - EY, EZ), F32)
        for at, row, count in third_rows():
            hd_ref[first + 2, row : row + count, :] = jnp.where(there, side(at, count), 0.0)


def x_kernel(shared, own_ref, even_own_ref, odd_own_ref, top_ref, even_ref, odd_ref, coarse_ref, dofs_ref,
             tx_ref, yeven_ref, yodd_ref, up_ref, down_ref, t_ref):
    sides = low_rows, high_rows = x_sides(even_ref, odd_ref)
    corners = corner_values(coarse_ref, dofs_ref[:, 0:1], shared)
    corners_low, corners_high = side_corners(shared, coarse_ref, sides)
    lower, upper = has_lower("gx"), has_upper("gx")
    for out_ref, start, skip in ((up_ref, EY - 4, 1), (down_ref, 0, 0)):
        for c, p, value in x_faces(own_ref, sides, (corners_low, corners_high), start, 8):
            at = node_row(c, p) - OWN_ROWS
            out_ref[at : at + 4, :] = value[skip : skip + 4]
        for x in (0, 1, 2, 19, 20, 21):
            j, side, there = (x, low_rows, lower) if x < 3 else (x - 19, high_rows, upper)
            row = start + skip
            if j < 2:
                value = side(X_DENSITY + j * ROWS + row, 3)
            else:
                value = side(NY if row == 0 else X_DENSITY + ROWS + EY + 1, 3)
            at = dens_row(x) - OWN_ROWS
            out_ref[at : at + 3, :] = jnp.where(there, value, 0.0)
        out_ref[TOP_AT - 6 - OWN_ROWS : TOP_AT - OWN_ROWS, :] = jnp.zeros((6, EZ), F32)

    t_ref[...] = jnp.zeros(t_ref.shape, F32)
    for c in range(3):
        t_ref[0] = top_ref[c] + top_interp(corners, c, XR)
        for side, side_rows in ((1, low_rows), (2, high_rows)):
            both = side_rows(X_TOP, 6)
            both = jnp.concatenate([both, pltpu.roll(both, 64, 1)], axis=0)
            t_ref[side, 0:4, :] = both[4 * c : 4 * c + 4]
        t_low = t_ref[1, 0:8, :] + pltpu.roll(top_interp(corners_low, c, 24), 24 - (EX - RADIUS), 0)[0:8]
        t_high = t_ref[2, 0:8, :] + top_interp(corners_high, c, 8)
        first = average(lower, t_low[3:4], t_ref[0, 0:1, :], t_ref[0, 0:1, :])
        last = average(upper, t_ref[0, EX : EX + 1, :], t_high[0:1], t_ref[0, EX : EX + 1, :])
        t_ref[3, 0:3, :] = t_low[0:3]
        t_ref[3, 3:4, :] = first
        t_ref[3, 4:19, :] = t_ref[0, 1:EX, :]
        t_ref[3, 19:20, :] = last
        t_ref[3, 20:23, :] = t_high[1:4]
        lane = iota((XR, EZ), 1)
        tx_ref[c] = jnp.where(lane < NY + 8, pltpu.roll(t_ref[3], 8, 1), 0.0)

    lane = iota((XR, EZ), 1)
    for out_ref, lane_at in ((up_ref, EY - RADIUS + 8), (down_ref, 8)):
        total = jnp.zeros((XR, EZ), F32)
        for c in range(3):
            moved = pltpu.roll(tx_ref[c], (4 * c - lane_at) % EZ, 1)
            total = jnp.where((lane >= 4 * c) & (lane < 4 * c + 4), moved, total)
        out_ref[TOP_AT - OWN_ROWS :, :] = total[0:8] + pltpu.roll(total[8:16], 16, 1) + pltpu.roll(total[16:24], 32, 1)
    odd = odd_place("gy")
    yeven_ref[0:OWN_ROWS, :] = even_own_ref[...]
    yodd_ref[0:OWN_ROWS, :] = odd_own_ref[...]
    for mine, other, out_ref in ((up_ref, down_ref, yeven_ref), (down_ref, up_ref, yodd_ref)):
        out_ref[OWN_ROWS:, :] = jnp.where(odd, other[...], mine[...])


def side_kernel(own_ref, xl_ref, xh_ref, lhs_ref, e_ref, *refs):
    high = XE - 4 - OWN

    def plane(c, p):
        if p < 5:
            return x_plane(own_ref, xl_ref, xh_ref, c, p)
        return x_plane(own_ref, xl_ref, xh_ref, c, p - 5 + 4 + OWN)

    build_nodes(plane, range(5 + high + 1), ROWS, refs)
    for first, count, out_first in ((0, 4, 0), (5, high, 4)):
        blocks = [(p, r) for p in range(count) for r in range(1, EY - 1, 3)]
        energy_planes(lhs_ref[...], 3, refs, e_ref, first, count, ROWS, blocks, out_first)


Z_MESSAGE = 184


def x_plane(own_ref, xl_ref, xh_ref, c, p):
    if p < 4:
        return xl_ref[c * 4 + p]
    if p < 19:
        return own_ref[c * NX + p - 3]
    return xh_ref[c * 4 + p - 19]


def x_density(dens_ref, hd_ref, x, rows=EY):
    if x < 3:
        return hd_ref[x, 0:rows, :]
    if x < 19:
        return dens_ref[x - 3, 0:rows, :]
    return hd_ref[x - 16, 0:rows, :]


def end_planes(turned):
    return jnp.concatenate([turned[0:4], turned[EZ - 4 : EZ]], axis=0)


def turn_kernel(own_ref, xl_ref, xh_ref, dens_ref, hd_ref, z_ref):
    head = jnp.zeros((8, EZ), F32)

    def padded(slot):
        kind, c, p = SLOTS[min(slot, len(SLOTS) - 1)]
        if kind == "node":
            return [head, x_plane(own_ref, xl_ref, xh_ref, c, p), head]
        return [head, x_density(dens_ref, hd_ref, c, ROWS), head]

    lane = iota((8, EZ), 1)
    for slot in range(0, len(SLOTS), 2):
        both = end_planes(jnp.concatenate(padded(slot) + padded(slot + 1), axis=0).T)
        z_ref[slot] = jnp.where(lane < 64, both, 0.0)
        if slot + 1 < len(SLOTS):
            z_ref[slot + 1] = jnp.where(lane < 64, pltpu.roll(both, 64, 1), 0.0)


def y_kernel(tx_ref, zo_ref, eb_ref, even_ref, odd_ref,
             low_ref, high_ref, oa_ref, ob_ref, od_ref, *refs):
    del eb_ref
    z_ref, d_ref, up_ref, down_ref = refs[-4:]
    sort_sides("gy", even_ref, odd_ref, low_ref, high_ref)
    lower, upper = has_lower("gy"), has_upper("gy")
    clear(z_ref)
    clear(d_ref)
    lane = iota((8, EZ), 1)
    turned = []
    for first in range(0, TOP_AT, EZ):
        turned.append([])
        for ref in (low_ref, high_ref):
            block = ref[first : min(first + EZ, TOP_AT), :]
            if block.shape[0] < EZ:
                block = jnp.concatenate([block, jnp.zeros((EZ - block.shape[0], EZ), F32)], axis=0)
            turned[-1].append(end_planes(block.T))
    for slot, (kind, c, p) in enumerate(SLOTS):
        at = node_row(c, p) if kind == "node" else dens_row(c)
        low = pltpu.roll(turned[at // EZ][0], (5 - at) % EZ, 1)
        high = pltpu.roll(turned[at // EZ][1], (52 - at) % EZ, 1)
        mine = zo_ref[slot]
        value = jnp.where((lane >= 5) & (lane < 8), low, mine)
        if kind == "node":
            at = c * XR + p
            value = jnp.where((lane == 8) & lower, 0.5 * low + 0.5 * mine, value)
            value = jnp.where((lane == 52) & upper, 0.5 * mine + 0.5 * high, value)
            z_ref[at * 8 : at * 8 + 8, :] = jnp.where((lane > 52) & (lane < 56), high, value)
        else:
            d_ref[c * 8 : c * 8 + 8, :] = jnp.where((lane >= 52) & (lane < 55), high, value)

    lane = iota((XR, EZ), 1)
    tops = []
    for c in range(3):
        mine = tx_ref[c]
        low, high = [
            jnp.concatenate([pltpu.roll(ref[TOP_AT:Y_MESSAGE, :], (to - 4 * c - 16 * g) % EZ, 1) for g in range(3)], axis=0)
            for ref, to in ((low_ref, 5), (high_ref, 52))
        ]
        value = jnp.where((lane >= 5) & (lane < 8), low, mine)
        value = jnp.where(lane == 8, average(lower, low, mine, mine), value)
        value = jnp.where(lane == 52, average(upper, mine, high, mine), value)
        tops.append(jnp.where((lane > 52) & (lane < 56), high, value))
    top = jnp.concatenate(tops, axis=0)

    def nodes(k):
        return z_ref[pl.ds(k, 3 * XR, stride=8), :]

    def dens(k):
        return d_ref[pl.ds(k, XR, stride=8), :]

    def pack(low, high):
        return low + pltpu.roll(high, 64, 1)

    def fold(value):
        return jnp.concatenate([pack(value[0:8], value[8:16]), value[16:24]], axis=0)

    oa_ref[...] = pack(nodes(0), top)
    ob_ref[...] = pack(nodes(1), nodes(7))
    od_ref[...] = pack(dens(0), dens(7))
    up_ref[0:72, :] = pack(nodes(5), nodes(6))
    up_ref[72:144, :] = pack(nodes(7), top)
    up_ref[144:168, :] = pack(dens(5), dens(6))
    up_ref[168:184, :] = fold(dens(7))
    down_ref[0:72, :] = pack(nodes(0), nodes(1))
    down_ref[72:144, :] = pack(nodes(2), nodes(3))
    down_ref[144:168, :] = pack(dens(0), dens(1))
    down_ref[168:184, :] = fold(dens(2))
    odd = odd_place("gz")
    refs[0][...] = jnp.where(odd, down_ref[...], up_ref[...])
    if len(refs) > 5:
        refs[1][...] = jnp.where(odd, up_ref[...], down_ref[...])


def edge_kernel(own_ref, xl_ref, xh_ref, lowy_ref, highy_ref, lhs_ref, el_ref, eh_ref, *refs):
    lower, upper = has_lower("gy"), has_upper("gy")
    row = iota((8, EZ), 0)

    def low(c, p):
        mine = pltpu.roll(x_plane(own_ref, xl_ref, xh_ref, c, p)[0:8], 3, 0)
        other = lowy_ref[node_row(c, p) : node_row(c, p) + 4, :]
        other = jnp.concatenate([other, other], axis=0)
        value = jnp.where(row == 3, average(lower, other, mine, mine), jnp.where(row < 3, other, mine))
        return jnp.where(row < 5, value, 0.0)

    def high(c, p):
        mine = pltpu.roll(x_plane(own_ref, xl_ref, xh_ref, c, p)[EY - 4 : EY + 4], 5, 0)
        other = highy_ref[node_row(c, p) : node_row(c, p) + 4, :]
        other = pltpu.roll(jnp.concatenate([other, other], axis=0), 1, 0)
        value = jnp.where(row == 1, average(upper, mine, other, mine), jnp.where(row < 1, mine, other))
        return jnp.where(row < 5, value, 0.0)

    for side, e_ref in ((low, el_ref), (high, eh_ref)):
        build_nodes(side, range(XN), 8, refs)
        energy_planes(lhs_ref[...], 4, refs, e_ref, 0, XE, 8, [(p, 0) for p in range(XE)], 0)


def triangle(value, axis):
    size = value.shape[axis]
    value = value + pltpu.roll(value, size - 1, axis)
    value = value + pltpu.roll(value, size - 2, axis)
    value = value + pltpu.roll(value, 1, axis)
    return value + pltpu.roll(value, 2, axis)


def weights(distance):
    return jnp.maximum(4 - jnp.abs(distance), 0).astype(F32)


def split_dot(value, right):
    rows = value.shape[0]
    product = jnp.dot(jnp.concatenate(halves(value), axis=0), right, preferred_element_type=F32)
    return product[0:rows] + product[rows:]


def edge_total(count, position, parts):
    total = None
    for offset in range(-RADIUS, RADIUS + 1):
        place = position + offset
        term = float(RADIUS + 1 - abs(offset)) * one_hot((place >= 0) & (place < count * parts))
        total = term if total is None else total + term
    return total


def field_kernel(ea_ref, eb_ref, el_ref, eh_ref, dens_ref, hd_ref, lowy_ref, highy_ref, g_ref, f_ref):
    rows = iota((QROWS, EZ), 0)
    lanes = iota((QROWS, EZ), 1)
    ok = (rows >= 5) & (rows < 55) & (lanes > 0) & (lanes < EZ - 1)
    row = iota((8, EZ), 0)
    for x in range(XE):
        if x < 4:
            middle = eb_ref[x]
        elif x < 4 + OWN:
            middle = ea_ref[x - 4]
        else:
            middle = eb_ref[x - OWN]
        low = pltpu.roll(el_ref[x], 5, 0)
        high = pltpu.roll(eh_ref[x], 3, 0)
        start = jnp.where(row < 1, low, middle[0:8])
        end = jnp.where(row < 3, middle[40:48], high)
        energy = jnp.concatenate([low, start, middle[8:40], end], axis=0)
        at = dens_row(x)
        pad = jnp.zeros((5, EZ), F32)
        d = jnp.concatenate(
            [pad, lowy_ref[at : at + 3, :], x_density(dens_ref, hd_ref, x), highy_ref[at : at + 3, :], pad[0:1]], axis=0)
        f_ref[0, x] = jnp.where(ok, (SCALE * d) * d * d * energy, 0.0)
        f_ref[1, x] = jnp.where(ok, d, 0.0)

    for f in range(2):
        for t in range(QROWS // 8):
            at = slice(t * 8, t * 8 + 8)
            line = [f_ref[f, x, at, :] for x in range(XE)]
            for step in (1, 2, 1, 2):
                line = [line[i] + line[i + step] for i in range(len(line) - step)]
            for x in range(EX):
                f_ref[f, x, at, :] = line[x]
    k, col = iota((EZ, EZ), 0), iota((EZ, EZ), 1)
    right = weights(k - col).astype(BF16)
    for f in range(2):
        for x in range(EX):
            g_ref[f, x] = split_dot(triangle(f_ref[f, x], 0)[8:QROWS], right)


def last_kernel(g_ref, along_ref, right_ref, rs_ref, rd_ref, oa_ref, ob_ref, od_ref, lhs_ref, *refs):
    messages, refs = refs[:-12], refs[-12:]
    outs, (ez_ref, c_ref, zl_ref, zh_ref, e_ref, o_ref, sem), refs = refs[:2], refs[2:9], refs[9:]
    if len(messages) > 1:
        sort_sides("gz", *messages, zl_ref, zh_ref)
    else:
        odd = odd_place("gz")
        zl_ref[...] = jnp.where(odd, messages[0][...], 0.0)
        zh_ref[...] = jnp.where(odd, 0.0, messages[0][...])
    lower, upper = has_lower("gz"), has_upper("gz")

    def swap(value):
        return pltpu.roll(value, 64, 1)

    is_low = iota((3 * XR, EZ), 1) < 64
    oa, ob = oa_ref[...], ob_ref[...]
    zl0, zl1 = zl_ref[0:72, :], zl_ref[72:144, :]
    zh0, zh1 = zh_ref[0:72, :], zh_ref[72:144, :]
    nodes = (
        jnp.where(is_low, zl0, ob),
        jnp.where(is_low, swap(zl0), average(upper, oa, swap(zh0), oa)),
        jnp.where(is_low, zl1, zh0),
        jnp.where(is_low, average(lower, swap(zl1), oa, oa), swap(zh1)),
        jnp.where(is_low, ob, zh1),
    )
    build_nodes(lambda c, k: nodes[k][c * XR : (c + 1) * XR], range(5), XR, refs)
    for ref, step in zip(refs, (8, 16, 16)):
        ref[5 * XR * step : (5 * XR + 8) * step, :] = jnp.zeros((8 * step, EZ), ref.dtype)

    lane = iota((XR, EZ), 1)
    low_side = lane < 64
    od = od_ref[...]
    dl0, dh0 = zl_ref[144:168, :], zh_ref[144:168, :]
    dl1, dh1 = [
        jnp.concatenate([ref[168:176, :], swap(ref[168:176, :]), ref[176:184, :]], axis=0) for ref in (zl_ref, zh_ref)
    ]
    dens = (
        jnp.where(low_side, dl0, od),
        jnp.where(low_side, swap(dl0), swap(dh0)),
        jnp.where(low_side, dl1, dh0),
        jnp.where(low_side, od, swap(dh1)),
    )
    inside = (lane % 64 >= 5) & (lane % 64 < 55) & (iota((XR, EZ), 0) < XE)
    energy_planes(lhs_ref[...], 4, refs, ez_ref, 0, 4, XR, [(j, x) for j in range(4) for x in range(0, XR, 4)], 0)
    parts = []
    for f in range(2):
        for j in range(4):
            d = dens[j]
            value = d if f == 1 else (SCALE * d) * d * d * ez_ref[j]
            c_ref[f, j * EX : (j + 1) * EX, :] = triangle_forward(jnp.where(inside, value, 0.0))[0:EX]
        turned = split_dot(c_ref[f], along_ref[...])
        turned = jnp.concatenate([turned, jnp.zeros((EZ - 4 * EX, EZ), F32)], axis=0).T
        parts.append(jnp.concatenate(halves(turned[8:56] + pltpu.roll(turned[72:120], 64, 1)), axis=1))
    both = jnp.concatenate(parts, axis=0)
    for x in range(0, EX, 2):
        e_ref[:, x * EZ : (x + 2) * EZ] = jnp.dot(both, right_ref[:, x * EZ : (x + 2) * EZ], preferred_element_type=F32)
    copies = []
    for y in (0, 16, 32):
        count = min(16, EY - y)
        for f, inverse_ref in ((0, rs_ref), (1, rd_ref)):
            for x in range(EX):
                end = e_ref[f * ROWS + y : f * ROWS + y + 16, x * EZ : (x + 1) * EZ]
                value = (g_ref[f, x, y : y + 16, :] + end) * inverse_ref[x, y : y + 16, :]
                o_ref[f, pl.ds(y * EX + x, count, stride=EX), :] = value[0:count]
            block = pl.ds(y * EX, count * EX)
            copies.append(pltpu.make_async_copy(o_ref.at[f, block], outs[f].at[block], sem.at[len(copies)]))
            copies[-1].start()
    for copy in copies:
        copy.wait()


def triangle_forward(value):
    size = value.shape[0]
    for step in (1, 2, 1, 2):
        value = value + pltpu.roll(value, size - step, 0)
    return value


def call(kernel, outs, ins, scratch=(), limit=16, micros=1.0, space=VM):
    return pl.pallas_call(
        kernel,
        out_shape=[jax.ShapeDtypeStruct(shape, dtype) for shape, dtype in outs],
        in_specs=[pl.BlockSpec(memory_space=space) for space in ins],
        out_specs=[pl.BlockSpec(memory_space=space)] * len(outs),
        scratch_shapes=[pltpu.VMEM(item[0], item[1]) if isinstance(item, tuple) else item for item in scratch],
        compiler_params=pltpu.CompilerParams(vmem_limit_bytes=limit * 2**20),
        cost_estimate=pl.CostEstimate(flops=0, bytes_accessed=int(micros * 3.6e6), transcendentals=0),
    )


def exchange(axis, spare, *values):
    count, others = lax.axis_size(axis), lax.axis_size(spare)
    names = tuple(sorted((axis, spare)))
    step, spare_step = (others, 1) if names[0] == axis else (1, count)
    results = []
    for first, value in enumerate(values):
        moves = []
        for i in range(count):
            j = i + 1 if i % 2 == first else i - 1
            for o in range(others):
                target = (j, o) if 0 <= j < count else (i, o ^ 1)
                moves.append((i * step + o * spare_step, target[0] * step + target[1] * spare_step))
        results.append(lax.ppermute(value, names, moves))
    return results


def local(local_solution, top_nodes, coarse_solution, corner_dofs, density, element_stiffness):
    dens = jnp.transpose(density, (1, 0, 2)).reshape(EY * EX, EZ)
    shared = lax.axis_size("gz") == 2
    if shared:
        other = lax.ppermute(coarse_solution, "gz", [(0, 1), (1, 0)])
        coarse = jnp.stack([coarse_solution, other])
    else:
        coarse = lax.all_gather(coarse_solution, "gz")

    message = ((X_MESSAGE, EZ), F32)
    even, odd, tops = call(
        pack_kernel,
        [message, message, ((3, XR, EZ), F32)],
        [pltpu.HBM] * 4,
        [((2, 3, 4, NY, EZ), F32), ((3, NX, 1, NY), F32), ((EY * EX, EZ), F32), ((1, 8), jnp.int32), pltpu.SemaphoreType.DMA((9,))],
    )(*[
        pltpu.with_memory_space_constraint(value, pltpu.HBM)
        for value in (local_solution, jnp.transpose(top_nodes, (0, 1, 3, 2)), dens, corner_dofs.reshape(1, 8))
    ])
    even_x, odd_x = exchange("gx", "gy", even, odd)

    own_planes = ((EX, ROWS, EZ), F32)
    rows3, rows4 = ((96, block_rows(3)), BF16), ((128, block_rows(4)), BF16)
    lhs, lhs_edge, lhs_z, dens, inverse_sens, inverse_smooth, dofs, along_y, ends = call(
        prepare_kernel,
        [rows3, rows4, rows4, own_planes, own_planes, own_planes, ((8, EZ), F32), ((EZ, EZ), BF16), ((2 * EZ, EX * EZ), BF16)],
        [VM] * 3,
        [((8, EZ), F32)],
        micros=1.0,
    )(element_stiffness, dens, corner_dofs.reshape(1, 8))

    own_part = ((OWN_ROWS, EZ), F32)
    own, ea, even_own, odd_own = call(
        functools.partial(own_kernel, shared),
        [((3 * NX, ROWS, EZ), F32), ((OWN, ROWS, EZ), F32), own_part, own_part],
        [VM] * 5,
        node_buffers((OWN + 1) * ROWS),
        micros=6.0,
    )(local_solution, lhs, dens, coarse, dofs)

    face = ((12, ROWS, EZ), F32)
    y_message = ((Y_MESSAGE, EZ), F32)
    halo_part = ((Y_MESSAGE - OWN_ROWS, EZ), F32)
    tx, even, odd = call(
        functools.partial(x_kernel, shared),
        [((3, XR, EZ), F32), y_message, y_message],
        [VM] * 8,
        [halo_part, halo_part, ((4, XR, EZ), F32)],
        micros=1.0,
    )(own, even_own, odd_own, tops, even_x, odd_x, coarse, dofs)
    even_y, odd_y = exchange("gy", "gz", even, odd)

    xl, xh, halo_dens = call(
        functools.partial(halo_kernel, shared), [face, face, ((6, ROWS, EZ), F32)], [VM] * 4, micros=0.7
    )(own, even_x, odd_x, coarse)
    (eb,) = call(
        side_kernel, [((XE - OWN, ROWS, EZ), F32)], [VM] * 4, node_buffers((XE - OWN + 2) * ROWS), micros=2.6
    )(own, xl, xh, lhs)

    (zo,) = call(turn_kernel, [((len(SLOTS), 8, EZ), F32)], [VM] * 5, micros=1.5)(own, xl, xh, dens, halo_dens)

    z_message = ((Z_MESSAGE, EZ), F32)
    low_y, high_y, oa, ob, od, *messages = call(
        y_kernel,
        [y_message, y_message, ((72, EZ), F32), ((72, EZ), F32), ((XR, EZ), F32)] + [z_message] * (1 if shared else 2),
        [VM] * 5,
        [((8 * 3 * XR, EZ), F32), ((8 * XR, EZ), F32), z_message, z_message],
        micros=1.0,
    )(tx, zo, eb, even_y, odd_y)
    received_z = exchange("gz", "gy", *messages)

    el, eh = call(
        edge_kernel,
        [((XE, 8, EZ), F32)] * 2,
        [VM] * 6,
        node_buffers(XN * 8),
        micros=2.3,
    )(own, xl, xh, low_y, high_y, lhs_edge)

    (filtered,) = call(
        field_kernel, [((2, EX, ROWS, EZ), F32)], [VM] * 8, [((2, XE, QROWS, EZ), F32)], micros=1.5
    )(ea, eb, el, eh, dens, halo_dens, low_y, high_y)

    sens, smooth = call(
        last_kernel,
        [((EY * EX, EZ), F32)] * 2,
        [VM] * (9 + len(received_z)),
        [((4, XR, EZ), F32), ((2, 4 * EX, EZ), F32), z_message, z_message, ((2 * ROWS, EX * EZ), F32), ((2, EY * EX, EZ), F32),
         pltpu.SemaphoreType.DMA((6,))] + node_buffers(5 * XR + 8),
        space=pltpu.HBM,
        micros=2.5,
    )(filtered, along_y, ends, inverse_sens, inverse_smooth, oa, ob, od, lhs_z, *received_z)

    def grid(value):
        return jnp.transpose(value.reshape(EY, EX, EZ), (1, 0, 2))

    return grid(sens), grid(smooth)


def solution(mesh):
    in_specs = (
        P(None, "gx", "gy", "gz"),
        P(None, "gx", "gy", "gz"),
        P(None, "gz"),
        P("gx", "gy", "gz", None),
        P("gx", "gy", "gz"),
        P(),
    )
    out_specs = (P("gx", "gy", "gz"), P("gx", "gy", "gz"))
    return jax.shard_map(local, mesh=mesh, in_specs=in_specs, out_specs=out_specs, check_vma=False)
```

```python
import functools

import jax
import jax.numpy as jnp
from jax import lax
from jax.experimental import pallas as pl
from jax.experimental.pallas import tpu as pltpu
from jax.sharding import PartitionSpec as P

RADIUS = 3
F32 = jnp.float32
BF16 = jnp.bfloat16
SCALE = -3.0 / 96.0
HIGHEST = lax.Precision.HIGHEST
VM = pltpu.VMEM

EX, EY, EZ = 16, 44, 128
NX, NY = EX + 1, EY + 1
XN, XE = NX + 2 * RADIUS, EX + 2 * RADIUS
ROWS = 48
QROWS = 56
OWN = 12
XR = 24


def iota(shape, dim):
    return lax.broadcasted_iota(jnp.int32, shape, dim)


def one_hot(mask):
    return jnp.where(mask, 1.0, 0.0).astype(F32)


def halves(value):
    high = value.astype(BF16)
    return high, (value - high.astype(F32)).astype(BF16)


def as_column(row):
    lane, sub = iota((8, EZ), 1), iota((8, EZ), 0)
    return jnp.sum(jnp.where(lane == sub, row, 0.0), axis=1, keepdims=True)


def corner_values(coarse_ref, dofs, shared):
    parts, _, width = coarse_ref.shape
    dofs = dofs.astype(jnp.int32)
    own = lax.axis_index("gz")
    lane = iota((8, width), 1)
    totals = [0.0] * 3
    for part in range(parts):
        place = part if not shared else own if part == 0 else 1 - own
        found = lane + place * width == dofs
        for c in range(3):
            totals[c] = totals[c] + jnp.where(found, coarse_ref[part, c : c + 1, :], 0.0)
    return [jnp.broadcast_to(jnp.sum(total, axis=1, keepdims=True), (8, EZ)) for total in totals]


def corner_rows(corners, c):
    rz = iota((8, EZ), 1).astype(F32) * (1.0 / EZ)
    other = 1.0 - rz
    value = [corners[c][k : k + 1] for k in range(8)]
    return [[value[4 * kx + 2 * ky] * other + value[4 * kx + 2 * ky + 1] * rz for ky in (0, 1)] for kx in (0, 1)]


def plane_interp(edges, i, rows, start=0):
    wx = i / EX
    first, second = [((1.0 - wx) * edges[0][ky] + wx * edges[1][ky])[0:1] for ky in (0, 1)]
    ry = (start + iota((rows, EZ), 0)).astype(F32) * (1.0 / EY)
    return (1.0 - ry) * first + ry * second


def block_rows(block):
    nodes = block + 1
    return 2 * (16 * nodes + 16 * ((nodes + 1) // 2))


def stiffness_rows(stiff, block, in_lanes):
    def target(h, t, r):
        s, c = r // 4, r % 4
        place = 4 * t + 2 * s + h if in_lanes else 4 * h + 2 * t + s
        return jnp.where(c < 3, 8 * c + place, -1)

    row = iota((32, 24), 0)
    left = one_hot(iota((32, 24), 1) == target(row // 16, row // 8 % 2, row % 8))
    full = jnp.dot(left, stiff, precision=HIGHEST, preferred_element_type=F32)
    nodes, width = block + 1, block_rows(block)
    split = 32 * nodes
    half = (width - split) // 2
    col = iota((24, width), 1)
    again = col >= split
    h = jnp.where(again, (col - split) // half, col // (16 * nodes))
    node = jnp.where(again, (col - split) % half // 8, col % (16 * nodes) // 16)
    wide = iota((32, width), 1) >= split
    rows = []
    for e in range(block):
        t = node - e
        right = one_hot((iota((24, width), 0) == target(h, t, col % 8)) & (t >= 0) & (t < 2))
        part = jnp.dot(full, right, precision=HIGHEST, preferred_element_type=F32)
        high = part.astype(BF16).astype(F32)
        rows.append(jnp.where(wide, part - high, high))
    return jnp.concatenate(rows, axis=0).astype(BF16)


def build_nodes(plane_of, planes, rows, refs, first=0):
    w_ref, b_ref, h_ref = refs
    for p in planes:
        base = (first + p) * rows * 8
        zero = jnp.zeros((rows, EZ), F32)
        for c in range(3):
            value = plane_of(c, p)
            w_ref[pl.ds(base + c, rows, stride=8), :] = value
            w_ref[pl.ds(base + 4 + c, rows, stride=8), :] = pltpu.roll(value, EZ - 1, 1)
        w_ref[pl.ds(base + 3, rows, stride=8), :] = zero
        w_ref[pl.ds(base + 7, rows, stride=8), :] = zero

    def split(p, _):
        base = (first + p) * rows
        last = None
        for r in range(rows):
            value = w_ref[pl.ds(pl.multiple_of((base + r) * 8, 8), 8), :]
            high = value.astype(BF16).astype(F32)
            at = pl.ds(pl.multiple_of((base + r) * 16, 16), 16)
            b_ref[at, :] = jnp.concatenate([high, value - high], axis=0).astype(BF16)
            if last is not None:
                h_ref[pl.ds(pl.multiple_of((base + r - 1) * 16, 16), 16), :] = jnp.concatenate([last, high], axis=0).astype(BF16)
            last = high
        h_ref[at, :] = jnp.concatenate([last, last], axis=0).astype(BF16)
        return 0

    lax.fori_loop(0, len(planes), split, 0)


def sum_rows(values):
    row = iota((8, EZ), 0)
    for step in (1, 2, 4):
        first = row % (2 * step) < step
        values = [
            jnp.where(first, a, b) + pltpu.roll(jnp.where(first, b, a), step, 0)
            for a, b in zip(values[::2], values[1::2])
        ]
    return values[0]


def energy_planes(lhs, block, refs, e_ref, first, count, rows, blocks, out_first):
    w_ref, b_ref, h_ref = refs
    nodes = block + 1
    zero = jnp.zeros((8, EZ), F32)
    found, left = {}, {(p, t) for p in range(count) for t in range(0, rows, 8)}

    def store(before):
        for p, t in sorted(left):
            if (p, t + 7) < before:
                values = [found.pop((p, t + i), zero) for i in range(8)]
                e_ref[out_first + p, t : t + 8, :] = zero if all(v is zero for v in values) else sum_rows(values)
                left.remove((p, t))

    for i in range(0, len(blocks), 2):
        pair = blocks[i : i + 2]
        right = []
        for p, r in pair:
            at = (first + p) * rows + r
            parts = [b_ref[(at + far) * 16 : (at + far + nodes) * 16, :] for far in (0, rows)]
            for far in (0, rows):
                parts += [h_ref[(at + far + t) * 16 : (at + far + t + 1) * 16, :] for t in range(0, nodes, 2)]
            right.append(jnp.concatenate(parts, axis=0))
        product = jnp.dot(lhs, jnp.concatenate(right, axis=1), preferred_element_type=F32)
        for u, (p, r) in enumerate(pair):
            at = (first + p) * rows + r
            for e in range(min(block, rows - r)):
                part = product[32 * e : 32 * e + 32, u * EZ : (u + 1) * EZ]
                low = w_ref[(at + e) * 8 : (at + e + 2) * 8, :] * part[0:16]
                high = w_ref[(at + rows + e) * 8 : (at + rows + e + 2) * 8, :] * part[16:32]
                both = low + high
                found[p, r + e] = both[0:8] + both[8:16]
        store(blocks[i + 2] if i + 2 < len(blocks) else (count, 0))


def node_buffers(count):
    return [((count * 8, EZ), F32), ((count * 16, EZ), BF16), ((count * 16, EZ), BF16)]


def odd_place(axis):
    return lax.axis_index(axis) % 2 == 1


X_MESSAGE = 680
X_DENSITY, X_TOP, X_DOFS = 576, 672, 678


def third_rows():
    spare = [(48 * i + NY, 3 * i, 3) for i in range(12)]
    return spare + [(X_DENSITY + EY, 36, 4), (X_DENSITY + ROWS + EY, 40, 4)]


def pack_kernel(local_ref, top_ref, dens_ref, dofs_ref, even_ref, odd_ref, tops_ref, l_ref, t_ref, d_ref, c_ref, sem):
    copies = []
    for source, dest in ((top_ref, t_ref), (dofs_ref, c_ref), (dens_ref, d_ref)):
        copies.append(pltpu.make_async_copy(source, dest, sem.at[len(copies)]))
    for c in range(3):
        for side, node in ((0, EX - RADIUS), (1, 0)):
            copies.append(pltpu.make_async_copy(local_ref.at[c, node : node + 4], l_ref.at[side, c], sem.at[len(copies)]))
    for copy in copies:
        copy.start()
    for out_ref in (even_ref, odd_ref):
        out_ref[X_TOP:X_MESSAGE, :] = jnp.zeros((X_MESSAGE - X_TOP, EZ), F32)
    clear(tops_ref)
    flip = odd_place("gx")
    outs = ((even_ref, flip), (odd_ref, jnp.logical_not(flip)))
    for copy in copies[:3]:
        copy.wait()
    for c in range(3):
        for i in range(NX):
            tops_ref[c, i : i + 1, 0:NY] = t_ref[c, i]
    for out_ref, flip in outs:
        faces = [jnp.where(flip, tops_ref[c, 0:4, :], tops_ref[c, EX - RADIUS : EX - RADIUS + 4, :]) for c in range(3)]
        faces = jnp.concatenate(faces, axis=0)
        out_ref[X_TOP : X_TOP + 6, :] = faces[0:6] + pltpu.roll(faces[6:12], 64, 1)
        for j in range(3):
            value = jnp.where(flip, d_ref[pl.ds(j, EY, stride=EX), :], d_ref[pl.ds(EX - RADIUS + j, EY, stride=EX), :])
            if j < 2:
                out_ref[X_DENSITY + j * ROWS : X_DENSITY + j * ROWS + EY, :] = value
            else:
                for at, first, count in third_rows():
                    out_ref[at : at + count, :] = value[first : first + count]
        out_ref[X_DOFS : X_DOFS + 1, 0:8] = c_ref[...].astype(F32)
    for c in range(3):
        for copy in copies[3 + 2 * c : 5 + 2 * c]:
            copy.wait()
        for out_ref, flip in outs:
            side = flip.astype(jnp.int32)
            for j in range(4):
                out_ref[(c * 4 + j) * ROWS : (c * 4 + j) * ROWS + NY, :] = l_ref[side, c, j]


def sort_sides(axis, even_ref, odd_ref, low_ref, high_ref):
    odd = odd_place(axis)
    even, other = even_ref[...], odd_ref[...]
    low_ref[...] = jnp.where(has_lower(axis), jnp.where(odd, even, other), 0.0)
    high_ref[...] = jnp.where(has_upper(axis), jnp.where(odd, other, even), 0.0)


def prepare_kernel(stiff_ref, dens_ref, dofs_in_ref, lhs_ref, lhs_edge_ref, lhs_z_ref, od_ref, rs_ref, rd_ref,
                   dofs_ref, along_ref, right_ref, row_ref):
    stiff = stiff_ref[...]
    clear(row_ref)
    row_ref[0:1, 0:8] = dofs_in_ref[...].astype(F32)
    dofs_ref[...] = jnp.broadcast_to(as_column(row_ref[0:1, :]), (8, EZ))
    k, col = iota((EZ, EZ), 0), iota((EZ, EZ), 1)
    along_ref[...] = jnp.where(k // 64 == col // 64, weights(k - col), 0.0).astype(BF16)
    j = (k % 64) // EX
    weight = weights(jnp.where(k < 64, j - 3, EZ - 1 + j) - col)
    for x in range(EX):
        part = jnp.where(k % EX == x, weight, 0.0).astype(BF16)
        right_ref[0:EZ, x * EZ : (x + 1) * EZ] = part
        right_ref[EZ : 2 * EZ, x * EZ : (x + 1) * EZ] = part
    lhs_ref[...] = stiffness_rows(stiff, 3, False)
    lhs_edge_ref[...] = stiffness_rows(stiff, 4, False)
    lhs_z_ref[...] = stiffness_rows(stiff, 4, True)
    base_x, base_y, base_z = lax.axis_index("gx") * EX, lax.axis_index("gy") * EY, lax.axis_index("gz") * EZ
    inside = iota((ROWS, EZ), 0) < EY
    norm_y = edge_total(EY, base_y + iota((ROWS, EZ), 0), lax.axis_size("gy"))
    norm_z = edge_total(EZ, base_z + iota((ROWS, EZ), 1), lax.axis_size("gz"))
    inverse = 1.0 / jnp.where(inside, norm_y * norm_z, 1.0)
    place = base_x + iota((8, EZ), 0)
    inverse_x = [1.0 / edge_total(EX, place + t, lax.axis_size("gx")) for t in (0, 8)]
    for x in range(EX):
        d = dens_ref[pl.ds(x, EY, stride=EX), :]
        od_ref[x, 0:EY, :] = d
        od_ref[x, EY:ROWS, :] = jnp.ones((ROWS - EY, EZ), F32)
        both = inverse * inverse_x[x // 8][x % 8 : x % 8 + 1, :]
        rd_ref[x] = both
        rs_ref[x] = both / od_ref[x]


def own_kernel(shared, local_ref, lhs_ref, dens_ref, coarse_ref, dofs_ref, own_ref, e_ref, even_ref, odd_ref, *refs):
    corners = corner_values(coarse_ref, dofs_ref[:, 0:1], shared)
    for c in range(3):
        edges = corner_rows(corners, c)
        for i in range(NX):
            own_ref[c * NX + i, 0:NY, :] = local_ref[c, i] + plane_interp(edges, i, NY)
            own_ref[c * NX + i, NY:ROWS, :] = jnp.zeros((ROWS - NY, EZ), F32)
    odd = odd_place("gy")
    for out_ref, first, second in ((even_ref, EY - RADIUS, 0), (odd_ref, 0, EY - RADIUS)):
        out_ref[OWN_ROWS - 4 : OWN_ROWS, :] = jnp.zeros((4, EZ), F32)
        for p in range(4, 19):
            for c in range(3):
                at = node_row(c, p)
                plane = own_ref[c * NX + p - 3]
                out_ref[at : at + 4, :] = jnp.where(odd, plane[second : second + 4], plane[first : first + 4])
        for x in range(3, 19):
            plane = dens_ref[x - 3]
            out_ref[dens_row(x) : dens_row(x) + 3, :] = jnp.where(odd, plane[second : second + 3], plane[first : first + 3])
    build_nodes(lambda c, p: own_ref[c * NX + p + 1], range(OWN + 1), ROWS, refs)
    blocks = [(p, r) for p in range(OWN) for r in range(1, EY - 1, 3)]
    energy_planes(lhs_ref[...], 3, refs, e_ref, 0, OWN, ROWS, blocks, 0)


def clear(ref):
    ref[...] = jnp.zeros(ref.shape, ref.dtype)


def average(flag, low, high, own):
    return jnp.where(flag, 0.5 * low + 0.5 * high, own)


OWN_ROWS = 232
TOP_AT = 352
Y_MESSAGE = TOP_AT + 8


def node_row(c, p):
    if 4 <= p < 19:
        return 4 * (c * 15 + p - 4)
    return OWN_ROWS + 4 * (c * 8 + (p if p < 4 else p - 15))


def dens_row(x):
    if 3 <= x < 19:
        return 180 + 3 * (x - 3)
    return OWN_ROWS + 96 + 3 * (x if x < 3 else x - 16)


SLOTS = sorted(
    [("node", c, p) for c in range(3) for p in range(XN)] + [("density", x, x) for x in range(XE)],
    key=lambda slot: node_row(*slot[1:]) if slot[0] == "node" else dens_row(slot[1]),
)


def has_lower(axis):
    return lax.axis_index(axis) > 0


def has_upper(axis):
    return lax.axis_index(axis) < lax.axis_size(axis) - 1


def top_interp(corners, c, rows):
    rx = iota((rows, EZ), 0).astype(F32) * (1.0 / EX)
    ry = iota((rows, EZ), 1).astype(F32) * (1.0 / EY)
    value = [corners[c][k : k + 1] for k in range(8)]
    low = (1.0 - ry) * value[1] + ry * value[3]
    high = (1.0 - ry) * value[5] + ry * value[7]
    return (1.0 - rx) * low + rx * high


def x_sides(even_ref, odd_ref):
    flip = odd_place("gx")

    def low(at, count):
        return jnp.where(flip, even_ref[at : at + count, :], odd_ref[at : at + count, :])

    def high(at, count):
        return jnp.where(flip, odd_ref[at : at + count, :], even_ref[at : at + count, :])

    return low, high


def side_corners(shared, coarse_ref, sides):
    return [corner_values(coarse_ref, as_column(side(X_DOFS, 1)), shared) for side in sides]


def x_faces(own_ref, sides, corners, start, rows):
    lower, upper = has_lower("gx"), has_upper("gx")
    for c in range(3):
        edges = [corner_rows(corner, c) for corner in corners]
        for j in range(4):
            low, high = [
                side((c * 4 + j) * ROWS + start, rows) + plane_interp(edge, i, rows, start)
                for side, edge, i in zip(sides, edges, (EX - RADIUS + j, j))
            ]
            if j == 3:
                mine = own_ref[c * NX, start : start + rows, :]
                low = average(lower, low, mine, mine)
            if j == 0:
                mine = own_ref[c * NX + EX, start : start + rows, :]
                high = average(upper, mine, high, mine)
            yield c, j, low
            yield c, 19 + j, high


def halo_kernel(shared, own_ref, even_ref, odd_ref, coarse_ref, xl_ref, xh_ref, hd_ref):
    sides = x_sides(even_ref, odd_ref)
    for c, p, value in x_faces(own_ref, sides, side_corners(shared, coarse_ref, sides), 0, ROWS):
        if p < 4:
            xl_ref[c * 4 + p] = value
        else:
            xh_ref[c * 4 + p - 19] = value
    for first, side, there in zip((0, 3), sides, (has_lower("gx"), has_upper("gx"))):
        for j in range(2):
            hd_ref[first + j] = jnp.where(there, side(X_DENSITY + j * ROWS, ROWS), 0.0)
        hd_ref[first + 2, EY:ROWS, :] = jnp.zeros((ROWS - EY, EZ), F32)
        for at, row, count in third_rows():
            hd_ref[first + 2, row : row + count, :] = jnp.where(there, side(at, count), 0.0)


def x_kernel(shared, own_ref, even_own_ref, odd_own_ref, top_ref, even_ref, odd_ref, coarse_ref, dofs_ref,
             tx_ref, yeven_ref, yodd_ref, up_ref, down_ref, t_ref):
    sides = low_rows, high_rows = x_sides(even_ref, odd_ref)
    corners = corner_values(coarse_ref, dofs_ref[:, 0:1], shared)
    corners_low, corners_high = side_corners(shared, coarse_ref, sides)
    lower, upper = has_lower("gx"), has_upper("gx")
    for out_ref, start, skip in ((up_ref, EY - 4, 1), (down_ref, 0, 0)):
        for c, p, value in x_faces(own_ref, sides, (corners_low, corners_high), start, 8):
            at = node_row(c, p) - OWN_ROWS
            out_ref[at : at + 4, :] = value[skip : skip + 4]
        for x in (0, 1, 2, 19, 20, 21):
            j, side, there = (x, low_rows, lower) if x < 3 else (x - 19, high_rows, upper)
            row = start + skip
            if j < 2:
                value = side(X_DENSITY + j * ROWS + row, 3)
            else:
                value = side(NY if row == 0 else X_DENSITY + ROWS + EY + 1, 3)
            at = dens_row(x) - OWN_ROWS
            out_ref[at : at + 3, :] = jnp.where(there, value, 0.0)
        out_ref[TOP_AT - 6 - OWN_ROWS : TOP_AT - OWN_ROWS, :] = jnp.zeros((6, EZ), F32)

    t_ref[...] = jnp.zeros(t_ref.shape, F32)
    for c in range(3):
        t_ref[0] = top_ref[c] + top_interp(corners, c, XR)
        for side, side_rows in ((1, low_rows), (2, high_rows)):
            both = side_rows(X_TOP, 6)
            both = jnp.concatenate([both, pltpu.roll(both, 64, 1)], axis=0)
            t_ref[side, 0:4, :] = both[4 * c : 4 * c + 4]
        t_low = t_ref[1, 0:8, :] + pltpu.roll(top_interp(corners_low, c, 24), 24 - (EX - RADIUS), 0)[0:8]
        t_high = t_ref[2, 0:8, :] + top_interp(corners_high, c, 8)
        first = average(lower, t_low[3:4], t_ref[0, 0:1, :], t_ref[0, 0:1, :])
        last = average(upper, t_ref[0, EX : EX + 1, :], t_high[0:1], t_ref[0, EX : EX + 1, :])
        t_ref[3, 0:3, :] = t_low[0:3]
        t_ref[3, 3:4, :] = first
        t_ref[3, 4:19, :] = t_ref[0, 1:EX, :]
        t_ref[3, 19:20, :] = last
        t_ref[3, 20:23, :] = t_high[1:4]
        lane = iota((XR, EZ), 1)
        tx_ref[c] = jnp.where(lane < NY + 8, pltpu.roll(t_ref[3], 8, 1), 0.0)

    lane = iota((XR, EZ), 1)
    for out_ref, lane_at in ((up_ref, EY - RADIUS + 8), (down_ref, 8)):
        total = jnp.zeros((XR, EZ), F32)
        for c in range(3):
            moved = pltpu.roll(tx_ref[c], (4 * c - lane_at) % EZ, 1)
            total = jnp.where((lane >= 4 * c) & (lane < 4 * c + 4), moved, total)
        out_ref[TOP_AT - OWN_ROWS :, :] = total[0:8] + pltpu.roll(total[8:16], 16, 1) + pltpu.roll(total[16:24], 32, 1)
    odd = odd_place("gy")
    yeven_ref[0:OWN_ROWS, :] = even_own_ref[...]
    yodd_ref[0:OWN_ROWS, :] = odd_own_ref[...]
    for mine, other, out_ref in ((up_ref, down_ref, yeven_ref), (down_ref, up_ref, yodd_ref)):
        out_ref[OWN_ROWS:, :] = jnp.where(odd, other[...], mine[...])


def side_kernel(own_ref, xl_ref, xh_ref, lhs_ref, e_ref, *refs):
    high = XE - 4 - OWN

    def plane(c, p):
        if p < 5:
            return x_plane(own_ref, xl_ref, xh_ref, c, p)
        return x_plane(own_ref, xl_ref, xh_ref, c, p - 5 + 4 + OWN)

    build_nodes(plane, range(5 + high + 1), ROWS, refs)
    for first, count, out_first in ((0, 4, 0), (5, high, 4)):
        blocks = [(p, r) for p in range(count) for r in range(1, EY - 1, 3)]
        energy_planes(lhs_ref[...], 3, refs, e_ref, first, count, ROWS, blocks, out_first)


Z_MESSAGE = 184


def x_plane(own_ref, xl_ref, xh_ref, c, p):
    if p < 4:
        return xl_ref[c * 4 + p]
    if p < 19:
        return own_ref[c * NX + p - 3]
    return xh_ref[c * 4 + p - 19]


def x_density(dens_ref, hd_ref, x, rows=EY):
    if x < 3:
        return hd_ref[x, 0:rows, :]
    if x < 19:
        return dens_ref[x - 3, 0:rows, :]
    return hd_ref[x - 16, 0:rows, :]


def end_planes(turned):
    return jnp.concatenate([turned[0:4], turned[EZ - 4 : EZ]], axis=0)


def turn_kernel(own_ref, xl_ref, xh_ref, dens_ref, hd_ref, z_ref):
    head = jnp.zeros((8, EZ), F32)

    def padded(slot):
        kind, c, p = SLOTS[min(slot, len(SLOTS) - 1)]
        if kind == "node":
            return [head, x_plane(own_ref, xl_ref, xh_ref, c, p), head]
        return [head, x_density(dens_ref, hd_ref, c, ROWS), head]

    lane = iota((8, EZ), 1)
    for slot in range(0, len(SLOTS), 2):
        both = end_planes(jnp.concatenate(padded(slot) + padded(slot + 1), axis=0).T)
        z_ref[slot] = jnp.where(lane < 64, both, 0.0)
        if slot + 1 < len(SLOTS):
            z_ref[slot + 1] = jnp.where(lane < 64, pltpu.roll(both, 64, 1), 0.0)


def y_kernel(tx_ref, zo_ref, eb_ref, even_ref, odd_ref,
             low_ref, high_ref, oa_ref, ob_ref, od_ref, *refs):
    del eb_ref
    z_ref, d_ref = refs[-2:]
    sort_sides("gy", even_ref, odd_ref, low_ref, high_ref)
    lower, upper = has_lower("gy"), has_upper("gy")
    clear(z_ref)
    clear(d_ref)
    lane = iota((8, EZ), 1)
    turned = []
    for first in range(0, TOP_AT, EZ):
        turned.append([])
        for ref in (low_ref, high_ref):
            block = ref[first : min(first + EZ, TOP_AT), :]
            if block.shape[0] < EZ:
                block = jnp.concatenate([block, jnp.zeros((EZ - block.shape[0], EZ), F32)], axis=0)
            turned[-1].append(end_planes(block.T))
    for slot, (kind, c, p) in enumerate(SLOTS):
        at = node_row(c, p) if kind == "node" else dens_row(c)
        low = pltpu.roll(turned[at // EZ][0], (5 - at) % EZ, 1)
        high = pltpu.roll(turned[at // EZ][1], (52 - at) % EZ, 1)
        mine = zo_ref[slot]
        value = jnp.where((lane >= 5) & (lane < 8), low, mine)
        if kind == "node":
            at = c * XR + p
            value = jnp.where((lane == 8) & lower, 0.5 * low + 0.5 * mine, value)
            value = jnp.where((lane == 52) & upper, 0.5 * mine + 0.5 * high, value)
            z_ref[at * 8 : at * 8 + 8, :] = jnp.where((lane > 52) & (lane < 56), high, value)
        else:
            d_ref[c * 8 : c * 8 + 8, :] = jnp.where((lane >= 52) & (lane < 55), high, value)

    lane = iota((XR, EZ), 1)
    tops = []
    for c in range(3):
        mine = tx_ref[c]
        low, high = [
            jnp.concatenate([pltpu.roll(ref[TOP_AT:Y_MESSAGE, :], (to - 4 * c - 16 * g) % EZ, 1) for g in range(3)], axis=0)
            for ref, to in ((low_ref, 5), (high_ref, 52))
        ]
        value = jnp.where((lane >= 5) & (lane < 8), low, mine)
        value = jnp.where(lane == 8, average(lower, low, mine, mine), value)
        value = jnp.where(lane == 52, average(upper, mine, high, mine), value)
        tops.append(jnp.where((lane > 52) & (lane < 56), high, value))
    top = jnp.concatenate(tops, axis=0)

    def nodes(k):
        return z_ref[pl.ds(k, 3 * XR, stride=8), :]

    def dens(k):
        return d_ref[pl.ds(k, XR, stride=8), :]

    def pack(low, high):
        return low + pltpu.roll(high, 64, 1)

    def fold(value):
        return jnp.concatenate([pack(value[0:8], value[8:16]), value[16:24]], axis=0)

    oa_ref[...] = pack(nodes(0), top)
    ob_ref[...] = pack(nodes(1), nodes(7))
    od_ref[...] = pack(dens(0), dens(7))
    odd = odd_place("gz")
    for out_ref, down in zip(refs[:-2], (odd, jnp.logical_not(odd))):
        first = jnp.where(down, 0, 5)
        out_ref[0:72, :] = pack(nodes(first), nodes(first + 1))
        out_ref[72:144, :] = pack(nodes(first + 2), jnp.where(down, nodes(3), top))
        out_ref[144:168, :] = pack(dens(first), dens(first + 1))
        out_ref[168:184, :] = fold(dens(first + 2))


def edge_kernel(own_ref, xl_ref, xh_ref, lowy_ref, highy_ref, lhs_ref, el_ref, eh_ref, *refs):
    lower, upper = has_lower("gy"), has_upper("gy")
    row = iota((8, EZ), 0)

    def low(c, p):
        mine = pltpu.roll(x_plane(own_ref, xl_ref, xh_ref, c, p)[0:8], 3, 0)
        other = lowy_ref[node_row(c, p) : node_row(c, p) + 4, :]
        other = jnp.concatenate([other, other], axis=0)
        value = jnp.where(row == 3, average(lower, other, mine, mine), jnp.where(row < 3, other, mine))
        return jnp.where(row < 5, value, 0.0)

    def high(c, p):
        mine = pltpu.roll(x_plane(own_ref, xl_ref, xh_ref, c, p)[EY - 4 : EY + 4], 5, 0)
        other = highy_ref[node_row(c, p) : node_row(c, p) + 4, :]
        other = pltpu.roll(jnp.concatenate([other, other], axis=0), 1, 0)
        value = jnp.where(row == 1, average(upper, mine, other, mine), jnp.where(row < 1, mine, other))
        return jnp.where(row < 5, value, 0.0)

    for side, e_ref in ((low, el_ref), (high, eh_ref)):
        build_nodes(side, range(XN), 8, refs)
        energy_planes(lhs_ref[...], 4, refs, e_ref, 0, XE, 8, [(p, 0) for p in range(XE)], 0)


def triangle(value, axis):
    size = value.shape[axis]
    value = value + pltpu.roll(value, size - 1, axis)
    value = value + pltpu.roll(value, size - 2, axis)
    value = value + pltpu.roll(value, 1, axis)
    return value + pltpu.roll(value, 2, axis)


def weights(distance):
    return jnp.maximum(4 - jnp.abs(distance), 0).astype(F32)


def split_dot(value, right):
    rows = value.shape[0]
    product = jnp.dot(jnp.concatenate(halves(value), axis=0), right, preferred_element_type=F32)
    return product[0:rows] + product[rows:]


def edge_total(count, position, parts):
    total = None
    for offset in range(-RADIUS, RADIUS + 1):
        place = position + offset
        term = float(RADIUS + 1 - abs(offset)) * one_hot((place >= 0) & (place < count * parts))
        total = term if total is None else total + term
    return total


def field_kernel(ea_ref, eb_ref, el_ref, eh_ref, dens_ref, hd_ref, lowy_ref, highy_ref, g_ref, f_ref):
    rows = iota((QROWS, EZ), 0)
    lanes = iota((QROWS, EZ), 1)
    ok = (rows >= 5) & (rows < 55) & (lanes > 0) & (lanes < EZ - 1)
    row = iota((8, EZ), 0)
    for x in range(XE):
        if x < 4:
            middle = eb_ref[x]
        elif x < 4 + OWN:
            middle = ea_ref[x - 4]
        else:
            middle = eb_ref[x - OWN]
        low = pltpu.roll(el_ref[x], 5, 0)
        high = pltpu.roll(eh_ref[x], 3, 0)
        start = jnp.where(row < 1, low, middle[0:8])
        end = jnp.where(row < 3, middle[40:48], high)
        energy = jnp.concatenate([low, start, middle[8:40], end], axis=0)
        at = dens_row(x)
        pad = jnp.zeros((5, EZ), F32)
        d = jnp.concatenate(
            [pad, lowy_ref[at : at + 3, :], x_density(dens_ref, hd_ref, x), highy_ref[at : at + 3, :], pad[0:1]], axis=0)
        f_ref[0, x] = jnp.where(ok, (SCALE * d) * d * d * energy, 0.0)
        f_ref[1, x] = jnp.where(ok, d, 0.0)

    for f in range(2):
        for t in range(QROWS // 8):
            at = slice(t * 8, t * 8 + 8)
            line = [f_ref[f, x, at, :] for x in range(XE)]
            for step in (1, 2, 1, 2):
                line = [line[i] + line[i + step] for i in range(len(line) - step)]
            for x in range(EX):
                f_ref[f, x, at, :] = line[x]
    k, col = iota((EZ, EZ), 0), iota((EZ, EZ), 1)
    right = weights(k - col).astype(BF16)
    for f in range(2):
        for x in range(EX):
            g_ref[f, x] = split_dot(triangle(f_ref[f, x], 0)[8:QROWS], right)


def last_kernel(g_ref, along_ref, right_ref, rs_ref, rd_ref, oa_ref, ob_ref, od_ref, lhs_ref, *refs):
    messages, refs = refs[:-12], refs[-12:]
    outs, (ez_ref, c_ref, zl_ref, zh_ref, e_ref, o_ref, sem), refs = refs[:2], refs[2:9], refs[9:]
    if len(messages) > 1:
        sort_sides("gz", *messages, zl_ref, zh_ref)
    else:
        odd = odd_place("gz")
        zl_ref[...] = jnp.where(odd, messages[0][...], 0.0)
        zh_ref[...] = jnp.where(odd, 0.0, messages[0][...])
    lower, upper = has_lower("gz"), has_upper("gz")

    def swap(value):
        return pltpu.roll(value, 64, 1)

    is_low = iota((3 * XR, EZ), 1) < 64
    oa, ob = oa_ref[...], ob_ref[...]
    zl0, zl1 = zl_ref[0:72, :], zl_ref[72:144, :]
    zh0, zh1 = zh_ref[0:72, :], zh_ref[72:144, :]
    nodes = (
        jnp.where(is_low, zl0, ob),
        jnp.where(is_low, swap(zl0), average(upper, oa, swap(zh0), oa)),
        jnp.where(is_low, zl1, zh0),
        jnp.where(is_low, average(lower, swap(zl1), oa, oa), swap(zh1)),
        jnp.where(is_low, ob, zh1),
    )
    build_nodes(lambda c, k: nodes[k][c * XR : (c + 1) * XR], range(5), XR, refs)
    for ref, step in zip(refs, (8, 16, 16)):
        ref[5 * XR * step : (5 * XR + 8) * step, :] = jnp.zeros((8 * step, EZ), ref.dtype)

    lane = iota((XR, EZ), 1)
    low_side = lane < 64
    od = od_ref[...]
    dl0, dh0 = zl_ref[144:168, :], zh_ref[144:168, :]
    dl1, dh1 = [
        jnp.concatenate([ref[168:176, :], swap(ref[168:176, :]), ref[176:184, :]], axis=0) for ref in (zl_ref, zh_ref)
    ]
    dens = (
        jnp.where(low_side, dl0, od),
        jnp.where(low_side, swap(dl0), swap(dh0)),
        jnp.where(low_side, dl1, dh0),
        jnp.where(low_side, od, swap(dh1)),
    )
    inside = (lane % 64 >= 5) & (lane % 64 < 55) & (iota((XR, EZ), 0) < XE)
    energy_planes(lhs_ref[...], 4, refs, ez_ref, 0, 4, XR, [(j, x) for j in range(4) for x in range(0, XR, 4)], 0)
    parts = []
    for f in range(2):
        for j in range(4):
            d = dens[j]
            value = d if f == 1 else (SCALE * d) * d * d * ez_ref[j]
            c_ref[f, j * EX : (j + 1) * EX, :] = triangle_forward(jnp.where(inside, value, 0.0))[0:EX]
        turned = split_dot(c_ref[f], along_ref[...])
        turned = jnp.concatenate([turned, jnp.zeros((EZ - 4 * EX, EZ), F32)], axis=0).T
        parts.append(jnp.concatenate(halves(turned[8:56] + pltpu.roll(turned[72:120], 64, 1)), axis=1))
    both = jnp.concatenate(parts, axis=0)
    for x in range(0, EX, 2):
        e_ref[:, x * EZ : (x + 2) * EZ] = jnp.dot(both, right_ref[:, x * EZ : (x + 2) * EZ], preferred_element_type=F32)
    copies = []
    for y in (0, 16, 32):
        count = min(16, EY - y)
        for f, inverse_ref in ((0, rs_ref), (1, rd_ref)):
            for x in range(EX):
                end = e_ref[f * ROWS + y : f * ROWS + y + 16, x * EZ : (x + 1) * EZ]
                value = (g_ref[f, x, y : y + 16, :] + end) * inverse_ref[x, y : y + 16, :]
                o_ref[f, pl.ds(y * EX + x, count, stride=EX), :] = value[0:count]
            block = pl.ds(y * EX, count * EX)
            copies.append(pltpu.make_async_copy(o_ref.at[f, block], outs[f].at[block], sem.at[len(copies)]))
            copies[-1].start()
    for copy in copies:
        copy.wait()


def triangle_forward(value):
    size = value.shape[0]
    for step in (1, 2, 1, 2):
        value = value + pltpu.roll(value, size - step, 0)
    return value


def call(kernel, outs, ins, scratch=(), limit=16, micros=1.0, space=VM):
    return pl.pallas_call(
        kernel,
        out_shape=[jax.ShapeDtypeStruct(shape, dtype) for shape, dtype in outs],
        in_specs=[pl.BlockSpec(memory_space=space) for space in ins],
        out_specs=[pl.BlockSpec(memory_space=space)] * len(outs),
        scratch_shapes=[pltpu.VMEM(item[0], item[1]) if isinstance(item, tuple) else item for item in scratch],
        compiler_params=pltpu.CompilerParams(vmem_limit_bytes=limit * 2**20),
        cost_estimate=pl.CostEstimate(flops=0, bytes_accessed=int(micros * 3.6e6), transcendentals=0),
    )


def exchange(axis, spare, *values):
    count, others = lax.axis_size(axis), lax.axis_size(spare)
    names = tuple(sorted((axis, spare)))
    step, spare_step = (others, 1) if names[0] == axis else (1, count)
    results = []
    for first, value in enumerate(values):
        moves = []
        for i in range(count):
            j = i + 1 if i % 2 == first else i - 1
            for o in range(others):
                target = (j, o) if 0 <= j < count else (i, o ^ 1)
                moves.append((i * step + o * spare_step, target[0] * step + target[1] * spare_step))
        results.append(lax.ppermute(value, names, moves))
    return results


def local(local_solution, top_nodes, coarse_solution, corner_dofs, density, element_stiffness):
    dens = jnp.transpose(density, (1, 0, 2)).reshape(EY * EX, EZ)
    shared = lax.axis_size("gz") == 2
    if shared:
        other = lax.ppermute(coarse_solution, "gz", [(0, 1), (1, 0)])
        coarse = jnp.stack([coarse_solution, other])
    else:
        coarse = lax.all_gather(coarse_solution, "gz")

    message = ((X_MESSAGE, EZ), F32)
    even, odd, tops = call(
        pack_kernel,
        [message, message, ((3, XR, EZ), F32)],
        [pltpu.HBM] * 4,
        [((2, 3, 4, NY, EZ), F32), ((3, NX, 1, NY), F32), ((EY * EX, EZ), F32), ((1, 8), jnp.int32), pltpu.SemaphoreType.DMA((9,))],
    )(*[
        pltpu.with_memory_space_constraint(value, pltpu.HBM)
        for value in (local_solution, jnp.transpose(top_nodes, (0, 1, 3, 2)), dens, corner_dofs.reshape(1, 8))
    ])
    even_x, odd_x = exchange("gx", "gy", even, odd)

    own_planes = ((EX, ROWS, EZ), F32)
    rows3, rows4 = ((96, block_rows(3)), BF16), ((128, block_rows(4)), BF16)
    lhs, lhs_edge, lhs_z, dens, inverse_sens, inverse_smooth, dofs, along_y, ends = call(
        prepare_kernel,
        [rows3, rows4, rows4, own_planes, own_planes, own_planes, ((8, EZ), F32), ((EZ, EZ), BF16), ((2 * EZ, EX * EZ), BF16)],
        [VM] * 3,
        [((8, EZ), F32)],
        micros=1.0,
    )(element_stiffness, dens, corner_dofs.reshape(1, 8))

    own_part = ((OWN_ROWS, EZ), F32)
    own, ea, even_own, odd_own = call(
        functools.partial(own_kernel, shared),
        [((3 * NX, ROWS, EZ), F32), ((OWN, ROWS, EZ), F32), own_part, own_part],
        [VM] * 5,
        node_buffers((OWN + 1) * ROWS),
        micros=6.0,
    )(local_solution, lhs, dens, coarse, dofs)

    face = ((12, ROWS, EZ), F32)
    y_message = ((Y_MESSAGE, EZ), F32)
    halo_part = ((Y_MESSAGE - OWN_ROWS, EZ), F32)
    tx, even, odd = call(
        functools.partial(x_kernel, shared),
        [((3, XR, EZ), F32), y_message, y_message],
        [VM] * 8,
        [halo_part, halo_part, ((4, XR, EZ), F32)],
        micros=1.0,
    )(own, even_own, odd_own, tops, even_x, odd_x, coarse, dofs)
    even_y, odd_y = exchange("gy", "gz", even, odd)

    xl, xh, halo_dens = call(
        functools.partial(halo_kernel, shared), [face, face, ((6, ROWS, EZ), F32)], [VM] * 4, micros=0.7
    )(own, even_x, odd_x, coarse)
    (eb,) = call(
        side_kernel, [((XE - OWN, ROWS, EZ), F32)], [VM] * 4, node_buffers((XE - OWN + 2) * ROWS), micros=2.6
    )(own, xl, xh, lhs)

    (zo,) = call(turn_kernel, [((len(SLOTS), 8, EZ), F32)], [VM] * 5, micros=1.5)(own, xl, xh, dens, halo_dens)

    z_message = ((Z_MESSAGE, EZ), F32)
    low_y, high_y, oa, ob, od, *messages = call(
        y_kernel,
        [y_message, y_message, ((72, EZ), F32), ((72, EZ), F32), ((XR, EZ), F32)] + [z_message] * (1 if shared else 2),
        [VM] * 5,
        [((8 * 3 * XR, EZ), F32), ((8 * XR, EZ), F32)],
        micros=1.0,
    )(tx, zo, eb, even_y, odd_y)
    received_z = exchange("gz", "gy", *messages)

    el, eh = call(
        edge_kernel,
        [((XE, 8, EZ), F32)] * 2,
        [VM] * 6,
        node_buffers(XN * 8),
        micros=2.3,
    )(own, xl, xh, low_y, high_y, lhs_edge)

    (filtered,) = call(
        field_kernel, [((2, EX, ROWS, EZ), F32)], [VM] * 8, [((2, XE, QROWS, EZ), F32)], micros=1.5
    )(ea, eb, el, eh, dens, halo_dens, low_y, high_y)

    sens, smooth = call(
        last_kernel,
        [((EY * EX, EZ), F32)] * 2,
        [VM] * (9 + len(received_z)),
        [((4, XR, EZ), F32), ((2, 4 * EX, EZ), F32), z_message, z_message, ((2 * ROWS, EX * EZ), F32), ((2, EY * EX, EZ), F32),
         pltpu.SemaphoreType.DMA((6,))] + node_buffers(5 * XR + 8),
        space=pltpu.HBM,
        micros=2.5,
    )(filtered, along_y, ends, inverse_sens, inverse_smooth, oa, ob, od, lhs_z, *received_z)

    def grid(value):
        return jnp.transpose(value.reshape(EY, EX, EZ), (1, 0, 2))

    return grid(sens), grid(smooth)


def solution(mesh):
    in_specs = (
        P(None, "gx", "gy", "gz"),
        P(None, "gx", "gy", "gz"),
        P(None, "gz"),
        P("gx", "gy", "gz", None),
        P("gx", "gy", "gz"),
        P(),
    )
    out_specs = (P("gx", "gy", "gz"), P("gx", "gy", "gz"))
    return jax.shard_map(local, mesh=mesh, in_specs=in_specs, out_specs=out_specs, check_vma=False)
```
